512 devices in a mesh: role: 2 (over y_lo), seq: 32 (over z, y_hi), mp: 8 (over x, core).
Axes of the slice: x: 4, y: 4 (y_hi: 2, y_lo: 2; y = y_hi * 2 + y_lo), z: 16, core: 2. Of those that a mesh axis runs over, the one named last changes fastest.
Arguments:
- gen_hidden: bfloat16 [4096, 3072], P('seq'), may hold values from -6 to 6
- w_gen: bfloat16 [3072, 64], replicated, may hold values from -0.109375 to 0.109375
- noise_latent: bfloat16 [4096, 64], P('seq'), may hold values from -20 to 20, as said below
- level_index: int32 [1], replicated, may hold values from 0 to 999
- w_embed: bfloat16 [2, 64, 3072], P('role'), may hold values from -0.75 to 0.75
- modulation: float32 [2, 3, 3072], P('role'), may hold values from -3 to 3
- w_qkv: bfloat16 [2, 3072, 3, 3072], P('role', 'seq', None, 'mp'), may hold values from -0.109375 to 0.109375
- qk_gain: float32 [2, 2, 128], P('role'), may hold values from 1.6 to 4
- text_kv: bfloat16 [2, 512, 2, 3072], P('role', 'seq', None, 'mp'), may hold values from -305 to 305, as said below
- w_out: bfloat16 [2, 3072, 3072], P('role', 'mp'), may hold values from -0.109375 to 0.109375
- w_final: bfloat16 [2, 3072, 64], P('role'), may hold values from -0.109375 to 0.109375
Outputs:
- grad_x: float32 [4096, 64], P('seq', 'role')
- grad_hidden: bfloat16 [4096, 3072], P('seq', 'role')
- grad_wgen: float32 [3072, 64], P('mp', 'role')
The draws below stay inside these ranges and needn't reach their ends.
Inputs may be any that keep to these rules, and one draw needn't show every extreme that they name: `text_kv`: keys and values of the text stream, already projected and normalized. `noise_latent`: noise whose spread differs from row to row.
All inputs are finite; a program needn't handle non-finite values. Where the reference program divides by a largest or mean magnitude, that divisor is 1e-20 or more.
Results may differ from the reference program's by a relative error of at most 0.027.
Values may be sent and summed in bfloat16 or wider, within the bound.
No kernel may reach another device: no remote copies, remote signals or barrier semaphores. Data moves between devices by JAX's collectives and lax.ppermute only.
A program may use at most 64 MiB of HBM per device.

```python
import math
import jax
import jax.numpy as jnp
from jax import lax

D = 3072
H = 24
HD = 128
C = 64
TXT = 512
LEVELS = 1000
TOKENS = 4096


def draw_text_kv(key, part):
    key = jax.random.fold_in(key, 11)
    value_key = jax.random.fold_in(key, 0)
    values = jnp.clip(jax.random.normal(value_key, (2, TXT, 2, D), jnp.float32), -5.0, 5.0)
    keys_plane = jnp.clip(values[:, :, 0], -4.0, 4.0) * 2.5
    values_plane = values[:, :, 1]
    return jnp.stack([keys_plane, values_plane], axis=2).astype(jnp.bfloat16)


def draw_noise_latent(key, part):
    key = jax.random.fold_in(key, 23)
    place = jnp.arange(TOKENS, dtype=jnp.float32) / max(TOKENS - 1, 1)
    row_scale = 1.0 + 4.0 * place
    values = jnp.clip(jax.random.normal(key, (TOKENS, C), jnp.float32), -4.0, 4.0)
    return (values * row_scale[:, None]).astype(jnp.bfloat16)


def level_of(stream_key, shape, cuts, smallest, high):
    gain, own = 1.0, jax.random.fold_in(stream_key, 6)
    for dim, blocks in cuts:
        steps = jnp.exp(jax.random.uniform(jax.random.fold_in(own, dim), (blocks,), jnp.float32, smallest / len(cuts), high / len(cuts)))
        gain = gain * jnp.repeat(steps, shape[dim] // blocks).reshape([-1 if axis == dim else 1 for axis in range(len(shape))])
    return gain


def bell_draw(key, shape, deviation, bound, cuts=(), held_as=jnp.bfloat16):
    array = jax.random.normal(key, shape, jnp.float32) * deviation
    if len(cuts) > 0:
        array = level_of(key, shape, cuts, -0.22, 0.18) * array
    return jnp.clip(array, min=-bound, max=bound).astype(held_as)


def setup_inputs(seed: int = 0) -> dict:
    key_of = jax.random.split(jax.random.key(seed), 12)
    return {
        "gen_hidden": bell_draw(key_of[0], (TOKENS, D), 1.0, 6.0, ((0, 32),)),
        "w_gen": bell_draw(key_of[1], (D, C), D ** -0.5, 0.109375),
        "noise_latent": draw_noise_latent(jax.random.fold_in(key_of[11], 71), 0),
        "level_index": jax.random.randint(key_of[3], (1,), 0, LEVELS).astype(jnp.int32),
        "w_embed": bell_draw(key_of[4], (2, C, D), C ** -0.5, 0.75, ((0, 2),)),
        "modulation": bell_draw(key_of[5], (2, 3, D), 0.5, 3.0, ((0, 2),), jnp.float32),
        "w_qkv": bell_draw(key_of[6], (2, D, 3, D), D ** -0.5, 0.109375, ((0, 2), (1, 32), (3, 8))),
        "qk_gain": jnp.clip(jnp.exp(math.log(4.0) - 0.9162907 * jax.random.uniform(key_of[7], (2, 2, HD), jnp.float32) ** level_of(key_of[7], (2, 2, HD), ((0, 2),), -0.2, 0.2)), 1.6, 4.0),
        "text_kv": draw_text_kv(jax.random.fold_in(key_of[11], 71), 0),
        "w_out": bell_draw(key_of[9], (2, D, D), D ** -0.5, 0.109375, ((0, 2), (1, 8))),
        "w_final": bell_draw(key_of[10], (2, D, C), D ** -0.5, 0.109375, ((0, 2),)),
    }


def layer_rows(values):
    row_mean = lax.optimization_barrier(jnp.mean(values, axis=-1, keepdims=True))
    row_var = lax.optimization_barrier(jnp.mean(jnp.square(values - row_mean), axis=-1, keepdims=True))
    return (values - row_mean) * lax.rsqrt(row_var + 1e-06)

def head_norm(values, gains):
    return values * lax.rsqrt(lax.optimization_barrier(jnp.mean(values * values, axis=-1, keepdims=True)) + 1e-06) * gains

def score_block(noised, embed_w, modulate, qkv_w, gains, text_pair, out_w, final_w):
    h_start = jnp.dot(noised, embed_w, preferred_element_type=jnp.float32)
    normed = (layer_rows(h_start) * (1.0 + modulate[1]) + modulate[0]).astype(jnp.bfloat16)
    projected = jnp.dot(normed, qkv_w.reshape(D, 3 * D), preferred_element_type=jnp.float32)
    projected = projected.reshape(TOKENS, 3, H, HD)
    queries = head_norm(projected[:, 0], gains[0]).astype(jnp.bfloat16)
    own_keys = head_norm(projected[:, 1], gains[1]).astype(jnp.bfloat16)
    own_values = projected[:, 2].astype(jnp.bfloat16)
    all_keys = jnp.concatenate([text_pair[:, 0].reshape(TXT, H, HD), own_keys], axis=0)
    all_values = jnp.concatenate([text_pair[:, 1].reshape(TXT, H, HD), own_values], axis=0)
    score_scale = HD ** (-0.5)

    def one_head(operands):
        query_head, key_head, value_head = operands
        scores = jnp.dot(query_head, key_head.T, preferred_element_type=jnp.float32) * score_scale
        probs = jnp.exp(scores - lax.optimization_barrier(jnp.max(scores, axis=-1, keepdims=True)))
        row_sums = lax.optimization_barrier(jnp.sum(probs, axis=-1))
        mixed = jnp.dot(probs.astype(jnp.bfloat16), value_head, preferred_element_type=jnp.float32)
        return (mixed / row_sums[:, None]).astype(jnp.bfloat16)
    attended = lax.map(one_head, (jnp.transpose(queries, (1, 0, 2)), jnp.transpose(all_keys, (1, 0, 2)), jnp.transpose(all_values, (1, 0, 2))))
    attended = jnp.transpose(attended, (1, 0, 2)).reshape(TOKENS, D)
    h_after = h_start + modulate[2] * jnp.dot(attended, out_w, preferred_element_type=jnp.float32)
    final_rows = layer_rows(h_after).astype(jnp.bfloat16)
    return jnp.dot(final_rows, final_w, preferred_element_type=jnp.float32)

def reference(gen_hidden, w_gen, noise_latent, level_index, w_embed, modulation, w_qkv, qk_gain, text_kv, w_out, w_final):
    x_gen = jnp.dot(gen_hidden, w_gen, preferred_element_type=jnp.float32)
    time_frac = (level_index[0].astype(jnp.float32) + 1.0) / (LEVELS + 1.0)
    noise_scale = 3.0 * time_frac / (1.0 + 2.0 * time_frac)
    noised = ((1.0 - noise_scale) * x_gen + noise_scale * noise_latent.astype(jnp.float32)).astype(jnp.bfloat16)
    teacher = score_block(noised, w_embed[0], modulation[0], w_qkv[0], qk_gain[0], text_kv[0], w_out[0], w_final[0])
    student = score_block(noised, w_embed[1], modulation[1], w_qkv[1], qk_gain[1], text_kv[1], w_out[1], w_final[1])
    pred_real = noised.astype(jnp.float32) - noise_scale * teacher
    spread_weight = jnp.mean(jnp.abs(x_gen - pred_real)) + 1e-06
    grad_x = noise_scale * (teacher - student) / spread_weight
    grad_b = grad_x.astype(jnp.bfloat16)
    grad_hidden = jnp.dot(grad_b, w_gen.T, preferred_element_type=jnp.float32).astype(jnp.bfloat16)
    grad_wgen = jnp.dot(gen_hidden.T, grad_b, preferred_element_type=jnp.float32)
    return (grad_x, grad_hidden, grad_wgen)
```

```python
import jax
import jax.numpy as jnp
from jax import lax
from jax.experimental import pallas as pl
from jax.experimental.pallas import tpu as pltpu
from jax.sharding import PartitionSpec as P

LEVELS = 1000
HD = 128
CHANS = 64
HALF = CHANS // 2
MROWS = 80
PIECE = 80
F32 = jnp.float32
BF16 = jnp.bfloat16
NN = (((1,), (0,)), ((), ()))
NT = (((1,), (1,)), ((), ()))


def dot(a, b, dims=NN):
    return lax.dot_general(a, b, dims, preferred_element_type=F32)


def call(body, out_shape, args, scratch=(), smem=0, limit=24):
    vmem = pl.BlockSpec(memory_space=pltpu.VMEM)
    scalars = pl.BlockSpec(memory_space=pltpu.SMEM)
    return pl.pallas_call(
        body,
        out_shape=out_shape,
        in_specs=[scalars if i < smem else vmem for i in range(len(args))],
        out_specs=jax.tree.map(lambda out: scalars if out.dtype == jnp.int32 else vmem, out_shape),
        scratch_shapes=list(scratch),
        compiler_params=pltpu.CompilerParams(vmem_limit_bytes=limit * 1024 * 1024),
    )(*args)


def noise_scale_of(level, shape):
    time_frac = (jnp.full(shape, level, jnp.int32).astype(F32) + 1.0) / (LEVELS + 1.0)
    return 3.0 * time_frac / (1.0 + 2.0 * time_frac)


def weight_body(idx_ref, embed_ref, mod_ref, qkv_ref, payload_ref, idx_out_ref, term_ref):
    width = embed_ref.shape[1]
    features = qkv_ref.shape[1]
    offset = idx_ref[0] * features
    start = pl.multiple_of(jnp.minimum((offset >> 7) << 7, width - 256), HD)
    mean = jnp.sum(embed_ref[...].astype(F32), axis=1, keepdims=True) / width
    window = embed_ref[:, pl.ds(start, 256)].astype(F32)
    scale = 1.0 + mod_ref[1, :, pl.ds(start, 256)]
    shift = mod_ref[0, :, pl.ds(start, 256)]
    rows = jnp.concatenate(
        [(window - mean) * scale, shift, jnp.zeros((MROWS - CHANS - 1, 256), F32)], axis=0
    )
    select = jnp.where(
        lax.broadcasted_iota(jnp.int32, (256, features), 0)
        == lax.broadcasted_iota(jnp.int32, (256, features), 1) + (offset - start),
        1.0,
        0.0,
    ).astype(BF16)
    high = rows.astype(BF16)
    low = dot((rows - high.astype(F32)).astype(BF16), select).astype(BF16)
    high = dot(high, select).astype(BF16)
    for part in range(3):
        term = dot(high, qkv_ref[part]) + dot(low, qkv_ref[part])
        for head in range(3):
            j = part * 3 + head
            block = term[:, head * HD : (head + 1) * HD]
            term_ref[j * CHANS : (j + 1) * CHANS, :] = block[0:CHANS, :]
            term_ref[9 * CHANS + j : 9 * CHANS + j + 1, :] = block[CHANS : CHANS + 1, :]
    term_ref[9 * CHANS + 9 :, :] = jnp.zeros((term_ref.shape[0] - 9 * CHANS - 9, HD), F32)
    for p in range(payload_ref.shape[0]):
        payload_ref[p] = term_ref[p * PIECE : (p + 1) * PIECE, :].astype(BF16)
    for i in range(idx_out_ref.shape[0]):
        idx_out_ref[i] = idx_ref[i]


def latent_body(
    idx_ref, hidden_ref, gen_t_ref, noise_t_ref, embed_ref, text_in_ref, noised_ref, gap_ref, send_ref
):
    x_t = dot(gen_t_ref[...], hidden_ref[...], NT)
    noise_scale = noise_scale_of(idx_ref[3], x_t.shape)
    noised_t = ((1.0 - noise_scale) * x_t + noise_scale * noise_t_ref[...].astype(F32)).astype(BF16)
    noised = noised_t.astype(F32).T
    noised_ref[...] = noised
    gap_ref[...] = (x_t - noised_t.astype(F32)).T
    h = dot(noised.astype(BF16), embed_ref[...])
    width = h.shape[1]
    row_mean = jnp.sum(h, axis=1, keepdims=True) / width
    row_var = jnp.sum(jnp.square(h - row_mean), axis=1, keepdims=True) / width
    send_ref[0:CHANS, :] = (noised * lax.rsqrt(row_var + 1e-06)).T.astype(BF16)
    for j in range(6):
        send_ref[CHANS + j * 16 : CHANS + (j + 1) * 16, :] = text_in_ref[:, j * HD : (j + 1) * HD]


def total_of(ref, rows):
    total = ref[0, 0:rows, :].astype(F32)
    for i in range(1, ref.shape[0]):
        total = total + ref[i, 0:rows, :].astype(F32)
    return total.astype(BF16)


def far_body(idx_ref, recv_ref, send_ref, out_ref):
    piece = total_of(recv_ref, PIECE)
    channels = send_ref[pl.ds(pl.multiple_of((idx_ref[1] & 1) * HALF, HALF), HALF), :]
    for i in range(out_ref.shape[0]):
        out_ref[i, 0:PIECE, :] = piece
        out_ref[i, PIECE : PIECE + HALF, :] = channels
        out_ref[i, PIECE + HALF :, :] = send_ref[CHANS:, :]


def spread_body(recv_ref, out_ref, text_ref):
    piece = total_of(recv_ref, PIECE)
    text = PIECE + HALF
    for i in range(out_ref.shape[0]):
        out_ref[i, 0:PIECE, :] = piece
        for g in range(recv_ref.shape[0]):
            out_ref[i, PIECE + g * HALF : PIECE + (g + 1) * HALF, :] = recv_ref[g, PIECE:text, :]
            text_ref[i, g * 96 : (g + 1) * 96, :] = recv_ref[g, text:, :]


def image_body(
    idx_ref, send_ref, recv_ref, other_ref, gain_ref, out_ref, lat_ref, s_ref, v_ref, m_ref, own_ref
):
    tokens = lat_ref.shape[1]
    chunk = 512
    n_chunks = tokens // chunk
    ones = jnp.where(lax.broadcasted_iota(jnp.int32, (MROWS - CHANS, HD), 0) == 0, 1.0, 0.0).astype(BF16)
    n_far = (recv_ref.shape[1] - PIECE) // HALF
    for i in range(tokens // HD):
        near, first = i // n_far, (i % n_far) * HALF
        at = slice(i * HD, (i + 1) * HD)
        lat_ref[0:HALF, at] = recv_ref[near, PIECE + first : PIECE + first + HALF, :]
        lat_ref[HALF:CHANS, at] = other_ref[near, first : first + HALF, :]
        lat_ref[CHANS:MROWS, at] = ones
    for i in range(recv_ref.shape[0]):
        m_ref[i * PIECE : (i + 1) * PIECE, :] = recv_ref[i, 0:PIECE, :].astype(F32)
    own_ref[...] = send_ref[0:CHANS, :].astype(F32)

    def reordered(ref, base):
        core = idx_ref[1] & 1
        return jnp.concatenate(
            [ref[pl.ds(pl.multiple_of(k * HALF + base, HALF), HALF), :] for k in (core, 1 - core)], axis=0
        )

    own = jnp.concatenate([reordered(own_ref, 0).astype(BF16), ones], axis=0)
    score_scale = HD ** (-0.5) * 1.4426950408889634
    biases = m_ref[9 * CHANS : 9 * CHANS + 16, :]

    def weight(j):
        block = reordered(m_ref, j * CHANS)
        pad = jnp.zeros((HD - CHANS - 1, HD), F32)
        return jnp.concatenate([block, biases[j : j + 1, :], pad], axis=0).T[:, 0:MROWS].astype(BF16)

    q_image, w_k, w_v = [], [], []
    for head in range(3):
        q_t = dot(weight(head), own)
        q_t = q_t * lax.rsqrt(jnp.mean(q_t * q_t, axis=0, keepdims=True) + 1e-06)
        q = q_t.T * (gain_ref[0:1, :] * score_scale)
        out_ref[head, 3] = q
        q_image.append((q * gain_ref[1:2, :]).astype(BF16))
        w_k.append(weight(3 + head))
        w_v.append(weight(6 + head))
    rows = q_image[0].shape[0]

    def score_step(c, tops):
        at = pl.ds(pl.multiple_of(c * chunk, chunk), chunk)
        lat = lat_ref[:, at]
        out = []
        for head in range(3):
            k_t = dot(w_k[head], lat)
            k_t = k_t * lax.rsqrt(jnp.mean(k_t * k_t, axis=0, keepdims=True) + 1e-06)
            v_ref[head, :, at] = dot(w_v[head], lat).astype(BF16)
            s = dot(q_image[head], k_t.astype(BF16))
            s_ref[head, :, at] = s
            top = tops[head]
            for j in range(chunk // HD):
                top = jnp.maximum(top, s[:, j * HD : (j + 1) * HD])
            out.append(top)
        return tuple(out)

    tops = lax.fori_loop(0, n_chunks, score_step, (jnp.full((rows, HD), -3e38, F32),) * 3)
    for head in range(3):
        out_ref[head, 0] = jnp.zeros((rows, HD), F32)
        out_ref[head, 1] = jnp.zeros((rows, HD), F32)
        out_ref[head, 2] = jnp.broadcast_to(jnp.max(tops[head], axis=1, keepdims=True), (rows, HD))

    def mix_step(c, carry):
        at = pl.ds(pl.multiple_of(c * chunk, chunk), chunk)
        for head in range(3):
            p = jnp.exp2(s_ref[head, :, at] - out_ref[head, 2][:, 0:1])
            total = out_ref[head, 1]
            for j in range(chunk // HD):
                total = total + p[:, j * HD : (j + 1) * HD]
            out_ref[head, 1] = total
            out_ref[head, 0] += dot(p.astype(BF16), v_ref[head, :, at], NT)
        return carry

    lax.fori_loop(0, n_chunks, mix_step, 0)


def text_body(image_ref, text_ref, out_w_ref, y_ref, att_ref):
    def block(first):
        return text_ref[:, first : first + 16, :].reshape(text_ref.shape[0] * 16, HD)

    for head in range(3):
        s = dot(image_ref[head, 3].astype(BF16), block(head * 16), NT)
        image_top = image_ref[head, 2]
        top = jnp.maximum(image_top, jnp.max(s, axis=1, keepdims=True))
        keep = jnp.exp2(image_top - top)
        p = jnp.exp2(s - top[:, 0:1])
        acc = image_ref[head, 0] * keep + dot(p.astype(BF16), block(48 + head * 16))
        total = jnp.sum(image_ref[head, 1] * keep, axis=1, keepdims=True) + jnp.sum(p, axis=1, keepdims=True)
        att_ref[:, head * HD : (head + 1) * HD] = (acc / total).astype(BF16)
    att = att_ref[...]
    step = 512
    for j in range(out_w_ref.shape[1] // step):
        y = dot(att, out_w_ref[:, j * step : (j + 1) * step]).astype(BF16)
        y_ref[:, :, j * step : (j + 1) * step] = y.reshape(y_ref.shape[0], y_ref.shape[1], step)


def velocity_body(idx_ref, parts_ref, noised_ref, embed_ref, mod_ref, final_t_ref, v_ref):
    total = parts_ref[0].astype(F32)
    for i in range(1, parts_ref.shape[0]):
        total = total + parts_ref[i].astype(F32)
    own_rows = total.shape[0]
    own = noised_ref[pl.ds(pl.multiple_of(idx_ref[1] * own_rows, own_rows), own_rows), :].astype(BF16)
    h = dot(own, embed_ref[...]) + mod_ref[2] * total
    width = h.shape[1]
    h = h - jnp.sum(h, axis=1, keepdims=True) / width
    var = jnp.sum(h * h, axis=1, keepdims=True) / width
    v = dot((h * lax.rsqrt(var + 1e-06)).astype(BF16), final_t_ref[...], NT)
    v = jnp.concatenate([v[0:8, :], v[8:16, :]], axis=1)
    for i in range(v_ref.shape[0]):
        v_ref[i] = v


def grad_body(idx_ref, both_ref, gap_ref, hidden_ref, gen_t_ref, piece_ref, share_ref, raw_ref, diff_ref, grad_ref):
    n_mp = both_ref.shape[0] // 2
    chans = gap_ref.shape[1]

    def rows(first):
        blocks = []
        for i in range(first, first + n_mp):
            blocks += [both_ref[i][:, 0:chans], both_ref[i][:, chans : 2 * chans]]
        return jnp.concatenate(blocks, axis=0)

    teacher, student = rows(0), rows(n_mp)
    spread = jnp.abs(gap_ref[...] + noise_scale_of(idx_ref[3], gap_ref.shape) * teacher)
    spread = jnp.sum(jnp.sum(spread, axis=1, keepdims=True), axis=0, keepdims=True)
    diff = teacher - student
    diff_ref[...] = diff.T
    half = chans // 2
    share = diff_ref[pl.ds(pl.multiple_of(idx_ref[2] * half, half), half), :]
    share_ref[...] = share
    cols = grad_ref.shape[1]
    hidden = hidden_ref[:, pl.ds(pl.multiple_of(idx_ref[1] * cols, HD), cols)]
    grad_ref[...] = dot(share.astype(BF16), hidden)
    for p in range(8):
        for g in range(3):
            piece_ref[p, 4 * g : 4 * g + 4, :] = grad_ref[4 * p : 4 * p + 4, g * HD : (g + 1) * HD]
        piece_ref[p, 12:16, :] = jnp.broadcast_to(spread, (4, HD))
    feats = raw_ref.shape[1]
    raw_ref[...] = dot(diff.astype(BF16), gen_t_ref[:, pl.ds(pl.multiple_of(idx_ref[2] * feats, HD), feats)])


def near_body(recv_ref, out_ref):
    total = recv_ref[0]
    for i in range(1, recv_ref.shape[0]):
        total = total + recv_ref[i]
    row = lax.broadcasted_iota(jnp.int32, total.shape, 0)
    high = total.astype(BF16).astype(F32)
    mid = (total - high).astype(BF16).astype(F32)
    low = total - high - mid
    out = jnp.where(row == 13, mid, jnp.where(row == 14, low, high)).astype(BF16)
    for i in range(out_ref.shape[0]):
        out_ref[i] = out


def last_body(idx_ref, recv_ref, share_ref, raw_ref, x_ref, hidden_ref, gen_ref, *, entries):
    totals = []
    for p in range(8):
        total = recv_ref[p].astype(F32)
        for g in range(1, recv_ref.shape[0] // 8):
            total = total + recv_ref[8 * g + p].astype(F32)
        totals.append(total)
    spread = totals[0][12:13, 0:1] + totals[0][13:14, 0:1] + totals[0][14:15, 0:1]
    factor = noise_scale_of(idx_ref[3], (1, 1)) / (spread / entries + 1e-06)
    x_ref[...] = share_ref[...] * factor
    hidden_ref[...] = (raw_ref[...] * factor).astype(BF16)
    for p in range(8):
        scaled = totals[p] * factor
        for g in range(3):
            gen_ref[4 * p : 4 * p + 4, g * HD : (g + 1) * HD] = scaled[4 * g : 4 * g + 4, :]


def exchange(array, axis, groups=None):
    return lax.all_to_all(array, axis, 0, 0, axis_index_groups=groups, tiled=True)


def on_device(
    gen_hidden, w_gen, noise_latent, level_index, w_embed, modulation, w_qkv, qk_gain, text_kv, w_out, w_final
):
    rows_here, width = gen_hidden.shape
    n_seq, n_mp = lax.axis_size("seq"), lax.axis_size("mp")
    chans = w_gen.shape[1]
    tokens = rows_here * n_seq
    sds = jax.ShapeDtypeStruct
    mods = jnp.transpose(modulation, (1, 0, 2))
    embed = w_embed[0]
    gen_t = w_gen.T
    idx = jnp.stack(
        [lax.axis_index("seq"), lax.axis_index("mp"), lax.axis_index("role"), level_index[0]]
    ).astype(jnp.int32)
    near_groups = [[8 * g + i for i in range(8)] for g in range(n_seq // 8)]
    far_groups = [[8 * g + i for g in range(n_seq // 8)] for i in range(8)]

    n_far = n_seq // 8
    payload, idx_late = call(
        weight_body,
        (sds((8, PIECE, HD), BF16), sds(idx.shape, jnp.int32)),
        (idx, embed, mods, jnp.transpose(w_qkv[0], (1, 0, 2))),
        scratch=(pltpu.VMEM((8 * PIECE, HD), F32),),
        smem=1,
        limit=60,
    )
    noised, gap, send = call(
        latent_body,
        (sds((rows_here, chans), F32), sds((rows_here, chans), F32), sds((chans + 96, HD), BF16)),
        (idx_late, gen_hidden, gen_t, noise_latent.T, embed, text_kv[0].reshape(text_kv.shape[1], 6 * HD)),
        smem=1,
        limit=60,
    )
    pieces = exchange(payload, "seq", near_groups)
    pieces = call(far_body, sds((n_far, PIECE + HALF + 96, HD), BF16), (idx, pieces, send), smem=1)
    pieces = exchange(pieces, "seq", far_groups)
    pieces, text = call(
        spread_body,
        (sds((8, PIECE + n_far * HALF, HD), BF16), sds((8, n_far * 96, HD), BF16)),
        (pieces,),
    )
    pieces = exchange(pieces, "seq", near_groups)
    text = exchange(text, "seq", near_groups).reshape(n_seq, 96, HD)
    other = lax.ppermute(pieces[:, PIECE:, :], "mp", [(i, i ^ 1) for i in range(n_mp)])

    image = call(
        image_body,
        sds((3, 4, rows_here, HD), F32),
        (idx, send, pieces, other, qk_gain[0]),
        scratch=(
            pltpu.VMEM((MROWS, tokens), BF16),
            pltpu.VMEM((3, rows_here, tokens), F32),
            pltpu.VMEM((3, HD, tokens), BF16),
            pltpu.VMEM((8 * PIECE, HD), F32),
            pltpu.VMEM((chans, HD), F32),
        ),
        smem=1,
    )
    own_rows = rows_here // n_mp
    y = call(
        text_body,
        sds((n_mp, own_rows, width), BF16),
        (image, text, w_out[0]),
        scratch=(pltpu.VMEM((rows_here, 3 * HD), BF16),),
    )
    parts = exchange(y, "mp")
    velocity = call(
        velocity_body,
        sds((2 * n_mp, 8, 2 * chans), F32),
        (idx, parts, noised, embed, mods, w_final[0].T),
        smem=1,
    )
    both = exchange(velocity, ("role", "mp"))
    half = chans // 2
    grad_piece, share, raw = call(
        grad_body,
        (sds((8, 16, HD), F32), sds((half, rows_here), F32), sds((rows_here, width // 2), F32)),
        (idx, both, gap, gen_hidden, gen_t),
        scratch=(pltpu.VMEM((chans, rows_here), F32), pltpu.VMEM((half, 3 * HD), F32)),
        smem=1,
    )
    near = exchange(grad_piece, "seq", near_groups)
    near = call(near_body, sds((n_seq, 16, HD), BF16), (near,))
    everything = exchange(near, "seq")

    def last(*refs):
        last_body(*refs, entries=tokens * chans)

    grad_x_t, grad_hidden, grad_gen_t = call(
        last,
        (sds((half, rows_here), F32), sds((rows_here, width // 2), BF16), sds((half, 3 * HD), F32)),
        (idx, everything, share, raw),
        smem=1,
    )
    return grad_x_t.T, grad_hidden, grad_gen_t.T


def solution(mesh):
    placed = (
        P("seq", None),
        P(),
        P("seq", None),
        P(),
        P("role", None, None),
        P("role", None, None),
        P("role", "seq", None, "mp"),
        P("role", None, None),
        P("role", "seq", None, "mp"),
        P("role", "mp", None),
        P("role", None, None),
    )
    return jax.shard_map(
        on_device,
        mesh=mesh,
        in_specs=placed,
        out_specs=(P("seq", "role"), P("seq", "role"), P("mp", "role")),
        check_vma=False,
    )
```

```python
import jax
import jax.numpy as jnp
from jax import lax
from jax.experimental import pallas as pl
from jax.experimental.pallas import tpu as pltpu
from jax.sharding import PartitionSpec as P

LEVELS = 1000
HD = 128
SEQ = ("z_far", "z_near", "y_hi")
NEAR = ("z_near", "y_hi")
CHANS = 64
HALF = CHANS // 2
MROWS = 80
PIECE = 80
F32 = jnp.float32
BF16 = jnp.bfloat16
NN = (((1,), (0,)), ((), ()))
NT = (((1,), (1,)), ((), ()))


def dot(a, b, dims=NN):
    return lax.dot_general(a, b, dims, preferred_element_type=F32)


def call(body, out_shape, args, scratch=(), smem=0, limit=24):
    vmem = pl.BlockSpec(memory_space=pltpu.VMEM)
    scalars = pl.BlockSpec(memory_space=pltpu.SMEM)
    return pl.pallas_call(
        body,
        out_shape=out_shape,
        in_specs=[scalars if i < smem else vmem for i in range(len(args))],
        out_specs=jax.tree.map(lambda out: scalars if out.dtype == jnp.int32 else vmem, out_shape),
        scratch_shapes=list(scratch),
        compiler_params=pltpu.CompilerParams(vmem_limit_bytes=limit * 1024 * 1024),
    )(*args)


def noise_scale_of(level, shape):
    time_frac = (jnp.full(shape, level, jnp.int32).astype(F32) + 1.0) / (LEVELS + 1.0)
    return 3.0 * time_frac / (1.0 + 2.0 * time_frac)


def weight_body(idx_ref, embed_ref, mod_ref, qkv_ref, payload_ref, idx_out_ref, term_ref):
    width = embed_ref.shape[1]
    features = qkv_ref.shape[1]
    offset = idx_ref[0] * features
    start = pl.multiple_of(jnp.minimum((offset >> 7) << 7, width - 256), HD)
    mean = jnp.sum(embed_ref[...].astype(F32), axis=1, keepdims=True) / width
    window = embed_ref[:, pl.ds(start, 256)].astype(F32)
    scale = 1.0 + mod_ref[1, :, pl.ds(start, 256)]
    shift = mod_ref[0, :, pl.ds(start, 256)]
    rows = jnp.concatenate(
        [(window - mean) * scale, shift, jnp.zeros((MROWS - CHANS - 1, 256), F32)], axis=0
    )
    select = jnp.where(
        lax.broadcasted_iota(jnp.int32, (256, features), 0)
        == lax.broadcasted_iota(jnp.int32, (256, features), 1) + (offset - start),
        1.0,
        0.0,
    ).astype(BF16)
    high = rows.astype(BF16)
    low = dot((rows - high.astype(F32)).astype(BF16), select).astype(BF16)
    high = dot(high, select).astype(BF16)
    for part in range(3):
        term = dot(high, qkv_ref[part]) + dot(low, qkv_ref[part])
        for head in range(3):
            j = part * 3 + head
            block = term[:, head * HD : (head + 1) * HD]
            term_ref[j * CHANS : (j + 1) * CHANS, :] = block[0:CHANS, :]
            term_ref[9 * CHANS + j : 9 * CHANS + j + 1, :] = block[CHANS : CHANS + 1, :]
    term_ref[9 * CHANS + 9 :, :] = jnp.zeros((term_ref.shape[0] - 9 * CHANS - 9, HD), F32)
    for p in range(payload_ref.shape[0]):
        payload_ref[p] = term_ref[p * PIECE : (p + 1) * PIECE, :].astype(BF16)
    for i in range(idx_out_ref.shape[0]):
        idx_out_ref[i] = idx_ref[i]


def latent_body(
    idx_ref, hidden_ref, gen_t_ref, noise_t_ref, embed_ref, text_in_ref, noised_ref, gap_ref, send_ref
):
    x_t = dot(gen_t_ref[...], hidden_ref[...], NT)
    noise_scale = noise_scale_of(idx_ref[3], x_t.shape)
    noised_t = ((1.0 - noise_scale) * x_t + noise_scale * noise_t_ref[...].astype(F32)).astype(BF16)
    noised = noised_t.astype(F32).T
    noised_ref[...] = noised
    gap_ref[...] = (x_t - noised_t.astype(F32)).T
    h = dot(noised.astype(BF16), embed_ref[...])
    width = h.shape[1]
    row_mean = jnp.sum(h, axis=1, keepdims=True) / width
    row_var = jnp.sum(jnp.square(h - row_mean), axis=1, keepdims=True) / width
    send_ref[0:CHANS, :] = (noised * lax.rsqrt(row_var + 1e-06)).T.astype(BF16)
    text = text_in_ref[...].astype(F32)
    for j in range(6):
        block = text[:, j // 3, (j % 3) * HD : (j % 3 + 1) * HD]
        send_ref[CHANS + j * 16 : CHANS + (j + 1) * 16, :] = block.astype(BF16)


def total_of(ref, rows):
    total = ref[0, 0:rows, :].astype(F32)
    for i in range(1, ref.shape[0]):
        total = total + ref[i, 0:rows, :].astype(F32)
    return total.astype(BF16)


def far_body(idx_ref, recv_ref, send_ref, out_ref):
    piece = total_of(recv_ref, PIECE)
    channels = send_ref[pl.ds(pl.multiple_of((idx_ref[1] & 1) * HALF, HALF), HALF), :]
    for i in range(out_ref.shape[0]):
        out_ref[i, 0:PIECE, :] = piece
        out_ref[i, PIECE : PIECE + HALF, :] = channels
        out_ref[i, PIECE + HALF :, :] = send_ref[CHANS:, :]


def spread_body(recv_ref, out_ref, text_ref):
    piece = total_of(recv_ref, PIECE)
    text = PIECE + HALF
    for i in range(out_ref.shape[0]):
        out_ref[i, 0:PIECE, :] = piece
        for g in range(recv_ref.shape[0]):
            out_ref[i, PIECE + g * HALF : PIECE + (g + 1) * HALF, :] = recv_ref[g, PIECE:text, :]
            text_ref[i, g * 96 : (g + 1) * 96, :] = recv_ref[g, text:, :]


def image_body(
    idx_ref, send_ref, recv_ref, other_ref, gain_ref, out_ref, lat_ref, s_ref, v_ref, m_ref, own_ref
):
    tokens = lat_ref.shape[1]
    chunk = 1024
    n_chunks = tokens // chunk
    ones = jnp.where(lax.broadcasted_iota(jnp.int32, (MROWS - CHANS, HD), 0) == 0, 1.0, 0.0).astype(BF16)
    n_far = (recv_ref.shape[1] - PIECE) // HALF
    for i in range(tokens // HD):
        near, first = i // n_far, (i % n_far) * HALF
        at = slice(i * HD, (i + 1) * HD)
        lat_ref[0:HALF, at] = recv_ref[near, PIECE + first : PIECE + first + HALF, :]
        lat_ref[HALF:CHANS, at] = other_ref[near, first : first + HALF, :]
        lat_ref[CHANS:MROWS, at] = ones
    for i in range(recv_ref.shape[0]):
        m_ref[i * PIECE : (i + 1) * PIECE, :] = recv_ref[i, 0:PIECE, :].astype(F32)
    own_ref[...] = send_ref[0:CHANS, :].astype(F32)

    def reordered(ref, base):
        core = idx_ref[1] & 1
        return jnp.concatenate(
            [ref[pl.ds(pl.multiple_of(k * HALF + base, HALF), HALF), :] for k in (core, 1 - core)], axis=0
        )

    own = jnp.concatenate([reordered(own_ref, 0).astype(BF16), ones], axis=0)
    score_scale = HD ** (-0.5) * 1.4426950408889634
    biases = m_ref[9 * CHANS : 9 * CHANS + 16, :]

    def weight(j):
        block = reordered(m_ref, j * CHANS)
        pad = jnp.zeros((HD - CHANS - 1, HD), F32)
        return jnp.concatenate([block, biases[j : j + 1, :], pad], axis=0).T[:, 0:MROWS].astype(BF16)

    q_image, w_k, w_v = [], [], []
    for head in range(3):
        q_t = dot(weight(head), own)
        q_t = q_t * lax.rsqrt(jnp.mean(q_t * q_t, axis=0, keepdims=True) + 1e-06)
        q = q_t.T * (gain_ref[0:1, :] * score_scale)
        out_ref[head, 3] = q
        q_image.append((q * gain_ref[1:2, :]).astype(BF16))
        w_k.append(weight(3 + head))
        w_v.append(weight(6 + head))
    rows = q_image[0].shape[0]

    def score_step(c, tops):
        at = pl.ds(pl.multiple_of(c * chunk, chunk), chunk)
        lat = lat_ref[:, at]
        out = []
        for head in range(3):
            k_t = dot(w_k[head], lat)
            k_t = k_t * lax.rsqrt(jnp.mean(k_t * k_t, axis=0, keepdims=True) + 1e-06)
            v_ref[head, :, at] = dot(w_v[head], lat).astype(BF16)
            s = dot(q_image[head], k_t.astype(BF16))
            s_ref[head, :, at] = s
            top = tops[head]
            for j in range(chunk // HD):
                top = jnp.maximum(top, s[:, j * HD : (j + 1) * HD])
            out.append(top)
        return tuple(out)

    tops = lax.fori_loop(0, n_chunks, score_step, (jnp.full((rows, HD), -3e38, F32),) * 3)
    for head in range(3):
        out_ref[head, 0] = jnp.zeros((rows, HD), F32)
        out_ref[head, 1] = jnp.zeros((rows, HD), F32)
        out_ref[head, 2] = jnp.broadcast_to(jnp.max(tops[head], axis=1, keepdims=True), (rows, HD))

    def mix_step(c, carry):
        at = pl.ds(pl.multiple_of(c * chunk, chunk), chunk)
        for head in range(3):
            p = jnp.exp2(s_ref[head, :, at] - out_ref[head, 2][:, 0:1])
            total = out_ref[head, 1]
            for j in range(chunk // HD):
                total = total + p[:, j * HD : (j + 1) * HD]
            out_ref[head, 1] = total
            out_ref[head, 0] += dot(p.astype(BF16), v_ref[head, :, at], NT)
        return carry

    lax.fori_loop(0, n_chunks, mix_step, 0)


def text_body(image_ref, text_ref, out_w_ref, y_ref, att_ref):
    step = 512

    def block(first):
        return text_ref[:, first : first + 16, :].reshape(text_ref.shape[0] * 16, HD)

    for head in range(3):
        s = dot(image_ref[head, 3].astype(BF16), block(head * 16), NT)
        image_top = image_ref[head, 2]
        top = jnp.maximum(image_top, jnp.max(s, axis=1, keepdims=True))
        keep = jnp.exp2(image_top - top)
        p = jnp.exp2(s - top[:, 0:1])
        acc = image_ref[head, 0] * keep + dot(p.astype(BF16), block(48 + head * 16))
        total = jnp.sum(image_ref[head, 1] * keep, axis=1, keepdims=True) + jnp.sum(p, axis=1, keepdims=True)
        att_ref[:, head * HD : (head + 1) * HD] = (acc / total).astype(BF16)
    att = att_ref[...]
    for j in range(out_w_ref.shape[1] // step):
        y = dot(att, out_w_ref[:, j * step : (j + 1) * step]).astype(BF16)
        y_ref[:, :, j * step : (j + 1) * step] = y.reshape(y_ref.shape[0], y_ref.shape[1], step)


def velocity_body(idx_ref, parts_ref, noised_ref, embed_ref, mod_ref, final_t_ref, v_ref):
    total = parts_ref[0].astype(F32)
    for i in range(1, parts_ref.shape[0]):
        total = total + parts_ref[i].astype(F32)
    own_rows = total.shape[0]
    own = noised_ref[pl.ds(pl.multiple_of(idx_ref[1] * own_rows, own_rows), own_rows), :].astype(BF16)
    h = dot(own, embed_ref[...]) + mod_ref[2] * total
    width = h.shape[1]
    h = h - jnp.sum(h, axis=1, keepdims=True) / width
    var = jnp.sum(h * h, axis=1, keepdims=True) / width
    v = dot((h * lax.rsqrt(var + 1e-06)).astype(BF16), final_t_ref[...], NT)
    v = jnp.concatenate([v[0:8, :], v[8:16, :]], axis=1)
    for i in range(v_ref.shape[0]):
        v_ref[i] = v


def grad_body(idx_ref, both_ref, gap_ref, hidden_ref, gen_t_ref, piece_ref, share_ref, raw_ref, diff_ref, grad_ref):
    n_mp = both_ref.shape[0] // 2
    chans = gap_ref.shape[1]

    def rows(first):
        blocks = []
        for i in range(first, first + n_mp):
            blocks += [both_ref[i][:, 0:chans], both_ref[i][:, chans : 2 * chans]]
        return jnp.concatenate(blocks, axis=0)

    teacher, student = rows(0), rows(n_mp)
    spread = jnp.abs(gap_ref[...] + noise_scale_of(idx_ref[3], gap_ref.shape) * teacher)
    spread = jnp.sum(jnp.sum(spread, axis=1, keepdims=True), axis=0, keepdims=True)
    spread = jnp.broadcast_to(spread, (8, HD))
    diff = teacher - student
    diff_ref[...] = diff.T
    half = chans // 2
    share = diff_ref[pl.ds(pl.multiple_of(idx_ref[2] * half, half), half), :]
    share_ref[...] = share
    cols = grad_ref.shape[1]
    hidden = hidden_ref[:, pl.ds(pl.multiple_of(idx_ref[1] * cols, HD), cols)]
    grad_ref[...] = dot(share.astype(BF16), hidden)
    for p in range(4):
        terms = [grad_ref[8 * p : 8 * p + 8, g * HD : (g + 1) * HD] for g in range(3)]
        block = in_parts(jnp.concatenate([*terms, spread], axis=0))
        for y_hi in range(2):
            piece_ref[2 * p + y_hi] = block
    feats = raw_ref.shape[1]
    raw_ref[...] = dot(diff.astype(BF16), gen_t_ref[:, pl.ds(pl.multiple_of(idx_ref[2] * feats, HD), feats)])


def in_parts(block):
    row = lax.broadcasted_iota(jnp.int32, block.shape, 0)
    high = block.astype(BF16).astype(F32)
    mid = (block - high).astype(BF16).astype(F32)
    low = block - high - mid
    return jnp.where(row == 25, mid, jnp.where(row == 26, low, high)).astype(BF16)


def near_body(recv_ref, out_ref):
    total = recv_ref[0].astype(F32)
    for i in range(1, recv_ref.shape[0]):
        total = total + recv_ref[i].astype(F32)
    number = total[24:25, :] + total[25:26, :] + total[26:27, :]
    out = in_parts(jnp.concatenate([total[0:24, :], jnp.broadcast_to(number, (8, HD))], axis=0))
    for i in range(out_ref.shape[0]):
        out_ref[i] = out


def last_body(idx_ref, recv_ref, share_ref, raw_ref, x_ref, hidden_ref, gen_ref, *, entries):
    totals = []
    for p in range(4):
        total = recv_ref[p].astype(F32)
        for g in range(1, recv_ref.shape[0] // 4):
            total = total + recv_ref[4 * g + p].astype(F32)
        totals.append(total)
    spread = totals[0][24:25, 0:1] + totals[0][25:26, 0:1] + totals[0][26:27, 0:1]
    factor = noise_scale_of(idx_ref[3], (1, 1)) / (spread / entries + 1e-06)
    x_ref[...] = share_ref[...] * factor
    hidden_ref[...] = (raw_ref[...] * factor).astype(BF16)
    for p in range(4):
        for g in range(3):
            gen_ref[8 * p : 8 * p + 8, g * HD : (g + 1) * HD] = totals[p][8 * g : 8 * g + 8, :] * factor


def exchange(array, axis):
    return lax.all_to_all(array, axis, 0, 0, tiled=True)


def on_device(
    gen_hidden, w_gen, noise_latent, level_index, w_embed, modulation, w_qkv, qk_gain, text_kv, w_out, w_final
):
    rows_here, width = gen_hidden.shape
    n_seq, n_far, n_mp = lax.axis_size(SEQ), lax.axis_size("z_far"), lax.axis_size("mp")
    chans = w_gen.shape[1]
    tokens = rows_here * n_seq
    sds = jax.ShapeDtypeStruct
    mods = jnp.transpose(modulation, (1, 0, 2))
    embed = w_embed[0]
    gen_t = w_gen.T
    idx = jnp.stack(
        [lax.axis_index(SEQ), lax.axis_index("mp"), lax.axis_index("role"), level_index[0]]
    ).astype(jnp.int32)
    near_groups = [[8 * g + i for i in range(8)] for g in range(n_seq // 8)]
    far_groups = [[8 * g + i for g in range(n_seq // 8)] for i in range(8)]

    n_far = n_seq // 8
    payload, idx_late = call(
        weight_body,
        (sds((8, PIECE, HD), BF16), sds(idx.shape, jnp.int32)),
        (idx, embed, mods, jnp.transpose(w_qkv[0], (1, 0, 2))),
        scratch=(pltpu.VMEM((8 * PIECE, HD), F32),),
        smem=1,
        limit=60,
    )
    noised, gap, send = call(
        latent_body,
        (
            sds((rows_here, chans), F32),
            sds((rows_here, chans), F32),
            sds((chans + 96, HD), BF16),
        ),
        (idx_late, gen_hidden, gen_t, noise_latent.T, embed, text_kv[0]),
        smem=1,
        limit=60,
    )
    pieces = exchange(payload, NEAR)
    pieces = call(far_body, sds((n_far, PIECE + HALF + 96, HD), BF16), (idx, pieces, send), smem=1)
    pieces = exchange(pieces, "z_far")
    pieces, text = call(
        spread_body,
        (sds((8, PIECE + n_far * HALF, HD), BF16), sds((8, n_far * 96, HD), BF16)),
        (pieces,),
    )
    pieces = exchange(pieces, NEAR)
    text = exchange(text, NEAR).reshape(n_seq, 96, HD)
    other = lax.ppermute(pieces[:, PIECE:, :], "mp", [(i, i ^ 1) for i in range(n_mp)])

    image = call(
        image_body,
        sds((3, 4, rows_here, HD), F32),
        (idx, send, pieces, other, qk_gain[0]),
        scratch=(
            pltpu.VMEM((MROWS, tokens), BF16),
            pltpu.VMEM((3, rows_here, tokens), F32),
            pltpu.VMEM((3, HD, tokens), BF16),
            pltpu.VMEM((8 * PIECE, HD), F32),
            pltpu.VMEM((chans, HD), F32),
        ),
        smem=1,
    )
    own_rows = rows_here // n_mp
    y = call(
        text_body,
        sds((n_mp, own_rows, width), BF16),
        (image, text, w_out[0]),
        scratch=(pltpu.VMEM((rows_here, 3 * HD), BF16),),
    )
    parts = exchange(y, "mp")
    velocity = call(
        velocity_body,
        sds((2 * n_mp, 8, 2 * chans), F32),
        (idx, parts, noised, embed, mods, w_final[0].T),
        smem=1,
    )
    both = exchange(velocity, ("role", "mp"))
    half = chans // 2
    grad_piece, share, raw = call(
        grad_body,
        (sds((8, 32, HD), BF16), sds((half, rows_here), F32), sds((rows_here, width // 2), F32)),
        (idx, both, gap, gen_hidden, gen_t),
        scratch=(pltpu.VMEM((chans, rows_here), F32), pltpu.VMEM((half, 3 * HD), F32)),
        smem=1,
    )
    near = exchange(grad_piece, NEAR)
    near = call(near_body, sds((n_seq // 2, 32, HD), BF16), (near,))
    everything = exchange(near, ("z_far", "z_near"))

    def last(*refs):
        last_body(*refs, entries=tokens * chans)

    grad_x_t, grad_hidden, grad_gen_t = call(
        last,
        (sds((half, rows_here), F32), sds((rows_here, width // 2), BF16), sds((half, 3 * HD), F32)),
        (idx, everything, share, raw),
        smem=1,
    )
    return grad_x_t.T, grad_hidden, grad_gen_t.T


def solution(mesh):
    n_role, n_seq, n_mp = (mesh.shape[name] for name in ("role", "seq", "mp"))
    names = ("role", *SEQ, "mp")
    mesh = jax.sharding.Mesh(mesh.devices.reshape(n_role, n_seq // 8, 4, 2, n_mp), names)
    placed = (
        P(SEQ, None),
        P(),
        P(SEQ, None),
        P(),
        P("role", None, None),
        P("role", None, None),
        P("role", SEQ, None, "mp"),
        P("role", None, None),
        P("role", SEQ, None, "mp"),
        P("role", "mp", None),
        P("role", None, None),
    )
    return jax.shard_map(
        on_device,
        mesh=mesh,
        in_specs=placed,
        out_specs=(P(SEQ, "role"), P(SEQ, "role"), P("mp", "role")),
        check_vma=False,
    )
```

```python
import jax
import jax.numpy as jnp
from jax import lax
from jax.experimental import pallas as pl
from jax.experimental.pallas import tpu as pltpu
from jax.sharding import PartitionSpec as P

LEVELS = 1000
HD = 128
SEQ = ("z_far", "z_near", "y_hi")
NEAR = ("z_near", "y_hi")
CHANS = 64
HALF = CHANS // 2
MROWS = 80
PIECE = 80
F32 = jnp.float32
BF16 = jnp.bfloat16
NN = (((1,), (0,)), ((), ()))
NT = (((1,), (1,)), ((), ()))


def dot(a, b, dims=NN):
    return lax.dot_general(a, b, dims, preferred_element_type=F32)


def call(body, out_shape, args, scratch=(), smem=0, limit=24):
    vmem = pl.BlockSpec(memory_space=pltpu.VMEM)
    scalars = pl.BlockSpec(memory_space=pltpu.SMEM)
    return pl.pallas_call(
        body,
        out_shape=out_shape,
        in_specs=[scalars if i < smem else vmem for i in range(len(args))],
        out_specs=jax.tree.map(lambda out: scalars if out.dtype == jnp.int32 else vmem, out_shape),
        scratch_shapes=list(scratch),
        compiler_params=pltpu.CompilerParams(vmem_limit_bytes=limit * 1024 * 1024),
    )(*args)


def seq_here():
    return (lax.axis_index("z_far") * 4 + lax.axis_index("z_near")) * 2 + lax.axis_index("y_hi")


def noise_scale_of(level, shape):
    time_frac = (jnp.full(shape, level, jnp.int32).astype(F32) + 1.0) / (LEVELS + 1.0)
    return 3.0 * time_frac / (1.0 + 2.0 * time_frac)


def weight_body(level_ref, embed_ref, mod_ref, qkv_ref, payload_ref, level_out_ref, term_ref):
    width = embed_ref.shape[1]
    features = qkv_ref.shape[1]
    offset = seq_here() * features
    start = pl.multiple_of(jnp.minimum((offset >> 7) << 7, width - 256), HD)
    mean = jnp.sum(embed_ref[...].astype(F32), axis=1, keepdims=True) / width
    window = embed_ref[:, pl.ds(start, 256)].astype(F32)
    scale = 1.0 + mod_ref[1, :, pl.ds(start, 256)]
    shift = mod_ref[0, :, pl.ds(start, 256)]
    rows = jnp.concatenate(
        [(window - mean) * scale, shift, jnp.zeros((MROWS - CHANS - 1, 256), F32)], axis=0
    )
    select = jnp.where(
        lax.broadcasted_iota(jnp.int32, (256, features), 0)
        == lax.broadcasted_iota(jnp.int32, (256, features), 1) + (offset - start),
        1.0,
        0.0,
    ).astype(BF16)
    high = rows.astype(BF16)
    low = dot((rows - high.astype(F32)).astype(BF16), select).astype(BF16)
    high = dot(high, select).astype(BF16)
    for part in range(3):
        term = dot(high, qkv_ref[part]) + dot(low, qkv_ref[part])
        for head in range(3):
            j = part * 3 + head
            block = term[:, head * HD : (head + 1) * HD]
            term_ref[j * CHANS : (j + 1) * CHANS, :] = block[0:CHANS, :]
            term_ref[9 * CHANS + j : 9 * CHANS + j + 1, :] = block[CHANS : CHANS + 1, :]
    term_ref[9 * CHANS + 9 :, :] = jnp.zeros((term_ref.shape[0] - 9 * CHANS - 9, HD), F32)
    for p in range(payload_ref.shape[0]):
        payload_ref[p] = term_ref[p * PIECE : (p + 1) * PIECE, :].astype(BF16)
    level_out_ref[0] = level_ref[0]


def latent_body(
    level_ref, hidden_ref, gen_t_ref, noise_t_ref, embed_ref, text_in_ref, noised_ref, gap_ref, send_ref
):
    x_t = dot(gen_t_ref[...], hidden_ref[...], NT)
    noise_scale = noise_scale_of(level_ref[0], x_t.shape)
    noised_t = ((1.0 - noise_scale) * x_t + noise_scale * noise_t_ref[...].astype(F32)).astype(BF16)
    noised = noised_t.astype(F32).T
    noised_ref[...] = noised
    gap_ref[...] = (x_t - noised_t.astype(F32)).T
    h = dot(noised.astype(BF16), embed_ref[...])
    width = h.shape[1]
    row_mean = jnp.sum(h, axis=1, keepdims=True) / width
    row_var = jnp.sum(jnp.square(h - row_mean), axis=1, keepdims=True) / width
    send_ref[0:CHANS, :] = (noised * lax.rsqrt(row_var + 1e-06)).T.astype(BF16)
    text = text_in_ref[...].astype(F32)
    for j in range(6):
        block = text[:, j // 3, (j % 3) * HD : (j % 3 + 1) * HD]
        send_ref[CHANS + j * 16 : CHANS + (j + 1) * 16, :] = block.astype(BF16)


def total_of(ref, rows):
    total = ref[0, 0:rows, :].astype(F32)
    for i in range(1, ref.shape[0]):
        total = total + ref[i, 0:rows, :].astype(F32)
    return total.astype(BF16)


def far_body(recv_ref, send_ref, out_ref):
    piece = total_of(recv_ref, PIECE)
    channels = send_ref[pl.ds(pl.multiple_of((lax.axis_index("mp") & 1) * HALF, HALF), HALF), :]
    for i in range(out_ref.shape[0]):
        out_ref[i, 0:PIECE, :] = piece
        out_ref[i, PIECE : PIECE + HALF, :] = channels
        out_ref[i, PIECE + HALF :, :] = send_ref[CHANS:, :]


def spread_body(recv_ref, out_ref, text_ref):
    piece = total_of(recv_ref, PIECE)
    text = PIECE + HALF
    for i in range(out_ref.shape[0]):
        out_ref[i, 0:PIECE, :] = piece
        for g in range(recv_ref.shape[0]):
            out_ref[i, PIECE + g * HALF : PIECE + (g + 1) * HALF, :] = recv_ref[g, PIECE:text, :]
            text_ref[i, g * 96 : (g + 1) * 96, :] = recv_ref[g, text:, :]


def image_body(
    send_ref, recv_ref, other_ref, gain_ref, out_ref, lat_ref, s_ref, v_ref, m_ref, own_ref
):
    tokens = lat_ref.shape[1]
    chunk = 1024
    n_chunks = tokens // chunk
    ones = jnp.where(lax.broadcasted_iota(jnp.int32, (MROWS - CHANS, HD), 0) == 0, 1.0, 0.0).astype(BF16)
    n_far = (recv_ref.shape[1] - PIECE) // HALF
    for i in range(tokens // HD):
        near, first = i // n_far, (i % n_far) * HALF
        at = slice(i * HD, (i + 1) * HD)
        lat_ref[0:HALF, at] = recv_ref[near, PIECE + first : PIECE + first + HALF, :]
        lat_ref[HALF:CHANS, at] = other_ref[near, first : first + HALF, :]
        lat_ref[CHANS:MROWS, at] = ones
    for i in range(recv_ref.shape[0]):
        m_ref[i * PIECE : (i + 1) * PIECE, :] = recv_ref[i, 0:PIECE, :].astype(F32)
    own_ref[...] = send_ref[0:CHANS, :].astype(F32)

    def reordered(ref, base):
        core = lax.axis_index("mp") & 1
        return jnp.concatenate(
            [ref[pl.ds(pl.multiple_of(k * HALF + base, HALF), HALF), :] for k in (core, 1 - core)], axis=0
        )

    own = jnp.concatenate([reordered(own_ref, 0).astype(BF16), ones], axis=0)
    score_scale = HD ** (-0.5) * 1.4426950408889634
    biases = m_ref[9 * CHANS : 9 * CHANS + 16, :]

    def weight(j):
        block = reordered(m_ref, j * CHANS)
        pad = jnp.zeros((HD - CHANS - 1, HD), F32)
        return jnp.concatenate([block, biases[j : j + 1, :], pad], axis=0).T[:, 0:MROWS].astype(BF16)

    q_image, w_k, w_v = [], [], []
    for head in range(3):
        q_t = dot(weight(head), own)
        q_t = q_t * lax.rsqrt(jnp.mean(q_t * q_t, axis=0, keepdims=True) + 1e-06)
        q = q_t.T * (gain_ref[0:1, :] * score_scale)
        out_ref[head, 3] = q
        q_image.append((q * gain_ref[1:2, :]).astype(BF16))
        w_k.append(weight(3 + head))
        w_v.append(weight(6 + head))
    rows = q_image[0].shape[0]

    def score_step(c, tops):
        at = pl.ds(pl.multiple_of(c * chunk, chunk), chunk)
        lat = lat_ref[:, at]
        out = []
        for head in range(3):
            k_t = dot(w_k[head], lat)
            k_t = k_t * lax.rsqrt(jnp.mean(k_t * k_t, axis=0, keepdims=True) + 1e-06)
            v_ref[head, :, at] = dot(w_v[head], lat).astype(BF16)
            s = dot(q_image[head], k_t.astype(BF16))
            s_ref[head, :, at] = s
            top = tops[head]
            for j in range(chunk // HD):
                top = jnp.maximum(top, s[:, j * HD : (j + 1) * HD])
            out.append(top)
        return tuple(out)

    tops = lax.fori_loop(0, n_chunks, score_step, (jnp.full((rows, HD), -3e38, F32),) * 3)
    for head in range(3):
        out_ref[head, 0] = jnp.zeros((rows, HD), F32)
        out_ref[head, 1] = jnp.zeros((rows, HD), F32)
        out_ref[head, 2] = jnp.broadcast_to(jnp.max(tops[head], axis=1, keepdims=True), (rows, HD))

    def mix_step(c, carry):
        at = pl.ds(pl.multiple_of(c * chunk, chunk), chunk)
        for head in range(3):
            p = jnp.exp2(s_ref[head, :, at] - out_ref[head, 2][:, 0:1])
            total = out_ref[head, 1]
            for j in range(chunk // HD):
                total = total + p[:, j * HD : (j + 1) * HD]
            out_ref[head, 1] = total
            out_ref[head, 0] += dot(p.astype(BF16), v_ref[head, :, at], NT)
        return carry

    lax.fori_loop(0, n_chunks, mix_step, 0)


def text_body(image_ref, text_ref, att_ref):
    def block(first):
        return text_ref[:, first : first + 16, :].reshape(text_ref.shape[0] * 16, HD)

    for head in range(3):
        s = dot(image_ref[head, 3].astype(BF16), block(head * 16), NT)
        image_top = image_ref[head, 2]
        top = jnp.maximum(image_top, jnp.max(s, axis=1, keepdims=True))
        keep = jnp.exp2(image_top - top)
        p = jnp.exp2(s - top[:, 0:1])
        acc = image_ref[head, 0] * keep + dot(p.astype(BF16), block(48 + head * 16))
        total = jnp.sum(image_ref[head, 1] * keep, axis=1, keepdims=True) + jnp.sum(p, axis=1, keepdims=True)
        att_ref[:, head * HD : (head + 1) * HD] = (acc / total).astype(BF16)


def velocity_body(parts_ref, noised_ref, embed_ref, mod_ref, final_t_ref, v_ref):
    total = parts_ref[0].astype(F32)
    for i in range(1, parts_ref.shape[0]):
        total = total + parts_ref[i].astype(F32)
    own_rows = total.shape[0]
    own = noised_ref[pl.ds(pl.multiple_of(lax.axis_index("mp") * own_rows, own_rows), own_rows), :].astype(BF16)
    h = dot(own, embed_ref[...]) + mod_ref[2] * total
    width = h.shape[1]
    h = h - jnp.sum(h, axis=1, keepdims=True) / width
    var = jnp.sum(h * h, axis=1, keepdims=True) / width
    v = dot((h * lax.rsqrt(var + 1e-06)).astype(BF16), final_t_ref[...], NT)
    v = jnp.concatenate([v[0:8, :], v[8:16, :]], axis=1)
    for i in range(v_ref.shape[0]):
        v_ref[i] = v


def grad_body(level_ref, both_ref, gap_ref, hidden_ref, gen_t_ref, piece_ref, share_ref, raw_ref, diff_ref, grad_ref):
    n_mp = both_ref.shape[0] // 2
    chans = gap_ref.shape[1]

    def rows(first):
        blocks = []
        for i in range(first, first + n_mp):
            blocks += [both_ref[i][:, 0:chans], both_ref[i][:, chans : 2 * chans]]
        return jnp.concatenate(blocks, axis=0)

    teacher, student = rows(0), rows(n_mp)
    spread = jnp.abs(gap_ref[...] + noise_scale_of(level_ref[0], gap_ref.shape) * teacher)
    spread = jnp.sum(jnp.sum(spread, axis=1, keepdims=True), axis=0, keepdims=True)
    spread = jnp.broadcast_to(spread, (8, HD))
    diff = teacher - student
    diff_ref[...] = diff.T
    half = chans // 2
    share = diff_ref[pl.ds(pl.multiple_of(lax.axis_index("role") * half, half), half), :]
    share_ref[...] = share
    cols = grad_ref.shape[1]
    hidden = hidden_ref[:, pl.ds(pl.multiple_of(lax.axis_index("mp") * cols, HD), cols)]
    grad_ref[...] = dot(share.astype(BF16), hidden)
    for p in range(4):
        terms = [grad_ref[8 * p : 8 * p + 8, g * HD : (g + 1) * HD] for g in range(3)]
        block = in_parts(jnp.concatenate([*terms, spread], axis=0))
        for y_hi in range(2):
            piece_ref[2 * p + y_hi] = block
    feats = raw_ref.shape[1]
    raw_ref[...] = dot(diff.astype(BF16), gen_t_ref[:, pl.ds(pl.multiple_of(lax.axis_index("role") * feats, HD), feats)])


def in_parts(block):
    row = lax.broadcasted_iota(jnp.int32, block.shape, 0)
    high = block.astype(BF16).astype(F32)
    mid = (block - high).astype(BF16).astype(F32)
    low = block - high - mid
    return jnp.where(row == 25, mid, jnp.where(row == 26, low, high)).astype(BF16)


def near_body(recv_ref, out_ref):
    total = recv_ref[0].astype(F32)
    for i in range(1, recv_ref.shape[0]):
        total = total + recv_ref[i].astype(F32)
    number = total[24:25, :] + total[25:26, :] + total[26:27, :]
    out = in_parts(jnp.concatenate([total[0:24, :], jnp.broadcast_to(number, (8, HD))], axis=0))
    for i in range(out_ref.shape[0]):
        out_ref[i] = out


def last_body(level_ref, recv_ref, share_ref, raw_ref, x_ref, hidden_ref, gen_ref, *, entries):
    totals = []
    for p in range(4):
        total = recv_ref[p].astype(F32)
        for g in range(1, recv_ref.shape[0] // 4):
            total = total + recv_ref[4 * g + p].astype(F32)
        totals.append(total)
    spread = totals[0][24:25, 0:1] + totals[0][25:26, 0:1] + totals[0][26:27, 0:1]
    factor = noise_scale_of(level_ref[0], (1, 1)) / (spread / entries + 1e-06)
    x_ref[...] = share_ref[...] * factor
    hidden_ref[...] = (raw_ref[...] * factor).astype(BF16)
    for p in range(4):
        for g in range(3):
            gen_ref[8 * p : 8 * p + 8, g * HD : (g + 1) * HD] = totals[p][8 * g : 8 * g + 8, :] * factor


def exchange(array, axis):
    return lax.all_to_all(array, axis, 0, 0, tiled=True)


def on_device(
    gen_hidden, w_gen, noise_latent, level_index, w_embed, modulation, w_qkv, qk_gain, text_kv, w_out, w_final
):
    rows_here, width = gen_hidden.shape
    n_seq, n_far, n_mp = lax.axis_size(SEQ), lax.axis_size("z_far"), lax.axis_size("mp")
    chans = w_gen.shape[1]
    tokens = rows_here * n_seq
    sds = jax.ShapeDtypeStruct
    mods = jnp.transpose(modulation, (1, 0, 2))
    embed = w_embed[0]
    gen_t = w_gen.T
    payload, level_late = call(
        weight_body,
        (sds((8, PIECE, HD), BF16), sds((1,), jnp.int32)),
        (level_index, embed, mods, jnp.transpose(w_qkv[0], (1, 0, 2))),
        scratch=(pltpu.VMEM((8 * PIECE, HD), F32),),
        smem=1,
        limit=60,
    )
    noised, gap, send = call(
        latent_body,
        (
            sds((rows_here, chans), F32),
            sds((rows_here, chans), F32),
            sds((chans + 96, HD), BF16),
        ),
        (level_late, gen_hidden, gen_t, noise_latent.T, embed, text_kv[0]),
        smem=1,
        limit=60,
    )
    pieces = exchange(payload, NEAR)
    pieces = call(far_body, sds((n_far, PIECE + HALF + 96, HD), BF16), (pieces, send), limit=60)
    pieces = exchange(pieces, "z_far")
    pieces, text = call(
        spread_body,
        (sds((8, PIECE + n_far * HALF, HD), BF16), sds((8, n_far * 96, HD), BF16)),
        (pieces,),
    )
    pieces = exchange(pieces, NEAR)
    text = exchange(text, NEAR).reshape(n_seq, 96, HD)
    other = lax.ppermute(pieces[:, PIECE:, :], "mp", [(i, i ^ 1) for i in range(n_mp)])

    image = call(
        image_body,
        sds((3, 4, rows_here, HD), F32),
        (send, pieces, other, qk_gain[0]),
        scratch=(
            pltpu.VMEM((MROWS, tokens), BF16),
            pltpu.VMEM((3, rows_here, tokens), F32),
            pltpu.VMEM((3, HD, tokens), BF16),
            pltpu.VMEM((8 * PIECE, HD), F32),
            pltpu.VMEM((chans, HD), F32),
        ),
    )
    own_rows = rows_here // n_mp
    attended = call(text_body, sds((rows_here, 3 * HD), BF16), (image, text))
    y = dot(attended, w_out[0]).astype(BF16).reshape(n_mp, own_rows, width)
    parts = exchange(y, "mp")
    velocity = call(
        velocity_body,
        sds((2 * n_mp, 8, 2 * chans), F32),
        (parts, noised, embed, mods, w_final[0].T),
    )
    both = exchange(velocity, ("role", "mp"))
    half = chans // 2
    grad_piece, share, raw = call(
        grad_body,
        (sds((8, 32, HD), BF16), sds((half, rows_here), F32), sds((rows_here, width // 2), F32)),
        (level_index, both, gap, gen_hidden, gen_t),
        scratch=(pltpu.VMEM((chans, rows_here), F32), pltpu.VMEM((half, 3 * HD), F32)),
        smem=1,
    )
    near = exchange(grad_piece, NEAR)
    near = call(near_body, sds((n_seq // 2, 32, HD), BF16), (near,))
    everything = exchange(near, ("z_far", "z_near"))

    def last(*refs):
        last_body(*refs, entries=tokens * chans)

    grad_x_t, grad_hidden, grad_gen_t = call(
        last,
        (sds((half, rows_here), F32), sds((rows_here, width // 2), BF16), sds((half, 3 * HD), F32)),
        (level_index, everything, share, raw),
        smem=1,
    )
    return grad_x_t.T, grad_hidden, grad_gen_t.T


def solution(mesh):
    n_role, n_seq, n_mp = (mesh.shape[name] for name in ("role", "seq", "mp"))
    names = ("role", *SEQ, "mp")
    mesh = jax.sharding.Mesh(mesh.devices.reshape(n_role, n_seq // 8, 4, 2, n_mp), names)
    placed = (
        P(SEQ, None),
        P(),
        P(SEQ, None),
        P(),
        P("role", None, None),
        P("role", None, None),
        P("role", SEQ, None, "mp"),
        P("role", None, None),
        P("role", SEQ, None, "mp"),
        P("role", "mp", None),
        P("role", None, None),
    )
    return jax.shard_map(
        on_device,
        mesh=mesh,
        in_specs=placed,
        out_specs=(P(SEQ, "role"), P(SEQ, "role"), P("mp", "role")),
        check_vma=False,
    )
```

```python
import jax
import jax.numpy as jnp
from jax import lax
from jax.experimental import pallas as pl
from jax.experimental.pallas import tpu as pltpu
from jax.sharding import PartitionSpec as P

LEVELS = 1000
HD = 128
SEQ = ("z_far", "z_near", "y_hi")
NEAR = ("z_near", "y_hi")
CHANS = 64
HALF = CHANS // 2
MROWS = 80
PIECE = 80
F32 = jnp.float32
BF16 = jnp.bfloat16
NN = (((1,), (0,)), ((), ()))
NT = (((1,), (1,)), ((), ()))


def dot(a, b, dims=NN):
    return lax.dot_general(a, b, dims, preferred_element_type=F32)


def call(body, out_shape, args, scratch=(), smem=0, limit=24):
    vmem = pl.BlockSpec(memory_space=pltpu.VMEM)
    scalars = pl.BlockSpec(memory_space=pltpu.SMEM)
    return pl.pallas_call(
        body,
        out_shape=out_shape,
        in_specs=[scalars if i < smem else vmem for i in range(len(args))],
        out_specs=jax.tree.map(lambda out: scalars if out.dtype == jnp.int32 else vmem, out_shape),
        scratch_shapes=list(scratch),
        compiler_params=pltpu.CompilerParams(vmem_limit_bytes=limit * 1024 * 1024),
    )(*args)


def seq_here():
    return (lax.axis_index("z_far") * 4 + lax.axis_index("z_near")) * 2 + lax.axis_index("y_hi")


def noise_scale_of(level, shape):
    time_frac = (jnp.full(shape, level, jnp.int32).astype(F32) + 1.0) / (LEVELS + 1.0)
    return 3.0 * time_frac / (1.0 + 2.0 * time_frac)


def weight_body(level_ref, embed_ref, mod_ref, qkv_ref, payload_ref, level_out_ref, term_ref):
    width = embed_ref.shape[1]
    features = qkv_ref.shape[1]
    offset = seq_here() * features
    start = pl.multiple_of(jnp.minimum((offset >> 7) << 7, width - 256), HD)
    mean = jnp.sum(embed_ref[...].astype(F32), axis=1, keepdims=True) / width
    window = embed_ref[:, pl.ds(start, 256)].astype(F32)
    scale = 1.0 + mod_ref[1, :, pl.ds(start, 256)]
    shift = mod_ref[0, :, pl.ds(start, 256)]
    rows = jnp.concatenate(
        [(window - mean) * scale, shift, jnp.zeros((MROWS - CHANS - 1, 256), F32)], axis=0
    )
    select = jnp.where(
        lax.broadcasted_iota(jnp.int32, (256, features), 0)
        == lax.broadcasted_iota(jnp.int32, (256, features), 1) + (offset - start),
        1.0,
        0.0,
    ).astype(BF16)
    high = rows.astype(BF16)
    low = dot((rows - high.astype(F32)).astype(BF16), select).astype(BF16)
    high = dot(high, select).astype(BF16)
    for part in range(3):
        term = dot(high, qkv_ref[part]) + dot(low, qkv_ref[part])
        for head in range(3):
            j = part * 3 + head
            block = term[:, head * HD : (head + 1) * HD]
            term_ref[j * CHANS : (j + 1) * CHANS, :] = block[0:CHANS, :]
            term_ref[9 * CHANS + j : 9 * CHANS + j + 1, :] = block[CHANS : CHANS + 1, :]
    term_ref[9 * CHANS + 9 :, :] = jnp.zeros((term_ref.shape[0] - 9 * CHANS - 9, HD), F32)
    for p in range(payload_ref.shape[0]):
        payload_ref[p] = term_ref[p * PIECE : (p + 1) * PIECE, :].astype(BF16)
    level_out_ref[0] = level_ref[0]


def latent_body(
    level_ref, hidden_ref, gen_t_ref, noise_t_ref, embed_ref, text_in_ref, noised_ref, gap_ref, send_ref
):
    x_t = dot(gen_t_ref[...], hidden_ref[...], NT)
    noise_scale = noise_scale_of(level_ref[0], x_t.shape)
    noised_t = ((1.0 - noise_scale) * x_t + noise_scale * noise_t_ref[...].astype(F32)).astype(BF16)
    noised = noised_t.astype(F32).T
    noised_ref[...] = noised
    gap_ref[...] = (x_t - noised_t.astype(F32)).T
    h = dot(noised.astype(BF16), embed_ref[...])
    width = h.shape[1]
    row_mean = jnp.sum(h, axis=1, keepdims=True) / width
    row_var = jnp.sum(jnp.square(h - row_mean), axis=1, keepdims=True) / width
    send_ref[0:CHANS, :] = (noised * lax.rsqrt(row_var + 1e-06)).T.astype(BF16)
    text = text_in_ref[...].astype(F32)
    for j in range(6):
        block = text[:, j // 3, (j % 3) * HD : (j % 3 + 1) * HD]
        send_ref[CHANS + j * 16 : CHANS + (j + 1) * 16, :] = block.astype(BF16)


def total_of(ref, rows):
    total = ref[0, 0:rows, :].astype(F32)
    for i in range(1, ref.shape[0]):
        total = total + ref[i, 0:rows, :].astype(F32)
    return total.astype(BF16)


def far_body(recv_ref, send_ref, out_ref):
    piece = total_of(recv_ref, PIECE)
    channels = send_ref[pl.ds(pl.multiple_of((lax.axis_index("mp") & 1) * HALF, HALF), HALF), :]
    for i in range(out_ref.shape[0]):
        out_ref[i, 0:PIECE, :] = piece
        out_ref[i, PIECE : PIECE + HALF, :] = channels
        out_ref[i, PIECE + HALF :, :] = send_ref[CHANS:, :]


def spread_body(recv_ref, out_ref, text_ref):
    piece = total_of(recv_ref, PIECE)
    text = PIECE + HALF
    for i in range(out_ref.shape[0]):
        out_ref[i, 0:PIECE, :] = piece
        for g in range(recv_ref.shape[0]):
            out_ref[i, PIECE + g * HALF : PIECE + (g + 1) * HALF, :] = recv_ref[g, PIECE:text, :]
            text_ref[i, g * 96 : (g + 1) * 96, :] = recv_ref[g, text:, :]


def image_body(
    send_ref, recv_ref, other_ref, gain_ref, out_ref, lat_ref, s_ref, v_ref, m_ref, own_ref, sum_ref
):
    tokens = lat_ref.shape[1]
    chunk = 1024
    n_chunks = tokens // chunk
    ones = jnp.where(lax.broadcasted_iota(jnp.int32, (MROWS - CHANS, HD), 0) == 0, 1.0, 0.0).astype(BF16)
    n_far = (recv_ref.shape[1] - PIECE) // HALF
    for i in range(tokens // HD):
        near, first = i // n_far, (i % n_far) * HALF
        at = slice(i * HD, (i + 1) * HD)
        lat_ref[0:HALF, at] = recv_ref[near, PIECE + first : PIECE + first + HALF, :]
        lat_ref[HALF:CHANS, at] = other_ref[near, first : first + HALF, :]
        lat_ref[CHANS:MROWS, at] = ones
    for i in range(recv_ref.shape[0]):
        m_ref[i * PIECE : (i + 1) * PIECE, :] = recv_ref[i, 0:PIECE, :].astype(F32)
    own_ref[...] = send_ref[0:CHANS, :].astype(F32)

    def reordered(ref, base):
        core = lax.axis_index("mp") & 1
        return jnp.concatenate(
            [ref[pl.ds(pl.multiple_of(k * HALF + base, HALF), HALF), :] for k in (core, 1 - core)], axis=0
        )

    own = jnp.concatenate([reordered(own_ref, 0).astype(BF16), ones], axis=0)
    score_scale = HD ** (-0.5) * 1.4426950408889634
    biases = m_ref[9 * CHANS : 9 * CHANS + 16, :]

    def weight(j):
        block = reordered(m_ref, j * CHANS)
        pad = jnp.zeros((HD - CHANS - 1, HD), F32)
        return jnp.concatenate([block, biases[j : j + 1, :], pad], axis=0).T[:, 0:MROWS].astype(BF16)

    q_image, w_k, w_v = [], [], []
    for head in range(3):
        q_t = dot(weight(head), own)
        q_t = q_t * lax.rsqrt(jnp.mean(q_t * q_t, axis=0, keepdims=True) + 1e-06)
        q = q_t.T * (gain_ref[0:1, :] * score_scale)
        out_ref[3 + head] = q
        q_image.append((q * gain_ref[1:2, :]).astype(BF16))
        w_k.append(weight(3 + head))
        w_v.append(weight(6 + head))
    rows = q_image[0].shape[0]

    def score_step(c, tops):
        at = pl.ds(pl.multiple_of(c * chunk, chunk), chunk)
        lat = lat_ref[:, at]
        out = []
        for head in range(3):
            k_t = dot(w_k[head], lat)
            k_t = k_t * lax.rsqrt(jnp.mean(k_t * k_t, axis=0, keepdims=True) + 1e-06)
            v_ref[head, :, at] = dot(w_v[head], lat).astype(BF16)
            s = dot(q_image[head], k_t.astype(BF16))
            s_ref[head, :, at] = s
            top = tops[head]
            for j in range(chunk // HD):
                top = jnp.maximum(top, s[:, j * HD : (j + 1) * HD])
            out.append(top)
        return tuple(out)

    tops = lax.fori_loop(0, n_chunks, score_step, (jnp.full((rows, HD), -3e38, F32),) * 3)
    tops = [jnp.max(top, axis=1, keepdims=True) for top in tops]
    for head in range(3):
        out_ref[head] = jnp.zeros((rows, HD), F32)
        sum_ref[head] = jnp.zeros((rows, HD), F32)

    def mix_step(c, carry):
        at = pl.ds(pl.multiple_of(c * chunk, chunk), chunk)
        for head in range(3):
            p = jnp.exp2(s_ref[head, :, at] - tops[head])
            total = sum_ref[head]
            for j in range(chunk // HD):
                total = total + p[:, j * HD : (j + 1) * HD]
            sum_ref[head] = total
            out_ref[head] += dot(p.astype(BF16), v_ref[head, :, at], NT)
        return carry

    lax.fori_loop(0, n_chunks, mix_step, 0)
    lane = lax.broadcasted_iota(jnp.int32, (rows, HD), 1)
    numbers = jnp.zeros((rows, HD), F32)
    for head in range(3):
        numbers = jnp.where(lane == head, tops[head], numbers)
        numbers = jnp.where(lane == 3 + head, jnp.sum(sum_ref[head], axis=1, keepdims=True), numbers)
    out_ref[6] = numbers


def text_body(image_ref, text_ref, att_ref):
    def block(first):
        return text_ref[:, first : first + 16, :].reshape(text_ref.shape[0] * 16, HD)

    for head in range(3):
        s = dot(image_ref[3 + head].astype(BF16), block(head * 16), NT)
        image_top = image_ref[6][:, head : head + 1]
        top = jnp.maximum(image_top, jnp.max(s, axis=1, keepdims=True))
        keep = jnp.exp2(image_top - top)
        p = jnp.exp2(s - top)
        acc = image_ref[head] * keep + dot(p.astype(BF16), block(48 + head * 16))
        total = image_ref[6][:, 3 + head : 4 + head] * keep + jnp.sum(p, axis=1, keepdims=True)
        att_ref[:, head * HD : (head + 1) * HD] = (acc / total).astype(BF16)


def velocity_body(parts_ref, noised_ref, embed_ref, mod_ref, final_t_ref, v_ref):
    total = parts_ref[0].astype(F32)
    for i in range(1, parts_ref.shape[0]):
        total = total + parts_ref[i].astype(F32)
    own_rows = total.shape[0]
    own = noised_ref[pl.ds(pl.multiple_of(lax.axis_index("mp") * own_rows, own_rows), own_rows), :].astype(BF16)
    h = dot(own, embed_ref[...]) + mod_ref[2] * total
    width = h.shape[1]
    h = h - jnp.sum(h, axis=1, keepdims=True) / width
    var = jnp.sum(h * h, axis=1, keepdims=True) / width
    v = dot((h * lax.rsqrt(var + 1e-06)).astype(BF16), final_t_ref[...], NT)
    v = jnp.concatenate([v[0:8, :], v[8:16, :]], axis=1)
    for i in range(v_ref.shape[0]):
        v_ref[i] = v


def grad_body(level_ref, both_ref, gap_ref, hidden_ref, gen_t_ref, piece_ref, share_ref, raw_ref, diff_ref, grad_ref):
    n_mp = both_ref.shape[0] // 2
    chans = gap_ref.shape[1]

    def rows(first):
        blocks = []
        for i in range(first, first + n_mp):
            blocks += [both_ref[i][:, 0:chans], both_ref[i][:, chans : 2 * chans]]
        return jnp.concatenate(blocks, axis=0)

    teacher, student = rows(0), rows(n_mp)
    spread = jnp.abs(gap_ref[...] + noise_scale_of(level_ref[0], gap_ref.shape) * teacher)
    spread = jnp.sum(jnp.sum(spread, axis=1, keepdims=True), axis=0, keepdims=True)
    spread = jnp.broadcast_to(spread, (8, HD))
    diff = teacher - student
    diff_ref[...] = diff.T
    half = chans // 2
    share = diff_ref[pl.ds(pl.multiple_of(lax.axis_index("role") * half, half), half), :]
    share_ref[...] = share
    cols = grad_ref.shape[1]
    hidden = hidden_ref[:, pl.ds(pl.multiple_of(lax.axis_index("mp") * cols, HD), cols)]
    grad_ref[...] = dot(share.astype(BF16), hidden)
    terms = [grad_ref[:, g * HD : (g + 1) * HD] for g in range(3)]
    block = in_parts(jnp.concatenate([*terms, spread], axis=0))
    for i in range(piece_ref.shape[0]):
        piece_ref[i] = block
    feats = raw_ref.shape[1]
    raw_ref[...] = dot(diff.astype(BF16), gen_t_ref[:, pl.ds(pl.multiple_of(lax.axis_index("role") * feats, HD), feats)])


def in_parts(block):
    row = lax.broadcasted_iota(jnp.int32, block.shape, 0) - (block.shape[0] - 8)
    high = block.astype(BF16).astype(F32)
    mid = (block - high).astype(BF16).astype(F32)
    low = block - high - mid
    return jnp.where(row == 1, mid, jnp.where(row == 2, low, high)).astype(BF16)


def whole_total(ref):
    total = ref[0].astype(F32)
    for i in range(1, ref.shape[0]):
        total = total + ref[i].astype(F32)
    last = total.shape[0] - 8
    number = total[last : last + 1, :] + total[last + 1 : last + 2, :] + total[last + 2 : last + 3, :]
    return total[0:last, :], number


def near_body(recv_ref, out_ref):
    total, number = whole_total(recv_ref)
    out = in_parts(jnp.concatenate([total, jnp.broadcast_to(number, (8, HD))], axis=0))
    for i in range(out_ref.shape[0]):
        out_ref[i] = out


def last_body(level_ref, recv_ref, share_ref, raw_ref, x_ref, hidden_ref, gen_ref, *, entries):
    total, number = whole_total(recv_ref)
    factor = noise_scale_of(level_ref[0], (1, 1)) / (number[:, 0:1] / entries + 1e-06)
    x_ref[...] = share_ref[...] * factor
    hidden_ref[...] = (raw_ref[...] * factor).astype(BF16)
    half = gen_ref.shape[0]
    for g in range(3):
        gen_ref[:, g * HD : (g + 1) * HD] = total[g * half : (g + 1) * half, :] * factor


def exchange(array, axis):
    return lax.all_to_all(array, axis, 0, 0, tiled=True)


def on_device(
    gen_hidden, w_gen, noise_latent, level_index, w_embed, modulation, w_qkv, qk_gain, text_kv, w_out, w_final
):
    rows_here, width = gen_hidden.shape
    n_seq, n_far, n_mp = lax.axis_size(SEQ), lax.axis_size("z_far"), lax.axis_size("mp")
    chans = w_gen.shape[1]
    tokens = rows_here * n_seq
    sds = jax.ShapeDtypeStruct
    mods = jnp.transpose(modulation, (1, 0, 2))
    embed = w_embed[0]
    gen_t = w_gen.T
    payload, level_late = call(
        weight_body,
        (sds((8, PIECE, HD), BF16), sds((1,), jnp.int32)),
        (level_index, embed, mods, jnp.transpose(w_qkv[0], (1, 0, 2))),
        scratch=(pltpu.VMEM((8 * PIECE, HD), F32),),
        smem=1,
        limit=60,
    )
    noised, gap, send = call(
        latent_body,
        (
            sds((rows_here, chans), F32),
            sds((rows_here, chans), F32),
            sds((chans + 96, HD), BF16),
        ),
        (level_late, gen_hidden, gen_t, noise_latent.T, embed, text_kv[0]),
        smem=1,
        limit=60,
    )
    pieces = exchange(payload, NEAR)
    pieces = call(far_body, sds((n_far, PIECE + HALF + 96, HD), BF16), (pieces, send))
    pieces = exchange(pieces, "z_far")
    pieces, text = call(
        spread_body,
        (sds((8, PIECE + n_far * HALF, HD), BF16), sds((8, n_far * 96, HD), BF16)),
        (pieces,),
    )
    pieces = exchange(pieces, NEAR)
    text = exchange(text, NEAR).reshape(n_seq, 96, HD)
    other = lax.ppermute(pieces[:, PIECE:, :], "mp", [(i, i ^ 1) for i in range(n_mp)])

    image = call(
        image_body,
        sds((7, rows_here, HD), F32),
        (send, pieces, other, qk_gain[0]),
        scratch=(
            pltpu.VMEM((MROWS, tokens), BF16),
            pltpu.VMEM((3, rows_here, tokens), F32),
            pltpu.VMEM((3, HD, tokens), BF16),
            pltpu.VMEM((8 * PIECE, HD), F32),
            pltpu.VMEM((chans, HD), F32),
            pltpu.VMEM((3, rows_here, HD), F32),
        ),
    )
    own_rows = rows_here // n_mp
    attended = call(text_body, sds((rows_here, 3 * HD), BF16), (image, text))
    y = dot(attended, w_out[0]).astype(BF16).reshape(n_mp, own_rows, width)
    parts = exchange(y, "mp")
    velocity = call(
        velocity_body,
        sds((2 * n_mp, 8, 2 * chans), F32),
        (parts, noised, embed, mods, w_final[0].T),
    )
    both = exchange(velocity, ("role", "mp"))
    half = chans // 2
    grad_piece, share, raw = call(
        grad_body,
        (sds((8, 3 * half + 8, HD), BF16), sds((half, rows_here), F32), sds((rows_here, width // 2), F32)),
        (level_index, both, gap, gen_hidden, gen_t),
        scratch=(pltpu.VMEM((chans, rows_here), F32), pltpu.VMEM((half, 3 * HD), F32)),
        smem=1,
    )
    near = exchange(grad_piece, NEAR)
    near = call(near_body, sds((n_far, 3 * half + 8, HD), BF16), (near,))
    everything = exchange(near, "z_far")

    def last(*refs):
        last_body(*refs, entries=tokens * chans)

    grad_x_t, grad_hidden, grad_gen_t = call(
        last,
        (sds((half, rows_here), F32), sds((rows_here, width // 2), BF16), sds((half, 3 * HD), F32)),
        (level_index, everything, share, raw),
        smem=1,
    )
    return grad_x_t.T, grad_hidden, grad_gen_t.T


def solution(mesh):
    n_role, n_seq, n_mp = (mesh.shape[name] for name in ("role", "seq", "mp"))
    names = ("role", *SEQ, "mp")
    mesh = jax.sharding.Mesh(mesh.devices.reshape(n_role, n_seq // 8, 4, 2, n_mp), names)
    placed = (
        P(SEQ, None),
        P(),
        P(SEQ, None),
        P(),
        P("role", None, None),
        P("role", None, None),
        P("role", SEQ, None, "mp"),
        P("role", None, None),
        P("role", SEQ, None, "mp"),
        P("role", "mp", None),
        P("role", None, None),
    )
    return jax.shard_map(
        on_device,
        mesh=mesh,
        in_specs=placed,
        out_specs=(P(SEQ, "role"), P(SEQ, "role"), P("mp", "role")),
        check_vma=False,
    )
```

```python
import jax
import jax.numpy as jnp
from jax import lax
from jax.experimental import pallas as pl
from jax.experimental.pallas import tpu as pltpu
from jax.sharding import PartitionSpec as P

LEVELS = 1000
HD = 128
SEQ = ("z_far", "z_near", "y_hi")
NEAR = ("z_near", "y_hi")
CHANS = 64
HALF = CHANS // 2
MROWS = 80
PIECE = 80
F32 = jnp.float32
BF16 = jnp.bfloat16
NN = (((1,), (0,)), ((), ()))
NT = (((1,), (1,)), ((), ()))


def dot(a, b, dims=NN):
    return lax.dot_general(a, b, dims, preferred_element_type=F32)


def call(body, out_shape, args, scratch=(), smem=0, limit=24):
    vmem = pl.BlockSpec(memory_space=pltpu.VMEM)
    scalars = pl.BlockSpec(memory_space=pltpu.SMEM)
    return pl.pallas_call(
        body,
        out_shape=out_shape,
        in_specs=[scalars if i < smem else vmem for i in range(len(args))],
        out_specs=jax.tree.map(lambda out: scalars if out.dtype == jnp.int32 else vmem, out_shape),
        scratch_shapes=list(scratch),
        compiler_params=pltpu.CompilerParams(vmem_limit_bytes=limit * 1024 * 1024),
    )(*args)


def seq_here():
    return (lax.axis_index("z_far") * 4 + lax.axis_index("z_near")) * 2 + lax.axis_index("y_hi")


def noise_scale_of(level, shape):
    time_frac = (jnp.full(shape, level, jnp.int32).astype(F32) + 1.0) / (LEVELS + 1.0)
    return 3.0 * time_frac / (1.0 + 2.0 * time_frac)


def weight_body(embed_ref, mod_ref, qkv_ref, payload_ref, order_ref, term_ref):
    width = embed_ref.shape[1]
    features = qkv_ref.shape[1]
    offset = seq_here() * features
    start = pl.multiple_of(jnp.minimum((offset >> 7) << 7, width - 256), HD)
    mean = jnp.sum(embed_ref[...].astype(F32), axis=1, keepdims=True) / width
    window = embed_ref[:, pl.ds(start, 256)].astype(F32)
    scale = 1.0 + mod_ref[1, :, pl.ds(start, 256)]
    shift = mod_ref[0, :, pl.ds(start, 256)]
    rows = jnp.concatenate(
        [(window - mean) * scale, shift, jnp.zeros((MROWS - CHANS - 1, 256), F32)], axis=0
    )
    select = jnp.where(
        lax.broadcasted_iota(jnp.int32, (256, features), 0)
        == lax.broadcasted_iota(jnp.int32, (256, features), 1) + (offset - start),
        1.0,
        0.0,
    ).astype(BF16)
    high = rows.astype(BF16)
    low = dot((rows - high.astype(F32)).astype(BF16), select).astype(BF16)
    high = dot(high, select).astype(BF16)
    for part in range(3):
        term = dot(high, qkv_ref[part]) + dot(low, qkv_ref[part])
        for head in range(3):
            j = part * 3 + head
            block = term[:, head * HD : (head + 1) * HD]
            term_ref[j * CHANS : (j + 1) * CHANS, :] = block[0:CHANS, :]
            term_ref[9 * CHANS + j : 9 * CHANS + j + 1, :] = block[CHANS : CHANS + 1, :]
    term_ref[9 * CHANS + 9 :, :] = jnp.zeros((term_ref.shape[0] - 9 * CHANS - 9, HD), F32)
    for p in range(payload_ref.shape[0]):
        payload_ref[p] = term_ref[p * PIECE : (p + 1) * PIECE, :].astype(BF16)
    order_ref[0] = 0


def latent_body(
    level_ref, _, hidden_ref, gen_t_ref, noise_t_ref, embed_ref, text_in_ref, noised_ref, gap_ref, send_ref
):
    x_t = dot(gen_t_ref[...], hidden_ref[...], NT)
    noise_scale = noise_scale_of(level_ref[0], x_t.shape)
    noised_t = ((1.0 - noise_scale) * x_t + noise_scale * noise_t_ref[...].astype(F32)).astype(BF16)
    noised = noised_t.astype(F32).T
    noised_ref[...] = noised
    gap_ref[...] = (x_t - noised_t.astype(F32)).T
    width = embed_ref.shape[1]
    step = 512
    embed_mean = jnp.zeros((embed_ref.shape[0], HD), F32)
    for j in range(width // HD):
        embed_mean = embed_mean + embed_ref[:, j * HD : (j + 1) * HD].astype(F32)
    embed_mean = jnp.sum(embed_mean, axis=1, keepdims=True) / width
    row_mean = jnp.sum(noised_t.astype(F32) * embed_mean, axis=0, keepdims=True)
    row_mean = jnp.broadcast_to(row_mean, (HD, noised.shape[0])).T
    row_var = jnp.zeros(row_mean.shape, F32)
    noised_b = noised.astype(BF16)
    for j in range(width // step):
        h = dot(noised_b, embed_ref[:, j * step : (j + 1) * step])
        for k in range(step // HD):
            row_var = row_var + jnp.square(h[:, k * HD : (k + 1) * HD] - row_mean)
    row_var = jnp.sum(row_var, axis=1, keepdims=True) / width
    send_ref[0:CHANS, :] = (noised * lax.rsqrt(row_var + 1e-06)).T.astype(BF16)
    text = text_in_ref[...].astype(F32)
    for j in range(6):
        block = text[:, j // 3, (j % 3) * HD : (j % 3 + 1) * HD]
        send_ref[CHANS + j * 16 : CHANS + (j + 1) * 16, :] = block.astype(BF16)


def total_of(ref, rows):
    total = ref[0, 0:rows, :].astype(F32)
    for i in range(1, ref.shape[0]):
        total = total + ref[i, 0:rows, :].astype(F32)
    return total.astype(BF16)


def far_body(recv_ref, send_ref, out_ref):
    piece = total_of(recv_ref, PIECE)
    channels = send_ref[pl.ds(pl.multiple_of((lax.axis_index("mp") & 1) * HALF, HALF), HALF), :]
    for i in range(out_ref.shape[0]):
        out_ref[i, 0:PIECE, :] = piece
        out_ref[i, PIECE : PIECE + HALF, :] = channels
        out_ref[i, PIECE + HALF :, :] = send_ref[CHANS:, :]


def spread_body(recv_ref, out_ref, text_ref):
    piece = total_of(recv_ref, PIECE)
    text = PIECE + HALF
    for i in range(out_ref.shape[0]):
        out_ref[i, 0:PIECE, :] = piece
        for g in range(recv_ref.shape[0]):
            out_ref[i, PIECE + g * HALF : PIECE + (g + 1) * HALF, :] = recv_ref[g, PIECE:text, :]
            text_ref[i, g * 96 : (g + 1) * 96, :] = recv_ref[g, text:, :]


def image_body(
    send_ref, recv_ref, other_ref, gain_ref, out_ref, lat_ref, s_ref, v_ref, m_ref, own_ref, sum_ref
):
    tokens = lat_ref.shape[1]
    chunk = 1024
    n_chunks = tokens // chunk
    ones = jnp.where(lax.broadcasted_iota(jnp.int32, (MROWS - CHANS, HD), 0) == 0, 1.0, 0.0).astype(BF16)
    n_far = (recv_ref.shape[1] - PIECE) // HALF
    for i in range(tokens // HD):
        near, first = i // n_far, (i % n_far) * HALF
        at = slice(i * HD, (i + 1) * HD)
        lat_ref[0:HALF, at] = recv_ref[near, PIECE + first : PIECE + first + HALF, :]
        lat_ref[HALF:CHANS, at] = other_ref[near, first : first + HALF, :]
        lat_ref[CHANS:MROWS, at] = ones
    for i in range(recv_ref.shape[0]):
        m_ref[i * PIECE : (i + 1) * PIECE, :] = recv_ref[i, 0:PIECE, :].astype(F32)
    own_ref[...] = send_ref[0:CHANS, :].astype(F32)

    def reordered(ref, base):
        core = lax.axis_index("mp") & 1
        return jnp.concatenate(
            [ref[pl.ds(pl.multiple_of(k * HALF + base, HALF), HALF), :] for k in (core, 1 - core)], axis=0
        )

    own = jnp.concatenate([reordered(own_ref, 0).astype(BF16), ones], axis=0)
    score_scale = HD ** (-0.5) * 1.4426950408889634
    biases = m_ref[9 * CHANS : 9 * CHANS + 16, :]

    def weight(j):
        block = reordered(m_ref, j * CHANS)
        pad = jnp.zeros((HD - CHANS - 1, HD), F32)
        return jnp.concatenate([block, biases[j : j + 1, :], pad], axis=0).T[:, 0:MROWS].astype(BF16)

    q_image, w_k, w_v = [], [], []
    for head in range(3):
        q_t = dot(weight(head), own)
        q_t = q_t * lax.rsqrt(jnp.mean(q_t * q_t, axis=0, keepdims=True) + 1e-06)
        q = q_t.T * (gain_ref[0:1, :] * score_scale)
        out_ref[3 + head] = q
        q_image.append((q * gain_ref[1:2, :]).astype(BF16))
        w_k.append(weight(3 + head))
        w_v.append(weight(6 + head))
    rows = q_image[0].shape[0]

    def score_step(c, tops):
        at = pl.ds(pl.multiple_of(c * chunk, chunk), chunk)
        lat = lat_ref[:, at]
        out = []
        for head in range(3):
            k_t = dot(w_k[head], lat)
            k_t = k_t * lax.rsqrt(jnp.mean(k_t * k_t, axis=0, keepdims=True) + 1e-06)
            v_ref[head, :, at] = dot(w_v[head], lat).astype(BF16)
            s = dot(q_image[head], k_t.astype(BF16))
            s_ref[head, :, at] = s
            top = tops[head]
            for j in range(chunk // HD):
                top = jnp.maximum(top, s[:, j * HD : (j + 1) * HD])
            out.append(top)
        return tuple(out)

    tops = lax.fori_loop(0, n_chunks, score_step, (jnp.full((rows, HD), -3e38, F32),) * 3)
    tops = [jnp.max(top, axis=1, keepdims=True) for top in tops]
    for head in range(3):
        out_ref[head] = jnp.zeros((rows, HD), F32)
        sum_ref[head] = jnp.zeros((rows, HD), F32)

    def mix_step(c, carry):
        at = pl.ds(pl.multiple_of(c * chunk, chunk), chunk)
        for head in range(3):
            p = jnp.exp2(s_ref[head, :, at] - tops[head])
            total = sum_ref[head]
            for j in range(chunk // HD):
                total = total + p[:, j * HD : (j + 1) * HD]
            sum_ref[head] = total
            out_ref[head] += dot(p.astype(BF16), v_ref[head, :, at], NT)
        return carry

    lax.fori_loop(0, n_chunks, mix_step, 0)
    lane = lax.broadcasted_iota(jnp.int32, (rows, HD), 1)
    numbers = jnp.zeros((rows, HD), F32)
    for head in range(3):
        numbers = jnp.where(lane == head, tops[head], numbers)
        numbers = jnp.where(lane == 3 + head, jnp.sum(sum_ref[head], axis=1, keepdims=True), numbers)
    out_ref[6] = numbers


def text_body(image_ref, text_ref, att_ref):
    def block(first):
        return text_ref[:, first : first + 16, :].reshape(text_ref.shape[0] * 16, HD)

    for head in range(3):
        s = dot(image_ref[3 + head].astype(BF16), block(head * 16), NT)
        image_top = image_ref[6][:, head : head + 1]
        top = jnp.maximum(image_top, jnp.max(s, axis=1, keepdims=True))
        keep = jnp.exp2(image_top - top)
        p = jnp.exp2(s - top)
        acc = image_ref[head] * keep + dot(p.astype(BF16), block(48 + head * 16))
        total = image_ref[6][:, 3 + head : 4 + head] * keep + jnp.sum(p, axis=1, keepdims=True)
        att_ref[:, head * HD : (head + 1) * HD] = (acc / total).astype(BF16)


def velocity_body(parts_ref, noised_ref, embed_ref, mod_ref, final_t_ref, v_ref):
    total = parts_ref[0].astype(F32)
    for i in range(1, parts_ref.shape[0]):
        total = total + parts_ref[i].astype(F32)
    own_rows = total.shape[0]
    own = noised_ref[pl.ds(pl.multiple_of(lax.axis_index("mp") * own_rows, own_rows), own_rows), :].astype(BF16)
    h = dot(own, embed_ref[...]) + mod_ref[2] * total
    width = h.shape[1]
    h = h - jnp.sum(h, axis=1, keepdims=True) / width
    var = jnp.sum(h * h, axis=1, keepdims=True) / width
    v = dot((h * lax.rsqrt(var + 1e-06)).astype(BF16), final_t_ref[...], NT)
    v = jnp.concatenate([v[0:8, :], v[8:16, :]], axis=1)
    for i in range(v_ref.shape[0]):
        v_ref[i] = v


def grad_body(level_ref, both_ref, gap_ref, hidden_ref, gen_t_ref, piece_ref, share_ref, raw_ref, diff_ref, grad_ref):
    n_mp = both_ref.shape[0] // 2
    chans = gap_ref.shape[1]

    def rows(first):
        blocks = []
        for i in range(first, first + n_mp):
            blocks += [both_ref[i][:, 0:chans], both_ref[i][:, chans : 2 * chans]]
        return jnp.concatenate(blocks, axis=0)

    teacher, student = rows(0), rows(n_mp)
    spread = jnp.abs(gap_ref[...] + noise_scale_of(level_ref[0], gap_ref.shape) * teacher)
    spread = jnp.sum(jnp.sum(spread, axis=1, keepdims=True), axis=0, keepdims=True)
    spread = jnp.broadcast_to(spread, (8, HD))
    diff = teacher - student
    diff_ref[...] = diff.T
    half = chans // 2
    share = diff_ref[pl.ds(pl.multiple_of(lax.axis_index("role") * half, half), half), :]
    share_ref[...] = share
    cols = grad_ref.shape[1]
    hidden = hidden_ref[:, pl.ds(pl.multiple_of(lax.axis_index("mp") * cols, HD), cols)]
    grad_ref[...] = dot(share.astype(BF16), hidden)
    terms = [grad_ref[:, g * HD : (g + 1) * HD] for g in range(3)]
    block = in_parts(jnp.concatenate([*terms, spread], axis=0))
    for i in range(piece_ref.shape[0]):
        piece_ref[i] = block
    feats = raw_ref.shape[1]
    raw_ref[...] = dot(diff.astype(BF16), gen_t_ref[:, pl.ds(pl.multiple_of(lax.axis_index("role") * feats, HD), feats)])


def in_parts(block):
    row = lax.broadcasted_iota(jnp.int32, block.shape, 0) - (block.shape[0] - 8)
    high = block.astype(BF16).astype(F32)
    mid = (block - high).astype(BF16).astype(F32)
    low = block - high - mid
    return jnp.where(row == 1, mid, jnp.where(row == 2, low, high)).astype(BF16)


def whole_total(ref):
    total = ref[0].astype(F32)
    for i in range(1, ref.shape[0]):
        total = total + ref[i].astype(F32)
    last = total.shape[0] - 8
    number = total[last : last + 1, :] + total[last + 1 : last + 2, :] + total[last + 2 : last + 3, :]
    return total[0:last, :], number


def near_body(recv_ref, out_ref):
    total, number = whole_total(recv_ref)
    out = in_parts(jnp.concatenate([total, jnp.broadcast_to(number, (8, HD))], axis=0))
    for i in range(out_ref.shape[0]):
        out_ref[i] = out


def last_body(level_ref, recv_ref, share_ref, raw_ref, x_ref, hidden_ref, gen_ref, *, entries):
    total, number = whole_total(recv_ref)
    factor = noise_scale_of(level_ref[0], (1, 1)) / (number[:, 0:1] / entries + 1e-06)
    x_ref[...] = share_ref[...] * factor
    hidden_ref[...] = (raw_ref[...] * factor).astype(BF16)
    half = gen_ref.shape[0]
    for g in range(3):
        gen_ref[:, g * HD : (g + 1) * HD] = total[g * half : (g + 1) * half, :] * factor


def exchange(array, axis):
    return lax.all_to_all(array, axis, 0, 0, tiled=True)


def on_device(
    gen_hidden, w_gen, noise_latent, level_index, w_embed, modulation, w_qkv, qk_gain, text_kv, w_out, w_final
):
    rows_here, width = gen_hidden.shape
    n_seq, n_far, n_mp = lax.axis_size(SEQ), lax.axis_size("z_far"), lax.axis_size("mp")
    chans = w_gen.shape[1]
    tokens = rows_here * n_seq
    sds = jax.ShapeDtypeStruct
    mods = jnp.transpose(modulation, (1, 0, 2))
    embed = w_embed[0]
    gen_t = w_gen.T
    payload, order = call(
        weight_body,
        (sds((8, PIECE, HD), BF16), sds((1,), jnp.int32)),
        (embed, mods, jnp.transpose(w_qkv[0], (1, 0, 2))),
        scratch=(pltpu.VMEM((8 * PIECE, HD), F32),),
        limit=60,
    )
    noised, gap, send = call(
        latent_body,
        (
            sds((rows_here, chans), F32),
            sds((rows_here, chans), F32),
            sds((chans + 96, HD), BF16),
        ),
        (level_index, order, gen_hidden, gen_t, noise_latent.T, embed, text_kv[0]),
        smem=2,
        limit=60,
    )
    pieces = exchange(payload, NEAR)
    pieces = call(far_body, sds((n_far, PIECE + HALF + 96, HD), BF16), (pieces, send))
    pieces = exchange(pieces, "z_far")
    pieces, text = call(
        spread_body,
        (sds((8, PIECE + n_far * HALF, HD), BF16), sds((8, n_far * 96, HD), BF16)),
        (pieces,),
    )
    pieces = exchange(pieces, NEAR)
    text = exchange(text, NEAR).reshape(n_seq, 96, HD)
    other = lax.ppermute(pieces[:, PIECE:, :], "mp", [(i, i ^ 1) for i in range(n_mp)])

    image = call(
        image_body,
        sds((7, rows_here, HD), F32),
        (send, pieces, other, qk_gain[0]),
        scratch=(
            pltpu.VMEM((MROWS, tokens), BF16),
            pltpu.VMEM((3, rows_here, tokens), F32),
            pltpu.VMEM((3, HD, tokens), BF16),
            pltpu.VMEM((8 * PIECE, HD), F32),
            pltpu.VMEM((chans, HD), F32),
            pltpu.VMEM((3, rows_here, HD), F32),
        ),
    )
    own_rows = rows_here // n_mp
    attended = call(text_body, sds((rows_here, 3 * HD), BF16), (image, text))
    y = dot(attended, w_out[0]).astype(BF16).reshape(n_mp, own_rows, width)
    parts = exchange(y, "mp")
    velocity = call(
        velocity_body,
        sds((2 * n_mp, 8, 2 * chans), F32),
        (parts, noised, embed, mods, w_final[0].T),
    )
    both = exchange(velocity, ("role", "mp"))
    half = chans // 2
    grad_piece, share, raw = call(
        grad_body,
        (sds((8, 3 * half + 8, HD), BF16), sds((half, rows_here), F32), sds((rows_here, width // 2), F32)),
        (level_index, both, gap, gen_hidden, gen_t),
        scratch=(pltpu.VMEM((chans, rows_here), F32), pltpu.VMEM((half, 3 * HD), F32)),
        smem=1,
    )
    near = exchange(grad_piece, NEAR)
    near = call(near_body, sds((n_far, 3 * half + 8, HD), BF16), (near,))
    everything = exchange(near, "z_far")

    def last(*refs):
        last_body(*refs, entries=tokens * chans)

    grad_x_t, grad_hidden, grad_gen_t = call(
        last,
        (sds((half, rows_here), F32), sds((rows_here, width // 2), BF16), sds((half, 3 * HD), F32)),
        (level_index, everything, share, raw),
        smem=1,
    )
    return grad_x_t.T, grad_hidden, grad_gen_t.T


def solution(mesh):
    n_role, n_seq, n_mp = (mesh.shape[name] for name in ("role", "seq", "mp"))
    names = ("role", *SEQ, "mp")
    mesh = jax.sharding.Mesh(mesh.devices.reshape(n_role, n_seq // 8, 4, 2, n_mp), names)
    placed = (
        P(SEQ, None),
        P(),
        P(SEQ, None),
        P(),
        P("role", None, None),
        P("role", None, None),
        P("role", SEQ, None, "mp"),
        P("role", None, None),
        P("role", SEQ, None, "mp"),
        P("role", "mp", None),
        P("role", None, None),
    )
    return jax.shard_map(
        on_device,
        mesh=mesh,
        in_specs=placed,
        out_specs=(P(SEQ, "role"), P(SEQ, "role"), P("mp", "role")),
        check_vma=False,
    )
```

```python
import jax
import jax.numpy as jnp
from jax import lax
from jax.experimental import pallas as pl
from jax.experimental.pallas import tpu as pltpu
from jax.sharding import PartitionSpec as P

LEVELS = 1000
HD = 128
SEQ = ("z_far", "z_near", "y_hi")
NEAR = ("z_near", "y_hi")
CHANS = 64
PART = CHANS // 4
MROWS = 80
PIECE = 80
F32 = jnp.float32
BF16 = jnp.bfloat16
NN = (((1,), (0,)), ((), ()))
NT = (((1,), (1,)), ((), ()))


def dot(a, b, dims=NN):
    return lax.dot_general(a, b, dims, preferred_element_type=F32)


def call(body, out_shape, args, scratch=(), smem=0, limit=24):
    vmem = pl.BlockSpec(memory_space=pltpu.VMEM)
    scalars = pl.BlockSpec(memory_space=pltpu.SMEM)
    return pl.pallas_call(
        body,
        out_shape=out_shape,
        in_specs=[scalars if i < smem else vmem for i in range(len(args))],
        out_specs=jax.tree.map(lambda out: scalars if out.dtype == jnp.int32 else vmem, out_shape),
        scratch_shapes=list(scratch),
        compiler_params=pltpu.CompilerParams(vmem_limit_bytes=limit * 1024 * 1024),
    )(*args)


def seq_here():
    return (lax.axis_index("z_far") * 4 + lax.axis_index("z_near")) * 2 + lax.axis_index("y_hi")


def noise_scale_of(level, shape):
    time_frac = (jnp.full(shape, level, jnp.int32).astype(F32) + 1.0) / (LEVELS + 1.0)
    return 3.0 * time_frac / (1.0 + 2.0 * time_frac)


def weight_body(embed_ref, mod_ref, qkv_ref, payload_ref, order_ref, term_ref):
    width = embed_ref.shape[1]
    features = qkv_ref.shape[1]
    offset = seq_here() * features
    start = pl.multiple_of(jnp.minimum((offset >> 7) << 7, width - 256), HD)
    mean = jnp.sum(embed_ref[...].astype(F32), axis=1, keepdims=True) / width
    window = embed_ref[:, pl.ds(start, 256)].astype(F32)
    scale = 1.0 + mod_ref[1, :, pl.ds(start, 256)]
    shift = mod_ref[0, :, pl.ds(start, 256)]
    rows = jnp.concatenate(
        [(window - mean) * scale, shift, jnp.zeros((MROWS - CHANS - 1, 256), F32)], axis=0
    )
    select = jnp.where(
        lax.broadcasted_iota(jnp.int32, (256, features), 0)
        == lax.broadcasted_iota(jnp.int32, (256, features), 1) + (offset - start),
        1.0,
        0.0,
    ).astype(BF16)
    high = rows.astype(BF16)
    low = dot((rows - high.astype(F32)).astype(BF16), select).astype(BF16)
    high = dot(high, select).astype(BF16)
    for part in range(3):
        term = dot(high, qkv_ref[part]) + dot(low, qkv_ref[part])
        for head in range(3):
            j = part * 3 + head
            block = term[:, head * HD : (head + 1) * HD]
            term_ref[j * CHANS : (j + 1) * CHANS, :] = block[0:CHANS, :]
            term_ref[9 * CHANS + j : 9 * CHANS + j + 1, :] = block[CHANS : CHANS + 1, :]
    term_ref[9 * CHANS + 9 :, :] = jnp.zeros((term_ref.shape[0] - 9 * CHANS - 9, HD), F32)
    for p in range(payload_ref.shape[0]):
        payload_ref[p] = term_ref[p * PIECE : (p + 1) * PIECE, :].astype(BF16)
    order_ref[0] = 0


def latent_body(
    level_ref, _, hidden_ref, gen_t_ref, noise_t_ref, embed_ref, text_in_ref, noised_ref, gap_ref, send_ref
):
    x_t = dot(gen_t_ref[...], hidden_ref[...], NT)
    noise_scale = noise_scale_of(level_ref[0], x_t.shape)
    noised_t = ((1.0 - noise_scale) * x_t + noise_scale * noise_t_ref[...].astype(F32)).astype(BF16)
    noised = noised_t.astype(F32).T
    noised_ref[...] = noised
    gap_ref[...] = (x_t - noised_t.astype(F32)).T
    width = embed_ref.shape[1]
    step = 512
    embed_mean = jnp.zeros((embed_ref.shape[0], HD), F32)
    for j in range(width // HD):
        embed_mean = embed_mean + embed_ref[:, j * HD : (j + 1) * HD].astype(F32)
    embed_mean = jnp.sum(embed_mean, axis=1, keepdims=True) / width
    row_mean = jnp.sum(noised_t.astype(F32) * embed_mean, axis=0, keepdims=True)
    row_mean = jnp.broadcast_to(row_mean, (HD, noised.shape[0])).T
    row_var = jnp.zeros(row_mean.shape, F32)
    noised_b = noised.astype(BF16)
    for j in range(width // step):
        h = dot(noised_b, embed_ref[:, j * step : (j + 1) * step])
        for k in range(step // HD):
            row_var = row_var + jnp.square(h[:, k * HD : (k + 1) * HD] - row_mean)
    row_var = jnp.sum(row_var, axis=1, keepdims=True) / width
    send_ref[0:CHANS, :] = (noised * lax.rsqrt(row_var + 1e-06)).T.astype(BF16)
    text = text_in_ref[...].astype(F32)
    for j in range(6):
        block = text[:, j // 3, (j % 3) * HD : (j % 3 + 1) * HD]
        send_ref[CHANS + j * 16 : CHANS + (j + 1) * 16, :] = block.astype(BF16)


def total_of(ref, rows):
    total = ref[0, 0:rows, :].astype(F32)
    for i in range(1, ref.shape[0]):
        total = total + ref[i, 0:rows, :].astype(F32)
    return total.astype(BF16)


def far_body(recv_ref, send_ref, out_ref):
    piece = total_of(recv_ref, PIECE)
    channels = send_ref[pl.ds(pl.multiple_of((lax.axis_index("mp") & 3) * PART, PART), PART), :]
    for i in range(out_ref.shape[0]):
        out_ref[i, 0:PIECE, :] = piece
        out_ref[i, PIECE : PIECE + PART, :] = channels
        out_ref[i, PIECE + PART :, :] = send_ref[CHANS:, :]


def spread_body(recv_ref, out_ref, text_ref):
    piece = total_of(recv_ref, PIECE)
    text = PIECE + PART
    for i in range(out_ref.shape[0]):
        out_ref[i, 0:PIECE, :] = piece
        for g in range(recv_ref.shape[0]):
            out_ref[i, PIECE + g * PART : PIECE + (g + 1) * PART, :] = recv_ref[g, PIECE:text, :]
            text_ref[i, g * 96 : (g + 1) * 96, :] = recv_ref[g, text:, :]


def image_body(
    send_ref, recv_ref, other1_ref, other2_ref, other3_ref, gain_ref, out_ref, lat_ref, s_ref, v_ref, m_ref, own_ref, sum_ref
):
    tokens = lat_ref.shape[1]
    chunk = 1024
    n_chunks = tokens // chunk
    ones = jnp.where(lax.broadcasted_iota(jnp.int32, (MROWS - CHANS, HD), 0) == 0, 1.0, 0.0).astype(BF16)
    other_refs = (other1_ref, other2_ref, other3_ref)
    n_far = (recv_ref.shape[1] - PIECE) // PART
    for i in range(tokens // HD):
        near, first = i // n_far, (i % n_far) * PART
        at = slice(i * HD, (i + 1) * HD)
        lat_ref[0:PART, at] = recv_ref[near, PIECE + first : PIECE + first + PART, :]
        for k, ref in enumerate(other_refs):
            lat_ref[(k + 1) * PART : (k + 2) * PART, at] = ref[near, first : first + PART, :]
        lat_ref[CHANS:MROWS, at] = ones
    for i in range(recv_ref.shape[0]):
        m_ref[i * PIECE : (i + 1) * PIECE, :] = recv_ref[i, 0:PIECE, :].astype(F32)
    own_ref[...] = send_ref[0:CHANS, :].astype(F32)

    def reordered(ref, base):
        here = lax.axis_index("mp") & 3
        starts = [pl.multiple_of((here ^ k) * PART + base, PART) for k in range(4)]
        return jnp.concatenate([ref[pl.ds(start, PART), :] for start in starts], axis=0)

    own = jnp.concatenate([reordered(own_ref, 0).astype(BF16), ones], axis=0)
    score_scale = HD ** (-0.5) * 1.4426950408889634
    biases = m_ref[9 * CHANS : 9 * CHANS + 16, :]

    def weight(j):
        block = reordered(m_ref, j * CHANS)
        pad = jnp.zeros((HD - CHANS - 1, HD), F32)
        return jnp.concatenate([block, biases[j : j + 1, :], pad], axis=0).T[:, 0:MROWS].astype(BF16)

    q_image, w_k, w_v = [], [], []
    for head in range(3):
        q_t = dot(weight(head), own)
        q_t = q_t * lax.rsqrt(jnp.mean(q_t * q_t, axis=0, keepdims=True) + 1e-06)
        q = q_t.T * (gain_ref[0:1, :] * score_scale)
        out_ref[3 + head] = q
        q_image.append((q * gain_ref[1:2, :]).astype(BF16))
        w_k.append(weight(3 + head))
        w_v.append(weight(6 + head))
    rows = q_image[0].shape[0]

    def score_step(c, tops):
        at = pl.ds(pl.multiple_of(c * chunk, chunk), chunk)
        lat = lat_ref[:, at]
        out = []
        for head in range(3):
            k_t = dot(w_k[head], lat)
            k_t = k_t * lax.rsqrt(jnp.mean(k_t * k_t, axis=0, keepdims=True) + 1e-06)
            v_ref[head, :, at] = dot(w_v[head], lat).astype(BF16)
            s = dot(q_image[head], k_t.astype(BF16))
            s_ref[head, :, at] = s
            top = tops[head]
            for j in range(chunk // HD):
                top = jnp.maximum(top, s[:, j * HD : (j + 1) * HD])
            out.append(top)
        return tuple(out)

    tops = lax.fori_loop(0, n_chunks, score_step, (jnp.full((rows, HD), -3e38, F32),) * 3)
    tops = [jnp.max(top, axis=1, keepdims=True) for top in tops]
    for head in range(3):
        out_ref[head] = jnp.zeros((rows, HD), F32)
        sum_ref[head] = jnp.zeros((rows, HD), F32)

    def mix_step(c, carry):
        at = pl.ds(pl.multiple_of(c * chunk, chunk), chunk)
        for head in range(3):
            p = jnp.exp2(s_ref[head, :, at] - tops[head])
            total = sum_ref[head]
            for j in range(chunk // HD):
                total = total + p[:, j * HD : (j + 1) * HD]
            sum_ref[head] = total
            out_ref[head] += dot(p.astype(BF16), v_ref[head, :, at], NT)
        return carry

    lax.fori_loop(0, n_chunks, mix_step, 0)
    lane = lax.broadcasted_iota(jnp.int32, (rows, HD), 1)
    numbers = jnp.zeros((rows, HD), F32)
    for head in range(3):
        numbers = jnp.where(lane == head, tops[head], numbers)
        numbers = jnp.where(lane == 3 + head, jnp.sum(sum_ref[head], axis=1, keepdims=True), numbers)
    out_ref[6] = numbers


def text_body(image_ref, text_ref, att_ref):
    def block(first):
        return text_ref[:, first : first + 16, :].reshape(text_ref.shape[0] * 16, HD)

    for head in range(3):
        s = dot(image_ref[3 + head].astype(BF16), block(head * 16), NT)
        image_top = image_ref[6][:, head : head + 1]
        top = jnp.maximum(image_top, jnp.max(s, axis=1, keepdims=True))
        keep = jnp.exp2(image_top - top)
        p = jnp.exp2(s - top)
        acc = image_ref[head] * keep + dot(p.astype(BF16), block(48 + head * 16))
        total = image_ref[6][:, 3 + head : 4 + head] * keep + jnp.sum(p, axis=1, keepdims=True)
        att_ref[:, head * HD : (head + 1) * HD] = (acc / total).astype(BF16)


def velocity_body(parts_ref, noised_ref, embed_ref, mod_ref, final_t_ref, v_ref):
    total = parts_ref[0].astype(F32)
    for i in range(1, parts_ref.shape[0]):
        total = total + parts_ref[i].astype(F32)
    own_rows = total.shape[0]
    own = noised_ref[pl.ds(pl.multiple_of(lax.axis_index("mp") * own_rows, own_rows), own_rows), :].astype(BF16)
    h = dot(own, embed_ref[...]) + mod_ref[2] * total
    width = h.shape[1]
    h = h - jnp.sum(h, axis=1, keepdims=True) / width
    var = jnp.sum(h * h, axis=1, keepdims=True) / width
    v = dot((h * lax.rsqrt(var + 1e-06)).astype(BF16), final_t_ref[...], NT)
    v = jnp.concatenate([v[0:8, :], v[8:16, :]], axis=1)
    for i in range(v_ref.shape[0]):
        v_ref[i] = v


def grad_body(level_ref, both_ref, gap_ref, hidden_ref, gen_t_ref, piece_ref, share_ref, raw_ref, diff_ref, grad_ref):
    n_mp = both_ref.shape[0] // 2
    chans = gap_ref.shape[1]

    def rows(first):
        blocks = []
        for i in range(first, first + n_mp):
            blocks += [both_ref[i][:, 0:chans], both_ref[i][:, chans : 2 * chans]]
        return jnp.concatenate(blocks, axis=0)

    teacher, student = rows(0), rows(n_mp)
    spread = jnp.abs(gap_ref[...] + noise_scale_of(level_ref[0], gap_ref.shape) * teacher)
    spread = jnp.sum(jnp.sum(spread, axis=1, keepdims=True), axis=0, keepdims=True)
    spread = jnp.broadcast_to(spread, (8, HD))
    diff = teacher - student
    diff_ref[...] = diff.T
    half = chans // 2
    share = diff_ref[pl.ds(pl.multiple_of(lax.axis_index("role") * half, half), half), :]
    share_ref[...] = share
    cols = grad_ref.shape[1]
    hidden = hidden_ref[:, pl.ds(pl.multiple_of(lax.axis_index("mp") * cols, HD), cols)]
    grad_ref[...] = dot(share.astype(BF16), hidden)
    terms = [grad_ref[:, g * HD : (g + 1) * HD] for g in range(3)]
    block = in_parts(jnp.concatenate([*terms, spread], axis=0))
    for i in range(piece_ref.shape[0]):
        piece_ref[i] = block
    feats = raw_ref.shape[1]
    raw_ref[...] = dot(diff.astype(BF16), gen_t_ref[:, pl.ds(pl.multiple_of(lax.axis_index("role") * feats, HD), feats)])


def in_parts(block):
    row = lax.broadcasted_iota(jnp.int32, block.shape, 0) - (block.shape[0] - 8)
    high = block.astype(BF16).astype(F32)
    mid = (block - high).astype(BF16).astype(F32)
    low = block - high - mid
    return jnp.where(row == 1, mid, jnp.where(row == 2, low, high)).astype(BF16)


def whole_total(ref):
    total = ref[0].astype(F32)
    for i in range(1, ref.shape[0]):
        total = total + ref[i].astype(F32)
    last = total.shape[0] - 8
    number = total[last : last + 1, :] + total[last + 1 : last + 2, :] + total[last + 2 : last + 3, :]
    return total[0:last, :], number


def near_body(recv_ref, out_ref):
    total, number = whole_total(recv_ref)
    out = in_parts(jnp.concatenate([total, jnp.broadcast_to(number, (8, HD))], axis=0))
    for i in range(out_ref.shape[0]):
        out_ref[i] = out


def last_body(level_ref, recv_ref, share_ref, raw_ref, x_ref, hidden_ref, gen_ref, *, entries):
    total, number = whole_total(recv_ref)
    factor = noise_scale_of(level_ref[0], (1, 1)) / (number[:, 0:1] / entries + 1e-06)
    x_ref[...] = share_ref[...] * factor
    hidden_ref[...] = (raw_ref[...] * factor).astype(BF16)
    half = gen_ref.shape[0]
    for g in range(3):
        gen_ref[:, g * HD : (g + 1) * HD] = total[g * half : (g + 1) * half, :] * factor


def exchange(array, axis):
    return lax.all_to_all(array, axis, 0, 0, tiled=True)


def on_device(
    gen_hidden, w_gen, noise_latent, level_index, w_embed, modulation, w_qkv, qk_gain, text_kv, w_out, w_final
):
    rows_here, width = gen_hidden.shape
    n_seq, n_far, n_mp = lax.axis_size(SEQ), lax.axis_size("z_far"), lax.axis_size("mp")
    chans = w_gen.shape[1]
    tokens = rows_here * n_seq
    sds = jax.ShapeDtypeStruct
    mods = jnp.transpose(modulation, (1, 0, 2))
    embed = w_embed[0]
    gen_t = w_gen.T
    payload, order = call(
        weight_body,
        (sds((8, PIECE, HD), BF16), sds((1,), jnp.int32)),
        (embed, mods, jnp.transpose(w_qkv[0], (1, 0, 2))),
        scratch=(pltpu.VMEM((8 * PIECE, HD), F32),),
        limit=60,
    )
    noised, gap, send = call(
        latent_body,
        (
            sds((rows_here, chans), F32),
            sds((rows_here, chans), F32),
            sds((chans + 96, HD), BF16),
        ),
        (level_index, order, gen_hidden, gen_t, noise_latent.T, embed, text_kv[0]),
        smem=2,
        limit=60,
    )
    pieces = exchange(payload, NEAR)
    pieces = call(far_body, sds((n_far, PIECE + PART + 96, HD), BF16), (pieces, send))
    pieces = exchange(pieces, "z_far")
    pieces, text = call(
        spread_body,
        (sds((8, PIECE + n_far * PART, HD), BF16), sds((8, n_far * 96, HD), BF16)),
        (pieces,),
    )
    pieces = exchange(pieces, NEAR)
    text = exchange(text, NEAR).reshape(n_seq, 96, HD)
    channels = pieces[:, PIECE:, :]
    others = [lax.ppermute(channels, "mp", [(i, i ^ k) for i in range(n_mp)]) for k in (1, 2, 3)]

    image = call(
        image_body,
        sds((7, rows_here, HD), F32),
        (send, pieces, *others, qk_gain[0]),
        scratch=(
            pltpu.VMEM((MROWS, tokens), BF16),
            pltpu.VMEM((3, rows_here, tokens), F32),
            pltpu.VMEM((3, HD, tokens), BF16),
            pltpu.VMEM((8 * PIECE, HD), F32),
            pltpu.VMEM((chans, HD), F32),
            pltpu.VMEM((3, rows_here, HD), F32),
        ),
    )
    own_rows = rows_here // n_mp
    attended = call(text_body, sds((rows_here, 3 * HD), BF16), (image, text))
    y = dot(attended, w_out[0]).astype(BF16).reshape(n_mp, own_rows, width)
    parts = exchange(y, "mp")
    velocity = call(
        velocity_body,
        sds((2 * n_mp, 8, 2 * chans), F32),
        (parts, noised, embed, mods, w_final[0].T),
    )
    both = exchange(velocity, ("role", "mp"))
    half = chans // 2
    grad_piece, share, raw = call(
        grad_body,
        (sds((8, 3 * half + 8, HD), BF16), sds((half, rows_here), F32), sds((rows_here, width // 2), F32)),
        (level_index, both, gap, gen_hidden, gen_t),
        scratch=(pltpu.VMEM((chans, rows_here), F32), pltpu.VMEM((half, 3 * HD), F32)),
        smem=1,
    )
    near = exchange(grad_piece, NEAR)
    near = call(near_body, sds((n_far, 3 * half + 8, HD), BF16), (near,))
    everything = exchange(near, "z_far")

    def last(*refs):
        last_body(*refs, entries=tokens * chans)

    grad_x_t, grad_hidden, grad_gen_t = call(
        last,
        (sds((half, rows_here), F32), sds((rows_here, width // 2), BF16), sds((half, 3 * HD), F32)),
        (level_index, everything, share, raw),
        smem=1,
    )
    return grad_x_t.T, grad_hidden, grad_gen_t.T


def solution(mesh):
    n_role, n_seq, n_mp = (mesh.shape[name] for name in ("role", "seq", "mp"))
    names = ("role", *SEQ, "mp")
    mesh = jax.sharding.Mesh(mesh.devices.reshape(n_role, n_seq // 8, 4, 2, n_mp), names)
    placed = (
        P(SEQ, None),
        P(),
        P(SEQ, None),
        P(),
        P("role", None, None),
        P("role", None, None),
        P("role", SEQ, None, "mp"),
        P("role", None, None),
        P("role", SEQ, None, "mp"),
        P("role", "mp", None),
        P("role", None, None),
    )
    return jax.shard_map(
        on_device,
        mesh=mesh,
        in_specs=placed,
        out_specs=(P(SEQ, "role"), P(SEQ, "role"), P("mp", "role")),
        check_vma=False,
    )
```

```python
import jax
import jax.numpy as jnp
from jax import lax
from jax.experimental import pallas as pl
from jax.experimental.pallas import tpu as pltpu
from jax.sharding import PartitionSpec as P

LEVELS = 1000
HD = 128
SEQ = ("z_far", "z_near", "y_hi")
NEAR = ("z_near", "y_hi")
CHANS = 64
PART = CHANS // 4
MROWS = 80
PIECE = 80
F32 = jnp.float32
BF16 = jnp.bfloat16
NN = (((1,), (0,)), ((), ()))
NT = (((1,), (1,)), ((), ()))


def dot(a, b, dims=NN):
    return lax.dot_general(a, b, dims, preferred_element_type=F32)


def call(body, out_shape, args, scratch=(), smem=0, limit=24):
    vmem = pl.BlockSpec(memory_space=pltpu.VMEM)
    scalars = pl.BlockSpec(memory_space=pltpu.SMEM)
    return pl.pallas_call(
        body,
        out_shape=out_shape,
        in_specs=[scalars if i < smem else vmem for i in range(len(args))],
        out_specs=jax.tree.map(lambda out: scalars if out.dtype == jnp.int32 else vmem, out_shape),
        scratch_shapes=list(scratch),
        compiler_params=pltpu.CompilerParams(vmem_limit_bytes=limit * 1024 * 1024),
    )(*args)


def seq_here():
    return (lax.axis_index("z_far") * 4 + lax.axis_index("z_near")) * 2 + lax.axis_index("y_hi")


def noise_scale_of(level, shape):
    time_frac = (jnp.full(shape, level, jnp.int32).astype(F32) + 1.0) / (LEVELS + 1.0)
    return 3.0 * time_frac / (1.0 + 2.0 * time_frac)


def weight_body(embed_ref, mod_ref, qkv_ref, payload_ref, order_ref, term_ref):
    width = embed_ref.shape[1]
    features = qkv_ref.shape[1]
    offset = seq_here() * features
    start = pl.multiple_of(jnp.minimum((offset >> 7) << 7, width - 256), HD)
    mean = jnp.sum(embed_ref[...].astype(F32), axis=1, keepdims=True) / width
    window = embed_ref[:, pl.ds(start, 256)].astype(F32)
    scale = 1.0 + mod_ref[1, :, pl.ds(start, 256)]
    shift = mod_ref[0, :, pl.ds(start, 256)]
    rows = jnp.concatenate(
        [(window - mean) * scale, shift, jnp.zeros((MROWS - CHANS - 1, 256), F32)], axis=0
    )
    select = jnp.where(
        lax.broadcasted_iota(jnp.int32, (256, features), 0)
        == lax.broadcasted_iota(jnp.int32, (256, features), 1) + (offset - start),
        1.0,
        0.0,
    ).astype(BF16)
    high = rows.astype(BF16)
    low = dot((rows - high.astype(F32)).astype(BF16), select).astype(BF16)
    high = dot(high, select).astype(BF16)
    for part in range(3):
        term = dot(high, qkv_ref[part]) + dot(low, qkv_ref[part])
        for head in range(3):
            j = part * 3 + head
            block = term[:, head * HD : (head + 1) * HD]
            term_ref[j * CHANS : (j + 1) * CHANS, :] = block[0:CHANS, :]
            term_ref[9 * CHANS + j : 9 * CHANS + j + 1, :] = block[CHANS : CHANS + 1, :]
    term_ref[9 * CHANS + 9 :, :] = jnp.zeros((term_ref.shape[0] - 9 * CHANS - 9, HD), F32)
    for p in range(payload_ref.shape[0]):
        payload_ref[p] = term_ref[p * PIECE : (p + 1) * PIECE, :].astype(BF16)
    order_ref[0] = 0


def latent_body(
    level_ref, _, hidden_ref, gen_t_ref, noise_t_ref, embed_ref, text_in_ref, noised_ref, gap_ref, send_ref
):
    x_t = dot(gen_t_ref[...], hidden_ref[...], NT)
    noise_scale = noise_scale_of(level_ref[0], x_t.shape)
    noised_t = ((1.0 - noise_scale) * x_t + noise_scale * noise_t_ref[...].astype(F32)).astype(BF16)
    noised = noised_t.astype(F32).T
    noised_ref[...] = noised
    gap_ref[...] = (x_t - noised_t.astype(F32)).T
    width = embed_ref.shape[1]
    step = 512
    embed_mean = jnp.zeros((embed_ref.shape[0], HD), F32)
    for j in range(width // HD):
        embed_mean = embed_mean + embed_ref[:, j * HD : (j + 1) * HD].astype(F32)
    embed_mean = jnp.sum(embed_mean, axis=1, keepdims=True) / width
    row_mean = jnp.sum(noised_t.astype(F32) * embed_mean, axis=0, keepdims=True)
    row_mean = jnp.broadcast_to(row_mean, (HD, noised.shape[0])).T
    row_var = jnp.zeros(row_mean.shape, F32)
    noised_b = noised.astype(BF16)
    for j in range(width // step):
        h = dot(noised_b, embed_ref[:, j * step : (j + 1) * step])
        for k in range(step // HD):
            row_var = row_var + jnp.square(h[:, k * HD : (k + 1) * HD] - row_mean)
    row_var = jnp.sum(row_var, axis=1, keepdims=True) / width
    send_ref[0:CHANS, :] = (noised * lax.rsqrt(row_var + 1e-06)).T.astype(BF16)
    text = text_in_ref[...].astype(F32)
    for j in range(6):
        block = text[:, j // 3, (j % 3) * HD : (j % 3 + 1) * HD]
        send_ref[CHANS + j * 16 : CHANS + (j + 1) * 16, :] = block.astype(BF16)


def total_of(ref, rows):
    total = ref[0, 0:rows, :].astype(F32)
    for i in range(1, ref.shape[0]):
        total = total + ref[i, 0:rows, :].astype(F32)
    return total.astype(BF16)


def far_body(recv_ref, send_ref, out_ref):
    piece = total_of(recv_ref, PIECE)
    channels = send_ref[pl.ds(pl.multiple_of((lax.axis_index("mp") & 3) * PART, PART), PART), :]
    for i in range(out_ref.shape[0]):
        out_ref[i, 0:PIECE, :] = piece
        out_ref[i, PIECE : PIECE + PART, :] = channels
        out_ref[i, PIECE + PART :, :] = send_ref[CHANS:, :]


def spread_body(recv_ref, out_ref, text_ref):
    piece = total_of(recv_ref, PIECE)
    text = PIECE + PART
    for i in range(out_ref.shape[0]):
        out_ref[i, 0:PIECE, :] = piece
        for g in range(recv_ref.shape[0]):
            out_ref[i, PIECE + g * PART : PIECE + (g + 1) * PART, :] = recv_ref[g, PIECE:text, :]
            text_ref[i, g * 96 : (g + 1) * 96, :] = recv_ref[g, text:, :]


def image_body(
    send_ref, recv_ref, other1_ref, other2_ref, other3_ref, gain_ref, out_ref, lat_ref, s_ref, v_ref, m_ref, own_ref, sum_ref
):
    tokens = lat_ref.shape[1]
    chunk = 2048
    n_chunks = tokens // chunk
    ones = jnp.where(lax.broadcasted_iota(jnp.int32, (MROWS - CHANS, HD), 0) == 0, 1.0, 0.0).astype(BF16)
    other_refs = (other1_ref, other2_ref, other3_ref)
    n_far = (recv_ref.shape[1] - PIECE) // PART
    for i in range(tokens // HD):
        near, first = i // n_far, (i % n_far) * PART
        at = slice(i * HD, (i + 1) * HD)
        lat_ref[0:PART, at] = recv_ref[near, PIECE + first : PIECE + first + PART, :]
        for k, ref in enumerate(other_refs):
            lat_ref[(k + 1) * PART : (k + 2) * PART, at] = ref[near, first : first + PART, :]
        lat_ref[CHANS:MROWS, at] = ones
    for i in range(recv_ref.shape[0]):
        m_ref[i * PIECE : (i + 1) * PIECE, :] = recv_ref[i, 0:PIECE, :].astype(F32)
    own_ref[...] = send_ref[0:CHANS, :].astype(F32)

    def reordered(ref, base):
        here = lax.axis_index("mp") & 3
        starts = [pl.multiple_of((here ^ k) * PART + base, PART) for k in range(4)]
        return jnp.concatenate([ref[pl.ds(start, PART), :] for start in starts], axis=0)

    own = jnp.concatenate([reordered(own_ref, 0).astype(BF16), ones], axis=0)
    score_scale = HD ** (-0.5) * 1.4426950408889634
    biases = m_ref[9 * CHANS : 9 * CHANS + 16, :]

    def weight(j):
        block = reordered(m_ref, j * CHANS)
        pad = jnp.zeros((HD - CHANS - 1, HD), F32)
        return jnp.concatenate([block, biases[j : j + 1, :], pad], axis=0).T[:, 0:MROWS].astype(BF16)

    q_image, w_k, w_v = [], [], []
    for head in range(3):
        q_t = dot(weight(head), own)
        q_t = q_t * lax.rsqrt(jnp.mean(q_t * q_t, axis=0, keepdims=True) + 1e-06)
        q = q_t.T * (gain_ref[0:1, :] * score_scale)
        out_ref[3 + head] = q
        q_image.append((q * gain_ref[1:2, :]).astype(BF16))
        w_k.append(weight(3 + head))
        w_v.append(weight(6 + head))
    rows = q_image[0].shape[0]

    def score_step(c, tops):
        at = pl.ds(pl.multiple_of(c * chunk, chunk), chunk)
        lat = lat_ref[:, at]
        out = []
        for head in range(3):
            k_t = dot(w_k[head], lat)
            k_t = k_t * lax.rsqrt(jnp.mean(k_t * k_t, axis=0, keepdims=True) + 1e-06)
            v_ref[head, :, at] = dot(w_v[head], lat).astype(BF16)
            s = dot(q_image[head], k_t.astype(BF16))
            s_ref[head, :, at] = s
            top = tops[head]
            for j in range(chunk // HD):
                top = jnp.maximum(top, s[:, j * HD : (j + 1) * HD])
            out.append(top)
        return tuple(out)

    tops = lax.fori_loop(0, n_chunks, score_step, (jnp.full((rows, HD), -3e38, F32),) * 3)
    tops = [jnp.max(top, axis=1, keepdims=True) for top in tops]
    for head in range(3):
        out_ref[head] = jnp.zeros((rows, HD), F32)
        sum_ref[head] = jnp.zeros((rows, HD), F32)

    def mix_step(c, carry):
        at = pl.ds(pl.multiple_of(c * chunk, chunk), chunk)
        for head in range(3):
            p = jnp.exp2(s_ref[head, :, at] - tops[head])
            total = sum_ref[head]
            for j in range(chunk // HD):
                total = total + p[:, j * HD : (j + 1) * HD]
            sum_ref[head] = total
            out_ref[head] += dot(p.astype(BF16), v_ref[head, :, at], NT)
        return carry

    lax.fori_loop(0, n_chunks, mix_step, 0)
    lane = lax.broadcasted_iota(jnp.int32, (rows, HD), 1)
    numbers = jnp.zeros((rows, HD), F32)
    for head in range(3):
        numbers = jnp.where(lane == head, tops[head], numbers)
        numbers = jnp.where(lane == 3 + head, jnp.sum(sum_ref[head], axis=1, keepdims=True), numbers)
    out_ref[6] = numbers


def text_body(image_ref, text_ref, own_ref, other_ref, att_ref):
    def block(first):
        return text_ref[:, first : first + 16, :].reshape(text_ref.shape[0] * 16, HD)

    for head in range(3):
        s = dot(image_ref[3 + head].astype(BF16), block(head * 16), NT)
        image_top = image_ref[6][:, head : head + 1]
        top = jnp.maximum(image_top, jnp.max(s, axis=1, keepdims=True))
        keep = jnp.exp2(image_top - top)
        p = jnp.exp2(s - top)
        acc = image_ref[head] * keep + dot(p.astype(BF16), block(48 + head * 16))
        total = image_ref[6][:, 3 + head : 4 + head] * keep + jnp.sum(p, axis=1, keepdims=True)
        att_ref[:, :, head * HD : (head + 1) * HD] = (acc / total).reshape(att_ref.shape[0], -1, HD)
    core = lax.axis_index("mp") & 1
    for i in range(own_ref.shape[0]):
        own_ref[i] = att_ref[2 * i + core].astype(BF16)
        other_ref[i] = att_ref[2 * i + 1 - core].astype(BF16)


def velocity_body(parts_ref, noised_ref, embed_ref, mod_ref, final_t_ref, v_ref):
    total = parts_ref[0].astype(F32)
    for i in range(1, parts_ref.shape[0]):
        total = total + parts_ref[i].astype(F32)
    own_rows = total.shape[0]
    own = noised_ref[pl.ds(pl.multiple_of(lax.axis_index("mp") * own_rows, own_rows), own_rows), :].astype(BF16)
    h = dot(own, embed_ref[...]) + mod_ref[2] * total
    width = h.shape[1]
    h = h - jnp.sum(h, axis=1, keepdims=True) / width
    var = jnp.sum(h * h, axis=1, keepdims=True) / width
    v = dot((h * lax.rsqrt(var + 1e-06)).astype(BF16), final_t_ref[...], NT)
    v = jnp.concatenate([v[0:8, :], v[8:16, :]], axis=1)
    for i in range(v_ref.shape[0]):
        v_ref[i] = v


def grad_body(level_ref, both_ref, gap_ref, hidden_ref, gen_t_ref, piece_ref, share_ref, raw_ref, diff_ref, grad_ref):
    n_mp = both_ref.shape[0] // 2
    chans = gap_ref.shape[1]

    def rows(first):
        blocks = []
        for i in range(first, first + n_mp):
            blocks += [both_ref[i][:, 0:chans], both_ref[i][:, chans : 2 * chans]]
        return jnp.concatenate(blocks, axis=0)

    teacher, student = rows(0), rows(n_mp)
    spread = jnp.abs(gap_ref[...] + noise_scale_of(level_ref[0], gap_ref.shape) * teacher)
    spread = jnp.sum(jnp.sum(spread, axis=1, keepdims=True), axis=0, keepdims=True)
    spread = jnp.broadcast_to(spread, (8, HD))
    diff = teacher - student
    diff_ref[...] = diff.T
    half = chans // 2
    share = diff_ref[pl.ds(pl.multiple_of(lax.axis_index("role") * half, half), half), :]
    share_ref[...] = share
    cols = grad_ref.shape[1]
    hidden = hidden_ref[:, pl.ds(pl.multiple_of(lax.axis_index("mp") * cols, HD), cols)]
    grad_ref[...] = dot(share.astype(BF16), hidden)
    terms = [grad_ref[:, g * HD : (g + 1) * HD] for g in range(3)]
    block = in_parts(jnp.concatenate([*terms, spread], axis=0))
    for i in range(piece_ref.shape[0]):
        piece_ref[i] = block
    feats = raw_ref.shape[1]
    raw_ref[...] = dot(diff.astype(BF16), gen_t_ref[:, pl.ds(pl.multiple_of(lax.axis_index("role") * feats, HD), feats)])


def in_parts(block):
    row = lax.broadcasted_iota(jnp.int32, block.shape, 0) - (block.shape[0] - 8)
    high = block.astype(BF16).astype(F32)
    mid = (block - high).astype(BF16).astype(F32)
    low = block - high - mid
    return jnp.where(row == 1, mid, jnp.where(row == 2, low, high)).astype(BF16)


def whole_total(ref):
    total = ref[0].astype(F32)
    for i in range(1, ref.shape[0]):
        total = total + ref[i].astype(F32)
    last = total.shape[0] - 8
    number = total[last : last + 1, :] + total[last + 1 : last + 2, :] + total[last + 2 : last + 3, :]
    return total[0:last, :], number


def near_body(recv_ref, out_ref):
    total, number = whole_total(recv_ref)
    out = in_parts(jnp.concatenate([total, jnp.broadcast_to(number, (8, HD))], axis=0))
    for i in range(out_ref.shape[0]):
        out_ref[i] = out


def last_body(level_ref, recv_ref, share_ref, raw_ref, x_ref, hidden_ref, gen_ref, *, entries):
    total, number = whole_total(recv_ref)
    factor = noise_scale_of(level_ref[0], (1, 1)) / (number[:, 0:1] / entries + 1e-06)
    x_ref[...] = share_ref[...] * factor
    hidden_ref[...] = (raw_ref[...] * factor).astype(BF16)
    half = gen_ref.shape[0]
    for g in range(3):
        gen_ref[:, g * HD : (g + 1) * HD] = total[g * half : (g + 1) * half, :] * factor


def exchange(array, axis, groups=None):
    return lax.all_to_all(array, axis, 0, 0, axis_index_groups=groups, tiled=True)


def on_device(
    gen_hidden, w_gen, noise_latent, level_index, w_embed, modulation, w_qkv, qk_gain, text_kv, w_out, w_final
):
    rows_here, width = gen_hidden.shape
    n_seq, n_far, n_mp = lax.axis_size(SEQ), lax.axis_size("z_far"), lax.axis_size("mp")
    chans = w_gen.shape[1]
    tokens = rows_here * n_seq
    sds = jax.ShapeDtypeStruct
    mods = jnp.transpose(modulation, (1, 0, 2))
    embed = w_embed[0]
    gen_t = w_gen.T
    payload, order = call(
        weight_body,
        (sds((8, PIECE, HD), BF16), sds((1,), jnp.int32)),
        (embed, mods, jnp.transpose(w_qkv[0], (1, 0, 2))),
        scratch=(pltpu.VMEM((8 * PIECE, HD), F32),),
        limit=60,
    )
    noised, gap, send = call(
        latent_body,
        (
            sds((rows_here, chans), F32),
            sds((rows_here, chans), F32),
            sds((chans + 96, HD), BF16),
        ),
        (level_index, order, gen_hidden, gen_t, noise_latent.T, embed, text_kv[0]),
        smem=2,
        limit=60,
    )
    pieces = exchange(payload, NEAR)
    pieces = call(far_body, sds((n_far, PIECE + PART + 96, HD), BF16), (pieces, send))
    pieces = exchange(pieces, "z_far")
    pieces, text = call(
        spread_body,
        (sds((8, PIECE + n_far * PART, HD), BF16), sds((8, n_far * 96, HD), BF16)),
        (pieces,),
    )
    pieces = exchange(pieces, NEAR)
    text = exchange(text, NEAR).reshape(n_seq, 96, HD)
    channels = pieces[:, PIECE:, :]
    others = [lax.ppermute(channels, "mp", [(i, i ^ k) for i in range(n_mp)]) for k in (1, 2, 3)]

    image = call(
        image_body,
        sds((7, rows_here, HD), F32),
        (send, pieces, *others, qk_gain[0]),
        scratch=(
            pltpu.VMEM((MROWS, tokens), BF16),
            pltpu.VMEM((3, rows_here, tokens), F32),
            pltpu.VMEM((3, HD, tokens), BF16),
            pltpu.VMEM((8 * PIECE, HD), F32),
            pltpu.VMEM((chans, HD), F32),
            pltpu.VMEM((3, rows_here, HD), F32),
        ),
    )
    own_rows = rows_here // n_mp
    share = sds((n_mp // 2, own_rows, 3 * HD), BF16)
    att_own, att_other = call(
        text_body, (share, share), (image, text), scratch=(pltpu.VMEM((n_mp, own_rows, 3 * HD), F32),)
    )
    y_other = dot(att_other.reshape(-1, 3 * HD), w_out[0]).astype(BF16)
    y_other = lax.ppermute(y_other, "mp", [(i, i ^ 1) for i in range(n_mp)])
    y = (dot(att_own.reshape(-1, 3 * HD), w_out[0]) + y_other.astype(F32)).astype(BF16)
    same_core = [[2 * x + core for x in range(n_mp // 2)] for core in range(2)]
    parts = exchange(y.reshape(n_mp // 2, own_rows, width), "mp", same_core)
    velocity = call(
        velocity_body,
        sds((2 * n_mp, 8, 2 * chans), F32),
        (parts, noised, embed, mods, w_final[0].T),
    )
    both = exchange(velocity, ("role", "mp"))
    half = chans // 2
    grad_piece, share, raw = call(
        grad_body,
        (sds((8, 3 * half + 8, HD), BF16), sds((half, rows_here), F32), sds((rows_here, width // 2), F32)),
        (level_index, both, gap, gen_hidden, gen_t),
        scratch=(pltpu.VMEM((chans, rows_here), F32), pltpu.VMEM((half, 3 * HD), F32)),
        smem=1,
    )
    near = exchange(grad_piece, NEAR)
    near = call(near_body, sds((n_far, 3 * half + 8, HD), BF16), (near,))
    everything = exchange(near, "z_far")

    def last(*refs):
        last_body(*refs, entries=tokens * chans)

    grad_x_t, grad_hidden, grad_gen_t = call(
        last,
        (sds((half, rows_here), F32), sds((rows_here, width // 2), BF16), sds((half, 3 * HD), F32)),
        (level_index, everything, share, raw),
        smem=1,
    )
    return grad_x_t.T, grad_hidden, grad_gen_t.T


def solution(mesh):
    n_role, n_seq, n_mp = (mesh.shape[name] for name in ("role", "seq", "mp"))
    names = ("role", *SEQ, "mp")
    mesh = jax.sharding.Mesh(mesh.devices.reshape(n_role, n_seq // 8, 4, 2, n_mp), names)
    placed = (
        P(SEQ, None),
        P(),
        P(SEQ, None),
        P(),
        P("role", None, None),
        P("role", None, None),
        P("role", SEQ, None, "mp"),
        P("role", None, None),
        P("role", SEQ, None, "mp"),
        P("role", "mp", None),
        P("role", None, None),
    )
    return jax.shard_map(
        on_device,
        mesh=mesh,
        in_specs=placed,
        out_specs=(P(SEQ, "role"), P(SEQ, "role"), P("mp", "role")),
        check_vma=False,
    )
```

```python
import jax
import jax.numpy as jnp
from jax import lax
from jax.experimental import pallas as pl
from jax.experimental.pallas import tpu as pltpu
from jax.sharding import PartitionSpec as P

LEVELS = 1000
HD = 128
SEQ = ("z_far", "z_near", "y_hi")
NEAR = ("z_near", "y_hi")
CHANS = 64
PART = CHANS // 4
MROWS = 80
PIECE = 80
F32 = jnp.float32
BF16 = jnp.bfloat16
NN = (((1,), (0,)), ((), ()))
NT = (((1,), (1,)), ((), ()))


def dot(a, b, dims=NN):
    return lax.dot_general(a, b, dims, preferred_element_type=F32)


def call(body, out_shape, args, scratch=(), smem=0, limit=24):
    vmem = pl.BlockSpec(memory_space=pltpu.VMEM)
    scalars = pl.BlockSpec(memory_space=pltpu.SMEM)
    return pl.pallas_call(
        body,
        out_shape=out_shape,
        in_specs=[scalars if i < smem else vmem for i in range(len(args))],
        out_specs=jax.tree.map(lambda out: scalars if out.dtype == jnp.int32 else vmem, out_shape),
        scratch_shapes=list(scratch),
        compiler_params=pltpu.CompilerParams(vmem_limit_bytes=limit * 1024 * 1024),
    )(*args)


def seq_here():
    return (lax.axis_index("z_far") * 4 + lax.axis_index("z_near")) * 2 + lax.axis_index("y_hi")


def noise_scale_of(level, shape):
    time_frac = (jnp.full(shape, level, jnp.int32).astype(F32) + 1.0) / (LEVELS + 1.0)
    return 3.0 * time_frac / (1.0 + 2.0 * time_frac)


def weight_body(embed_ref, mod_ref, qkv_ref, payload_ref, order_ref, term_ref):
    width = embed_ref.shape[1]
    features = qkv_ref.shape[1]
    offset = seq_here() * features
    start = pl.multiple_of(jnp.minimum((offset >> 7) << 7, width - 256), HD)
    mean = jnp.sum(embed_ref[...].astype(F32), axis=1, keepdims=True) / width
    window = embed_ref[:, pl.ds(start, 256)].astype(F32)
    scale = 1.0 + mod_ref[1, :, pl.ds(start, 256)]
    shift = mod_ref[0, :, pl.ds(start, 256)]
    rows = jnp.concatenate(
        [(window - mean) * scale, shift, jnp.zeros((MROWS - CHANS - 1, 256), F32)], axis=0
    )
    select = jnp.where(
        lax.broadcasted_iota(jnp.int32, (256, features), 0)
        == lax.broadcasted_iota(jnp.int32, (256, features), 1) + (offset - start),
        1.0,
        0.0,
    ).astype(BF16)
    high = rows.astype(BF16)
    low = dot((rows - high.astype(F32)).astype(BF16), select).astype(BF16)
    high = dot(high, select).astype(BF16)
    for part in range(3):
        term = dot(high, qkv_ref[part]) + dot(low, qkv_ref[part])
        for head in range(3):
            j = part * 3 + head
            block = term[:, head * HD : (head + 1) * HD]
            term_ref[j * CHANS : (j + 1) * CHANS, :] = block[0:CHANS, :]
            term_ref[9 * CHANS + j : 9 * CHANS + j + 1, :] = block[CHANS : CHANS + 1, :]
    term_ref[9 * CHANS + 9 :, :] = jnp.zeros((term_ref.shape[0] - 9 * CHANS - 9, HD), F32)
    for p in range(payload_ref.shape[0]):
        payload_ref[p] = term_ref[p * PIECE : (p + 1) * PIECE, :].astype(BF16)
    order_ref[0] = 0


def latent_body(
    level_ref, _, hidden_ref, gen_t_ref, noise_t_ref, embed_ref, text_in_ref, noised_ref, gap_ref, send_ref
):
    x_t = dot(gen_t_ref[...], hidden_ref[...], NT)
    noise_scale = noise_scale_of(level_ref[0], x_t.shape)
    noised_t = ((1.0 - noise_scale) * x_t + noise_scale * noise_t_ref[...].astype(F32)).astype(BF16)
    noised = noised_t.astype(F32).T
    noised_ref[...] = noised
    gap_ref[...] = (x_t - noised_t.astype(F32)).T
    width = embed_ref.shape[1]
    step = 512
    embed_mean = jnp.zeros((embed_ref.shape[0], HD), F32)
    for j in range(width // HD):
        embed_mean = embed_mean + embed_ref[:, j * HD : (j + 1) * HD].astype(F32)
    embed_mean = jnp.sum(embed_mean, axis=1, keepdims=True) / width
    row_mean = jnp.sum(noised_t.astype(F32) * embed_mean, axis=0, keepdims=True)
    row_mean = jnp.broadcast_to(row_mean, (HD, noised.shape[0])).T
    row_var = jnp.zeros(row_mean.shape, F32)
    noised_b = noised.astype(BF16)
    for j in range(width // step):
        h = dot(noised_b, embed_ref[:, j * step : (j + 1) * step])
        for k in range(step // HD):
            row_var = row_var + jnp.square(h[:, k * HD : (k + 1) * HD] - row_mean)
    row_var = jnp.sum(row_var, axis=1, keepdims=True) / width
    send_ref[0:CHANS, :] = (noised * lax.rsqrt(row_var + 1e-06)).T.astype(BF16)
    text = text_in_ref[...].astype(F32)
    for j in range(6):
        block = text[:, j // 3, (j % 3) * HD : (j % 3 + 1) * HD]
        send_ref[CHANS + j * 16 : CHANS + (j + 1) * 16, :] = block.astype(BF16)


def total_of(ref, rows):
    total = ref[0, 0:rows, :].astype(F32)
    for i in range(1, ref.shape[0]):
        total = total + ref[i, 0:rows, :].astype(F32)
    return total.astype(BF16)


def far_body(recv_ref, send_ref, out_ref):
    piece = total_of(recv_ref, PIECE)
    channels = send_ref[pl.ds(pl.multiple_of((lax.axis_index("mp") & 3) * PART, PART), PART), :]
    for i in range(out_ref.shape[0]):
        out_ref[i, 0:PIECE, :] = piece
        out_ref[i, PIECE : PIECE + PART, :] = channels
        out_ref[i, PIECE + PART :, :] = send_ref[CHANS:, :]


def spread_body(recv_ref, out_ref, text_ref):
    piece = total_of(recv_ref, PIECE)
    text = PIECE + PART
    for i in range(out_ref.shape[0]):
        out_ref[i, 0:PIECE, :] = piece
        for g in range(recv_ref.shape[0]):
            out_ref[i, PIECE + g * PART : PIECE + (g + 1) * PART, :] = recv_ref[g, PIECE:text, :]
            text_ref[i, g * 96 : (g + 1) * 96, :] = recv_ref[g, text:, :]


def image_body(
    send_ref, recv_ref, other1_ref, other2_ref, other3_ref, gain_ref, out_ref, lat_ref, s_ref, v_ref, m_ref, own_ref, sum_ref
):
    tokens = lat_ref.shape[1]
    chunk = 2048
    n_chunks = tokens // chunk
    ones = jnp.where(lax.broadcasted_iota(jnp.int32, (MROWS - CHANS, HD), 0) == 0, 1.0, 0.0).astype(BF16)
    other_refs = (other1_ref, other2_ref, other3_ref)
    n_far = (recv_ref.shape[1] - PIECE) // PART
    for i in range(tokens // HD):
        near, first = i // n_far, (i % n_far) * PART
        at = slice(i * HD, (i + 1) * HD)
        lat_ref[0:PART, at] = recv_ref[near, PIECE + first : PIECE + first + PART, :]
        for k, ref in enumerate(other_refs):
            lat_ref[(k + 1) * PART : (k + 2) * PART, at] = ref[near, first : first + PART, :]
        lat_ref[CHANS:MROWS, at] = ones
    for i in range(recv_ref.shape[0]):
        m_ref[i * PIECE : (i + 1) * PIECE, :] = recv_ref[i, 0:PIECE, :].astype(F32)
    own_ref[...] = send_ref[0:CHANS, :].astype(F32)

    def reordered(ref, base):
        here = lax.axis_index("mp") & 3
        starts = [pl.multiple_of((here ^ k) * PART + base, PART) for k in range(4)]
        return jnp.concatenate([ref[pl.ds(start, PART), :] for start in starts], axis=0)

    own = jnp.concatenate([reordered(own_ref, 0).astype(BF16), ones], axis=0)
    score_scale = HD ** (-0.5) * 1.4426950408889634
    biases = m_ref[9 * CHANS : 9 * CHANS + 16, :]

    def weight(j):
        block = reordered(m_ref, j * CHANS)
        pad = jnp.zeros((HD - CHANS - 1, HD), F32)
        return jnp.concatenate([block, biases[j : j + 1, :], pad], axis=0).T[:, 0:MROWS].astype(BF16)

    q_image, w_k, w_v = [], [], []
    for head in range(3):
        q_t = dot(weight(head), own)
        q_t = q_t * lax.rsqrt(jnp.mean(q_t * q_t, axis=0, keepdims=True) + 1e-06)
        q = q_t.T * (gain_ref[0:1, :] * score_scale)
        out_ref[3 + head] = q
        q_image.append((q * gain_ref[1:2, :]).astype(BF16))
        w_k.append(weight(3 + head))
        w_v.append(weight(6 + head))
    rows = q_image[0].shape[0]

    def score_step(c, tops):
        at = pl.ds(pl.multiple_of(c * chunk, chunk), chunk)
        lat = lat_ref[:, at]
        out = []
        for head in range(3):
            k_t = dot(w_k[head], lat)
            k_t = k_t * lax.rsqrt(jnp.mean(k_t * k_t, axis=0, keepdims=True) + 1e-06)
            v_ref[head, :, at] = dot(w_v[head], lat).astype(BF16)
            s = dot(q_image[head], k_t.astype(BF16))
            s_ref[head, :, at] = s
            top = tops[head]
            for j in range(chunk // HD):
                top = jnp.maximum(top, s[:, j * HD : (j + 1) * HD])
            out.append(top)
        return tuple(out)

    tops = lax.fori_loop(0, n_chunks, score_step, (jnp.full((rows, HD), -3e38, F32),) * 3)
    tops = [jnp.max(top, axis=1, keepdims=True) for top in tops]
    for head in range(3):
        out_ref[head] = jnp.zeros((rows, HD), F32)
        sum_ref[head] = jnp.zeros((rows, HD), F32)

    def mix_step(c, carry):
        at = pl.ds(pl.multiple_of(c * chunk, chunk), chunk)
        for head in range(3):
            p = jnp.exp2(s_ref[head, :, at] - tops[head])
            total = sum_ref[head]
            for j in range(chunk // HD):
                total = total + p[:, j * HD : (j + 1) * HD]
            sum_ref[head] = total
            out_ref[head] += dot(p.astype(BF16), v_ref[head, :, at], NT)
        return carry

    lax.fori_loop(0, n_chunks, mix_step, 0)
    lane = lax.broadcasted_iota(jnp.int32, (rows, HD), 1)
    numbers = jnp.zeros((rows, HD), F32)
    for head in range(3):
        numbers = jnp.where(lane == head, tops[head], numbers)
        numbers = jnp.where(lane == 3 + head, jnp.sum(sum_ref[head], axis=1, keepdims=True), numbers)
    out_ref[6] = numbers


def text_body(image_ref, text_ref, own_ref, other_ref, att_ref):
    def block(first):
        return text_ref[:, first : first + 16, :].reshape(text_ref.shape[0] * 16, HD)

    for head in range(3):
        s = dot(image_ref[3 + head].astype(BF16), block(head * 16), NT)
        image_top = image_ref[6][:, head : head + 1]
        top = jnp.maximum(image_top, jnp.max(s, axis=1, keepdims=True))
        keep = jnp.exp2(image_top - top)
        p = jnp.exp2(s - top)
        acc = image_ref[head] * keep + dot(p.astype(BF16), block(48 + head * 16))
        total = image_ref[6][:, 3 + head : 4 + head] * keep + jnp.sum(p, axis=1, keepdims=True)
        att_ref[:, :, head * HD : (head + 1) * HD] = (acc / total).reshape(att_ref.shape[0], -1, HD)
    core = lax.axis_index("mp") & 1
    for i in range(own_ref.shape[0]):
        own_ref[i] = att_ref[2 * i + core].astype(BF16)
        other_ref[i] = att_ref[2 * i + 1 - core].astype(BF16)


def project_body(own_ref, other_ref, out_w_ref, y_own_ref, y_other_ref):
    own = own_ref[...].reshape(-1, own_ref.shape[2])
    other = other_ref[...].reshape(-1, own_ref.shape[2])
    step = 512
    for j in range(out_w_ref.shape[1] // step):
        at = slice(j * step, (j + 1) * step)
        out_w = out_w_ref[:, at]
        y_other_ref[:, at] = dot(other, out_w).astype(BF16)
        y_own_ref[:, at] = dot(own, out_w)


def velocity_body(parts_ref, noised_ref, embed_ref, mod_ref, final_t_ref, v_ref):
    total = parts_ref[0].astype(F32)
    for i in range(1, parts_ref.shape[0]):
        total = total + parts_ref[i].astype(F32)
    own_rows = total.shape[0]
    own = noised_ref[pl.ds(pl.multiple_of(lax.axis_index("mp") * own_rows, own_rows), own_rows), :].astype(BF16)
    h = dot(own, embed_ref[...]) + mod_ref[2] * total
    width = h.shape[1]
    h = h - jnp.sum(h, axis=1, keepdims=True) / width
    var = jnp.sum(h * h, axis=1, keepdims=True) / width
    v = dot((h * lax.rsqrt(var + 1e-06)).astype(BF16), final_t_ref[...], NT)
    v = jnp.concatenate([v[0:8, :], v[8:16, :]], axis=1)
    for i in range(v_ref.shape[0]):
        v_ref[i] = v


def grad_body(level_ref, both_ref, gap_ref, hidden_ref, gen_t_ref, piece_ref, share_ref, raw_ref, diff_ref, grad_ref):
    n_mp = both_ref.shape[0] // 2
    chans = gap_ref.shape[1]

    def rows(first):
        blocks = []
        for i in range(first, first + n_mp):
            blocks += [both_ref[i][:, 0:chans], both_ref[i][:, chans : 2 * chans]]
        return jnp.concatenate(blocks, axis=0)

    teacher, student = rows(0), rows(n_mp)
    spread = jnp.abs(gap_ref[...] + noise_scale_of(level_ref[0], gap_ref.shape) * teacher)
    spread = jnp.sum(jnp.sum(spread, axis=1, keepdims=True), axis=0, keepdims=True)
    spread = jnp.broadcast_to(spread, (8, HD))
    diff = teacher - student
    diff_ref[...] = diff.T
    half = chans // 2
    share = diff_ref[pl.ds(pl.multiple_of(lax.axis_index("role") * half, half), half), :]
    share_ref[...] = share
    cols = grad_ref.shape[1]
    hidden = hidden_ref[:, pl.ds(pl.multiple_of(lax.axis_index("mp") * cols, HD), cols)]
    grad_ref[...] = dot(share.astype(BF16), hidden)
    terms = [grad_ref[:, g * HD : (g + 1) * HD] for g in range(3)]
    block = in_parts(jnp.concatenate([*terms, spread], axis=0))
    for i in range(piece_ref.shape[0]):
        piece_ref[i] = block
    feats = raw_ref.shape[1]
    raw_ref[...] = dot(diff.astype(BF16), gen_t_ref[:, pl.ds(pl.multiple_of(lax.axis_index("role") * feats, HD), feats)])


def in_parts(block):
    row = lax.broadcasted_iota(jnp.int32, block.shape, 0) - (block.shape[0] - 8)
    high = block.astype(BF16).astype(F32)
    mid = (block - high).astype(BF16).astype(F32)
    low = block - high - mid
    return jnp.where(row == 1, mid, jnp.where(row == 2, low, high)).astype(BF16)


def whole_total(ref):
    total = ref[0].astype(F32)
    for i in range(1, ref.shape[0]):
        total = total + ref[i].astype(F32)
    last = total.shape[0] - 8
    number = total[last : last + 1, :] + total[last + 1 : last + 2, :] + total[last + 2 : last + 3, :]
    return total[0:last, :], number


def near_body(recv_ref, out_ref):
    total, number = whole_total(recv_ref)
    out = in_parts(jnp.concatenate([total, jnp.broadcast_to(number, (8, HD))], axis=0))
    for i in range(out_ref.shape[0]):
        out_ref[i] = out


def last_body(level_ref, recv_ref, share_ref, raw_ref, x_ref, hidden_ref, gen_ref, *, entries):
    total, number = whole_total(recv_ref)
    factor = noise_scale_of(level_ref[0], (1, 1)) / (number[:, 0:1] / entries + 1e-06)
    x_ref[...] = share_ref[...] * factor
    hidden_ref[...] = (raw_ref[...] * factor).astype(BF16)
    half = gen_ref.shape[0]
    for g in range(3):
        gen_ref[:, g * HD : (g + 1) * HD] = total[g * half : (g + 1) * half, :] * factor


def exchange(array, axis, groups=None):
    return lax.all_to_all(array, axis, 0, 0, axis_index_groups=groups, tiled=True)


def on_device(
    gen_hidden, w_gen, noise_latent, level_index, w_embed, modulation, w_qkv, qk_gain, text_kv, w_out, w_final
):
    rows_here, width = gen_hidden.shape
    n_seq, n_far, n_mp = lax.axis_size(SEQ), lax.axis_size("z_far"), lax.axis_size("mp")
    chans = w_gen.shape[1]
    tokens = rows_here * n_seq
    sds = jax.ShapeDtypeStruct
    mods = jnp.transpose(modulation, (1, 0, 2))
    embed = w_embed[0]
    gen_t = w_gen.T
    payload, order = call(
        weight_body,
        (sds((8, PIECE, HD), BF16), sds((1,), jnp.int32)),
        (embed, mods, jnp.transpose(w_qkv[0], (1, 0, 2))),
        scratch=(pltpu.VMEM((8 * PIECE, HD), F32),),
        limit=60,
    )
    noised, gap, send = call(
        latent_body,
        (
            sds((rows_here, chans), F32),
            sds((rows_here, chans), F32),
            sds((chans + 96, HD), BF16),
        ),
        (level_index, order, gen_hidden, gen_t, noise_latent.T, embed, text_kv[0]),
        smem=2,
        limit=60,
    )
    pieces = exchange(payload, NEAR)
    pieces = call(far_body, sds((n_far, PIECE + PART + 96, HD), BF16), (pieces, send))
    pieces = exchange(pieces, "z_far")
    pieces, text = call(
        spread_body,
        (sds((8, PIECE + n_far * PART, HD), BF16), sds((8, n_far * 96, HD), BF16)),
        (pieces,),
    )
    pieces = exchange(pieces, NEAR)
    text = exchange(text, NEAR).reshape(n_seq, 96, HD)
    channels = pieces[:, PIECE:, :]
    others = [lax.ppermute(channels, "mp", [(i, i ^ k) for i in range(n_mp)]) for k in (1, 2, 3)]

    image = call(
        image_body,
        sds((7, rows_here, HD), F32),
        (send, pieces, *others, qk_gain[0]),
        scratch=(
            pltpu.VMEM((MROWS, tokens), BF16),
            pltpu.VMEM((3, rows_here, tokens), F32),
            pltpu.VMEM((3, HD, tokens), BF16),
            pltpu.VMEM((8 * PIECE, HD), F32),
            pltpu.VMEM((chans, HD), F32),
            pltpu.VMEM((3, rows_here, HD), F32),
        ),
    )
    own_rows = rows_here // n_mp
    share = sds((n_mp // 2, own_rows, 3 * HD), BF16)
    att_own, att_other = call(
        text_body, (share, share), (image, text), scratch=(pltpu.VMEM((n_mp, own_rows, 3 * HD), F32),)
    )
    y_own, y_other = call(
        project_body,
        (sds((rows_here // 2, width), F32), sds((rows_here // 2, width), BF16)),
        (att_own, att_other, w_out[0]),
    )
    y_other = lax.ppermute(y_other, "mp", [(i, i ^ 1) for i in range(n_mp)])
    y = (y_own + y_other.astype(F32)).astype(BF16)
    same_core = [[2 * x + core for x in range(n_mp // 2)] for core in range(2)]
    parts = exchange(y.reshape(n_mp // 2, own_rows, width), "mp", same_core)
    velocity = call(
        velocity_body,
        sds((2 * n_mp, 8, 2 * chans), F32),
        (parts, noised, embed, mods, w_final[0].T),
    )
    both = exchange(velocity, ("role", "mp"))
    half = chans // 2
    grad_piece, share, raw = call(
        grad_body,
        (sds((8, 3 * half + 8, HD), BF16), sds((half, rows_here), F32), sds((rows_here, width // 2), F32)),
        (level_index, both, gap, gen_hidden, gen_t),
        scratch=(pltpu.VMEM((chans, rows_here), F32), pltpu.VMEM((half, 3 * HD), F32)),
        smem=1,
    )
    near = exchange(grad_piece, NEAR)
    near = call(near_body, sds((n_far, 3 * half + 8, HD), BF16), (near,))
    everything = exchange(near, "z_far")

    def last(*refs):
        last_body(*refs, entries=tokens * chans)

    grad_x_t, grad_hidden, grad_gen_t = call(
        last,
        (sds((half, rows_here), F32), sds((rows_here, width // 2), BF16), sds((half, 3 * HD), F32)),
        (level_index, everything, share, raw),
        smem=1,
    )
    return grad_x_t.T, grad_hidden, grad_gen_t.T


def solution(mesh):
    n_role, n_seq, n_mp = (mesh.shape[name] for name in ("role", "seq", "mp"))
    names = ("role", *SEQ, "mp")
    mesh = jax.sharding.Mesh(mesh.devices.reshape(n_role, n_seq // 8, 4, 2, n_mp), names)
    placed = (
        P(SEQ, None),
        P(),
        P(SEQ, None),
        P(),
        P("role", None, None),
        P("role", None, None),
        P("role", SEQ, None, "mp"),
        P("role", None, None),
        P("role", SEQ, None, "mp"),
        P("role", "mp", None),
        P("role", None, None),
    )
    return jax.shard_map(
        on_device,
        mesh=mesh,
        in_specs=placed,
        out_specs=(P(SEQ, "role"), P(SEQ, "role"), P("mp", "role")),
        check_vma=False,
    )
```

```python
import jax
import jax.numpy as jnp
from jax import lax
from jax.experimental import pallas as pl
from jax.experimental.pallas import tpu as pltpu
from jax.sharding import PartitionSpec as P

LEVELS = 1000
HD = 128
SEQ = ("z_far", "z_near", "y_hi")
NEAR = ("z_near", "y_hi")
CHANS = 64
PART = CHANS // 4
MROWS = 80
PIECE = 80
F32 = jnp.float32
BF16 = jnp.bfloat16
NN = (((1,), (0,)), ((), ()))
NT = (((1,), (1,)), ((), ()))


def dot(a, b, dims=NN):
    return lax.dot_general(a, b, dims, preferred_element_type=F32)


def call(body, out_shape, args, scratch=(), smem=0, limit=24):
    vmem = pl.BlockSpec(memory_space=pltpu.VMEM)
    scalars = pl.BlockSpec(memory_space=pltpu.SMEM)
    return pl.pallas_call(
        body,
        out_shape=out_shape,
        in_specs=[scalars if i < smem else vmem for i in range(len(args))],
        out_specs=jax.tree.map(lambda out: scalars if out.dtype == jnp.int32 else vmem, out_shape),
        scratch_shapes=list(scratch),
        compiler_params=pltpu.CompilerParams(vmem_limit_bytes=limit * 1024 * 1024),
    )(*args)


def seq_here():
    return (lax.axis_index("z_far") * 4 + lax.axis_index("z_near")) * 2 + lax.axis_index("y_hi")


def noise_scale_of(level, shape):
    time_frac = (jnp.full(shape, level, jnp.int32).astype(F32) + 1.0) / (LEVELS + 1.0)
    return 3.0 * time_frac / (1.0 + 2.0 * time_frac)


def weight_body(embed_ref, mod_ref, qkv_ref, payload_ref, order_ref, term_ref):
    width = embed_ref.shape[1]
    features = qkv_ref.shape[1]
    offset = seq_here() * features
    start = pl.multiple_of(jnp.minimum((offset >> 7) << 7, width - 256), HD)
    mean = jnp.sum(embed_ref[...].astype(F32), axis=1, keepdims=True) / width
    window = embed_ref[:, pl.ds(start, 256)].astype(F32)
    scale = 1.0 + mod_ref[1, :, pl.ds(start, 256)]
    shift = mod_ref[0, :, pl.ds(start, 256)]
    rows = jnp.concatenate(
        [(window - mean) * scale, shift, jnp.zeros((MROWS - CHANS - 1, 256), F32)], axis=0
    )
    select = jnp.where(
        lax.broadcasted_iota(jnp.int32, (256, features), 0)
        == lax.broadcasted_iota(jnp.int32, (256, features), 1) + (offset - start),
        1.0,
        0.0,
    ).astype(BF16)
    high = rows.astype(BF16)
    low = dot((rows - high.astype(F32)).astype(BF16), select).astype(BF16)
    high = dot(high, select).astype(BF16)
    for part in range(3):
        term = dot(high, qkv_ref[part]) + dot(low, qkv_ref[part])
        for head in range(3):
            j = part * 3 + head
            block = term[:, head * HD : (head + 1) * HD]
            term_ref[j * CHANS : (j + 1) * CHANS, :] = block[0:CHANS, :]
            term_ref[9 * CHANS + j : 9 * CHANS + j + 1, :] = block[CHANS : CHANS + 1, :]
    term_ref[9 * CHANS + 9 :, :] = jnp.zeros((term_ref.shape[0] - 9 * CHANS - 9, HD), F32)
    for p in range(payload_ref.shape[0]):
        payload_ref[p] = term_ref[p * PIECE : (p + 1) * PIECE, :].astype(BF16)
    order_ref[0] = 0


def latent_body(
    level_ref, _, hidden_ref, gen_t_ref, noise_t_ref, embed_ref, text_in_ref, noised_ref, gap_ref, send_ref
):
    x_t = dot(gen_t_ref[...], hidden_ref[...], NT)
    noise_scale = noise_scale_of(level_ref[0], x_t.shape)
    noised_t = ((1.0 - noise_scale) * x_t + noise_scale * noise_t_ref[...].astype(F32)).astype(BF16)
    noised = noised_t.astype(F32).T
    noised_ref[...] = noised
    gap_ref[...] = (x_t - noised_t.astype(F32)).T
    width = embed_ref.shape[1]
    step = 512
    embed_mean = jnp.zeros((embed_ref.shape[0], HD), F32)
    for j in range(width // HD):
        embed_mean = embed_mean + embed_ref[:, j * HD : (j + 1) * HD].astype(F32)
    embed_mean = jnp.sum(embed_mean, axis=1, keepdims=True) / width
    row_mean = jnp.sum(noised_t.astype(F32) * embed_mean, axis=0, keepdims=True)
    row_mean = jnp.broadcast_to(row_mean, (HD, noised.shape[0])).T
    row_var = jnp.zeros(row_mean.shape, F32)
    noised_b = noised.astype(BF16)
    for j in range(width // step):
        h = dot(noised_b, embed_ref[:, j * step : (j + 1) * step])
        for k in range(step // HD):
            row_var = row_var + jnp.square(h[:, k * HD : (k + 1) * HD] - row_mean)
    row_var = jnp.sum(row_var, axis=1, keepdims=True) / width
    send_ref[0:CHANS, :] = (noised * lax.rsqrt(row_var + 1e-06)).T.astype(BF16)
    text = text_in_ref[...].astype(F32)
    for j in range(6):
        block = text[:, j // 3, (j % 3) * HD : (j % 3 + 1) * HD]
        send_ref[CHANS + j * 16 : CHANS + (j + 1) * 16, :] = block.astype(BF16)


def total_of(ref, rows):
    total = ref[0, 0:rows, :].astype(F32)
    for i in range(1, ref.shape[0]):
        total = total + ref[i, 0:rows, :].astype(F32)
    return total.astype(BF16)


def far_body(recv_ref, send_ref, out_ref):
    piece = total_of(recv_ref, PIECE)
    channels = send_ref[pl.ds(pl.multiple_of((lax.axis_index("mp") & 3) * PART, PART), PART), :]
    for i in range(out_ref.shape[0]):
        out_ref[i, 0:PIECE, :] = piece
        out_ref[i, PIECE : PIECE + PART, :] = channels
        out_ref[i, PIECE + PART :, :] = send_ref[CHANS:, :]


def spread_body(recv_ref, out_ref, text_ref):
    piece = total_of(recv_ref, PIECE)
    text = PIECE + PART
    for i in range(out_ref.shape[0]):
        out_ref[i, 0:PIECE, :] = piece
        for g in range(recv_ref.shape[0]):
            out_ref[i, PIECE + g * PART : PIECE + (g + 1) * PART, :] = recv_ref[g, PIECE:text, :]
            text_ref[i, g * 96 : (g + 1) * 96, :] = recv_ref[g, text:, :]


def image_body(
    send_ref, recv_ref, other1_ref, other2_ref, other3_ref, gain_ref, out_ref, lat_ref, s_ref, v_ref, m_ref, own_ref, sum_ref
):
    tokens = lat_ref.shape[1]
    chunk = 4096
    n_chunks = tokens // chunk
    ones = jnp.where(lax.broadcasted_iota(jnp.int32, (MROWS - CHANS, HD), 0) == 0, 1.0, 0.0).astype(BF16)
    other_refs = (other1_ref, other2_ref, other3_ref)
    n_far = (recv_ref.shape[1] - PIECE) // PART
    for i in range(tokens // HD):
        near, first = i // n_far, (i % n_far) * PART
        at = slice(i * HD, (i + 1) * HD)
        lat_ref[0:PART, at] = recv_ref[near, PIECE + first : PIECE + first + PART, :]
        for k, ref in enumerate(other_refs):
            lat_ref[(k + 1) * PART : (k + 2) * PART, at] = ref[near, first : first + PART, :]
        lat_ref[CHANS:MROWS, at] = ones
    for i in range(recv_ref.shape[0]):
        m_ref[i * PIECE : (i + 1) * PIECE, :] = recv_ref[i, 0:PIECE, :].astype(F32)
    own_ref[...] = send_ref[0:CHANS, :].astype(F32)

    def reordered(ref, base):
        here = lax.axis_index("mp") & 3
        starts = [pl.multiple_of((here ^ k) * PART + base, PART) for k in range(4)]
        return jnp.concatenate([ref[pl.ds(start, PART), :] for start in starts], axis=0)

    own = jnp.concatenate([reordered(own_ref, 0).astype(BF16), ones], axis=0)
    score_scale = HD ** (-0.5) * 1.4426950408889634
    biases = m_ref[9 * CHANS : 9 * CHANS + 16, :]

    def weight(j):
        block = reordered(m_ref, j * CHANS)
        pad = jnp.zeros((HD - CHANS - 1, HD), F32)
        return jnp.concatenate([block, biases[j : j + 1, :], pad], axis=0).T[:, 0:MROWS].astype(BF16)

    q_image, w_k, w_v = [], [], []
    for head in range(3):
        q_t = dot(weight(head), own)
        q_t = q_t * lax.rsqrt(jnp.mean(q_t * q_t, axis=0, keepdims=True) + 1e-06)
        q = q_t.T * (gain_ref[0:1, :] * score_scale)
        out_ref[3 + head] = q
        q_image.append((q * gain_ref[1:2, :]).astype(BF16))
        w_k.append(weight(3 + head))
        w_v.append(weight(6 + head))
    rows = q_image[0].shape[0]

    def score_step(c, tops):
        at = pl.ds(pl.multiple_of(c * chunk, chunk), chunk)
        lat = lat_ref[:, at]
        out = []
        for head in range(3):
            k_t = dot(w_k[head], lat)
            k_t = k_t * lax.rsqrt(jnp.mean(k_t * k_t, axis=0, keepdims=True) + 1e-06)
            v_ref[head, :, at] = dot(w_v[head], lat).astype(BF16)
            s = dot(q_image[head], k_t.astype(BF16))
            s_ref[head, :, at] = s
            top = tops[head]
            for j in range(chunk // HD):
                top = jnp.maximum(top, s[:, j * HD : (j + 1) * HD])
            out.append(top)
        return tuple(out)

    tops = lax.fori_loop(0, n_chunks, score_step, (jnp.full((rows, HD), -3e38, F32),) * 3)
    tops = [jnp.max(top, axis=1, keepdims=True) for top in tops]
    for head in range(3):
        out_ref[head] = jnp.zeros((rows, HD), F32)
        sum_ref[head] = jnp.zeros((rows, HD), F32)

    def mix_step(c, carry):
        at = pl.ds(pl.multiple_of(c * chunk, chunk), chunk)
        for head in range(3):
            p = jnp.exp2(s_ref[head, :, at] - tops[head])
            total = sum_ref[head]
            for j in range(chunk // HD):
                total = total + p[:, j * HD : (j + 1) * HD]
            sum_ref[head] = total
            out_ref[head] += dot(p.astype(BF16), v_ref[head, :, at], NT)
        return carry

    lax.fori_loop(0, n_chunks, mix_step, 0)
    lane = lax.broadcasted_iota(jnp.int32, (rows, HD), 1)
    numbers = jnp.zeros((rows, HD), F32)
    for head in range(3):
        numbers = jnp.where(lane == head, tops[head], numbers)
        numbers = jnp.where(lane == 3 + head, jnp.sum(sum_ref[head], axis=1, keepdims=True), numbers)
    out_ref[6] = numbers


def text_body(image_ref, text_ref, own_ref, other_ref, att_ref):
    def block(first):
        return text_ref[:, first : first + 16, :].reshape(text_ref.shape[0] * 16, HD)

    for head in range(3):
        s = dot(image_ref[3 + head].astype(BF16), block(head * 16), NT)
        image_top = image_ref[6][:, head : head + 1]
        top = jnp.maximum(image_top, jnp.max(s, axis=1, keepdims=True))
        keep = jnp.exp2(image_top - top)
        p = jnp.exp2(s - top)
        acc = image_ref[head] * keep + dot(p.astype(BF16), block(48 + head * 16))
        total = image_ref[6][:, 3 + head : 4 + head] * keep + jnp.sum(p, axis=1, keepdims=True)
        att_ref[:, :, head * HD : (head + 1) * HD] = (acc / total).reshape(att_ref.shape[0], -1, HD)
    core = lax.axis_index("mp") & 1
    for i in range(own_ref.shape[0]):
        own_ref[i] = att_ref[2 * i + core].astype(BF16)
        other_ref[i] = att_ref[2 * i + 1 - core].astype(BF16)


def project_body(own_ref, other_ref, out_w_ref, y_own_ref, y_other_ref):
    own = own_ref[...].reshape(-1, own_ref.shape[2])
    other = other_ref[...].reshape(-1, own_ref.shape[2])
    step = 512
    for j in range(out_w_ref.shape[1] // step):
        at = slice(j * step, (j + 1) * step)
        out_w = out_w_ref[:, at]
        y_other_ref[:, at] = dot(other, out_w).astype(BF16)
        y_own_ref[:, at] = dot(own, out_w)


def velocity_body(parts_ref, noised_ref, embed_ref, mod_ref, final_t_ref, v_ref):
    total = parts_ref[0].astype(F32)
    for i in range(1, parts_ref.shape[0]):
        total = total + parts_ref[i].astype(F32)
    own_rows = total.shape[0]
    own = noised_ref[pl.ds(pl.multiple_of(lax.axis_index("mp") * own_rows, own_rows), own_rows), :].astype(BF16)
    h = dot(own, embed_ref[...]) + mod_ref[2] * total
    width = h.shape[1]
    h = h - jnp.sum(h, axis=1, keepdims=True) / width
    var = jnp.sum(h * h, axis=1, keepdims=True) / width
    v = dot((h * lax.rsqrt(var + 1e-06)).astype(BF16), final_t_ref[...], NT)
    v = jnp.concatenate([v[0:8, :], v[8:16, :]], axis=1)
    for i in range(v_ref.shape[0]):
        v_ref[i] = v


def grad_body(level_ref, both_ref, gap_ref, hidden_ref, gen_t_ref, piece_ref, share_ref, raw_ref, diff_ref, grad_ref):
    n_mp = both_ref.shape[0] // 2
    chans = gap_ref.shape[1]

    def rows(first):
        blocks = []
        for i in range(first, first + n_mp):
            blocks += [both_ref[i][:, 0:chans], both_ref[i][:, chans : 2 * chans]]
        return jnp.concatenate(blocks, axis=0)

    teacher, student = rows(0), rows(n_mp)
    spread = jnp.abs(gap_ref[...] + noise_scale_of(level_ref[0], gap_ref.shape) * teacher)
    spread = jnp.sum(jnp.sum(spread, axis=1, keepdims=True), axis=0, keepdims=True)
    spread = jnp.broadcast_to(spread, (8, HD))
    diff = teacher - student
    diff_ref[...] = diff.T
    half = chans // 2
    share = diff_ref[pl.ds(pl.multiple_of(lax.axis_index("role") * half, half), half), :]
    share_ref[...] = share
    cols = grad_ref.shape[1]
    hidden = hidden_ref[:, pl.ds(pl.multiple_of(lax.axis_index("mp") * cols, HD), cols)]
    grad_ref[...] = dot(share.astype(BF16), hidden)
    terms = [grad_ref[:, g * HD : (g + 1) * HD] for g in range(3)]
    block = in_parts(jnp.concatenate([*terms, spread], axis=0))
    for i in range(piece_ref.shape[0]):
        piece_ref[i] = block
    feats = raw_ref.shape[1]
    raw_ref[...] = dot(diff.astype(BF16), gen_t_ref[:, pl.ds(pl.multiple_of(lax.axis_index("role") * feats, HD), feats)])


def in_parts(block):
    row = lax.broadcasted_iota(jnp.int32, block.shape, 0) - (block.shape[0] - 8)
    high = block.astype(BF16).astype(F32)
    mid = (block - high).astype(BF16).astype(F32)
    low = block - high - mid
    return jnp.where(row == 1, mid, jnp.where(row == 2, low, high)).astype(BF16)


def whole_total(ref):
    total = ref[0].astype(F32)
    for i in range(1, ref.shape[0]):
        total = total + ref[i].astype(F32)
    last = total.shape[0] - 8
    number = total[last : last + 1, :] + total[last + 1 : last + 2, :] + total[last + 2 : last + 3, :]
    return total[0:last, :], number


def near_body(recv_ref, out_ref):
    total, number = whole_total(recv_ref)
    out = in_parts(jnp.concatenate([total, jnp.broadcast_to(number, (8, HD))], axis=0))
    for i in range(out_ref.shape[0]):
        out_ref[i] = out


def last_body(level_ref, recv_ref, share_ref, raw_ref, x_ref, hidden_ref, gen_ref, *, entries):
    total, number = whole_total(recv_ref)
    factor = noise_scale_of(level_ref[0], (1, 1)) / (number[:, 0:1] / entries + 1e-06)
    x_ref[...] = share_ref[...] * factor
    hidden_ref[...] = (raw_ref[...] * factor).astype(BF16)
    half = gen_ref.shape[0]
    for g in range(3):
        gen_ref[:, g * HD : (g + 1) * HD] = total[g * half : (g + 1) * half, :] * factor


def exchange(array, axis, groups=None):
    return lax.all_to_all(array, axis, 0, 0, axis_index_groups=groups, tiled=True)


def on_device(
    gen_hidden, w_gen, noise_latent, level_index, w_embed, modulation, w_qkv, qk_gain, text_kv, w_out, w_final
):
    rows_here, width = gen_hidden.shape
    n_seq, n_far, n_mp = lax.axis_size(SEQ), lax.axis_size("z_far"), lax.axis_size("mp")
    chans = w_gen.shape[1]
    tokens = rows_here * n_seq
    sds = jax.ShapeDtypeStruct
    mods = jnp.transpose(modulation, (1, 0, 2))
    embed = w_embed[0]
    gen_t = w_gen.T
    payload, order = call(
        weight_body,
        (sds((8, PIECE, HD), BF16), sds((1,), jnp.int32)),
        (embed, mods, jnp.transpose(w_qkv[0], (1, 0, 2))),
        scratch=(pltpu.VMEM((8 * PIECE, HD), F32),),
        limit=60,
    )
    noised, gap, send = call(
        latent_body,
        (
            sds((rows_here, chans), F32),
            sds((rows_here, chans), F32),
            sds((chans + 96, HD), BF16),
        ),
        (level_index, order, gen_hidden, gen_t, noise_latent.T, embed, text_kv[0]),
        smem=2,
        limit=60,
    )
    pieces = exchange(payload, NEAR)
    pieces = call(far_body, sds((n_far, PIECE + PART + 96, HD), BF16), (pieces, send))
    pieces = exchange(pieces, "z_far")
    pieces, text = call(
        spread_body,
        (sds((8, PIECE + n_far * PART, HD), BF16), sds((8, n_far * 96, HD), BF16)),
        (pieces,),
    )
    pieces = exchange(pieces, NEAR)
    text = exchange(text, NEAR).reshape(n_seq, 96, HD)
    channels = pieces[:, PIECE:, :]
    others = [lax.ppermute(channels, "mp", [(i, i ^ k) for i in range(n_mp)]) for k in (1, 2, 3)]

    image = call(
        image_body,
        sds((7, rows_here, HD), F32),
        (send, pieces, *others, qk_gain[0]),
        scratch=(
            pltpu.VMEM((MROWS, tokens), BF16),
            pltpu.VMEM((3, rows_here, tokens), F32),
            pltpu.VMEM((3, HD, tokens), BF16),
            pltpu.VMEM((8 * PIECE, HD), F32),
            pltpu.VMEM((chans, HD), F32),
            pltpu.VMEM((3, rows_here, HD), F32),
        ),
    )
    own_rows = rows_here // n_mp
    share = sds((n_mp // 2, own_rows, 3 * HD), BF16)
    att_own, att_other = call(
        text_body, (share, share), (image, text), scratch=(pltpu.VMEM((n_mp, own_rows, 3 * HD), F32),)
    )
    y_own, y_other = call(
        project_body,
        (sds((rows_here // 2, width), F32), sds((rows_here // 2, width), BF16)),
        (att_own, att_other, w_out[0]),
    )
    y_other = lax.ppermute(y_other, "mp", [(i, i ^ 1) for i in range(n_mp)])
    y = (y_own + y_other.astype(F32)).astype(BF16)
    same_core = [[2 * x + core for x in range(n_mp // 2)] for core in range(2)]
    parts = exchange(y.reshape(n_mp // 2, own_rows, width), "mp", same_core)
    velocity = call(
        velocity_body,
        sds((2 * n_mp, 8, 2 * chans), F32),
        (parts, noised, embed, mods, w_final[0].T),
    )
    both = exchange(velocity, ("role", "mp"))
    half = chans // 2
    grad_piece, share, raw = call(
        grad_body,
        (sds((8, 3 * half + 8, HD), BF16), sds((half, rows_here), F32), sds((rows_here, width // 2), F32)),
        (level_index, both, gap, gen_hidden, gen_t),
        scratch=(pltpu.VMEM((chans, rows_here), F32), pltpu.VMEM((half, 3 * HD), F32)),
        smem=1,
    )
    near = exchange(grad_piece, NEAR)
    near = call(near_body, sds((n_far, 3 * half + 8, HD), BF16), (near,))
    everything = exchange(near, "z_far")

    def last(*refs):
        last_body(*refs, entries=tokens * chans)

    grad_x_t, grad_hidden, grad_gen_t = call(
        last,
        (sds((half, rows_here), F32), sds((rows_here, width // 2), BF16), sds((half, 3 * HD), F32)),
        (level_index, everything, share, raw),
        smem=1,
    )
    return grad_x_t.T, grad_hidden, grad_gen_t.T


def solution(mesh):
    n_role, n_seq, n_mp = (mesh.shape[name] for name in ("role", "seq", "mp"))
    names = ("role", *SEQ, "mp")
    mesh = jax.sharding.Mesh(mesh.devices.reshape(n_role, n_seq // 8, 4, 2, n_mp), names)
    placed = (
        P(SEQ, None),
        P(),
        P(SEQ, None),
        P(),
        P("role", None, None),
        P("role", None, None),
        P("role", SEQ, None, "mp"),
        P("role", None, None),
        P("role", SEQ, None, "mp"),
        P("role", "mp", None),
        P("role", None, None),
    )
    return jax.shard_map(
        on_device,
        mesh=mesh,
        in_specs=placed,
        out_specs=(P(SEQ, "role"), P(SEQ, "role"), P("mp", "role")),
        check_vma=False,
    )
```

```python
import jax
import jax.numpy as jnp
from jax import lax
from jax.experimental import pallas as pl
from jax.experimental.pallas import tpu as pltpu
from jax.sharding import PartitionSpec as P

LEVELS = 1000
HD = 128
SEQ = ("z_far", "z_near", "y_hi")
NEAR = ("z_near", "y_hi")
CHANS = 64
PART = CHANS // 4
MROWS = 80
PIECE = 80
F32 = jnp.float32
BF16 = jnp.bfloat16
NN = (((1,), (0,)), ((), ()))
NT = (((1,), (1,)), ((), ()))


def dot(a, b, dims=NN):
    return lax.dot_general(a, b, dims, preferred_element_type=F32)


def call(body, out_shape, args, scratch=(), smem=0, limit=24):
    vmem = pl.BlockSpec(memory_space=pltpu.VMEM)
    scalars = pl.BlockSpec(memory_space=pltpu.SMEM)
    return pl.pallas_call(
        body,
        out_shape=out_shape,
        in_specs=[scalars if i < smem else vmem for i in range(len(args))],
        out_specs=jax.tree.map(lambda out: scalars if out.dtype == jnp.int32 else vmem, out_shape),
        scratch_shapes=list(scratch),
        compiler_params=pltpu.CompilerParams(vmem_limit_bytes=limit * 1024 * 1024),
    )(*args)


def seq_here():
    return (lax.axis_index("z_far") * 4 + lax.axis_index("z_near")) * 2 + lax.axis_index("y_hi")


def noise_scale_of(level, shape):
    time_frac = (jnp.full(shape, level, jnp.int32).astype(F32) + 1.0) / (LEVELS + 1.0)
    return 3.0 * time_frac / (1.0 + 2.0 * time_frac)


def weight_body(embed_ref, mod_ref, qkv_ref, payload_ref, order_ref, term_ref):
    width = embed_ref.shape[1]
    features = qkv_ref.shape[1]
    offset = seq_here() * features
    start = pl.multiple_of(jnp.minimum((offset >> 7) << 7, width - 256), HD)
    mean = jnp.sum(embed_ref[...].astype(F32), axis=1, keepdims=True) / width
    window = embed_ref[:, pl.ds(start, 256)].astype(F32)
    scale = 1.0 + mod_ref[1, :, pl.ds(start, 256)]
    shift = mod_ref[0, :, pl.ds(start, 256)]
    rows = jnp.concatenate(
        [(window - mean) * scale, shift, jnp.zeros((MROWS - CHANS - 1, 256), F32)], axis=0
    )
    select = jnp.where(
        lax.broadcasted_iota(jnp.int32, (256, features), 0)
        == lax.broadcasted_iota(jnp.int32, (256, features), 1) + (offset - start),
        1.0,
        0.0,
    ).astype(BF16)
    high = rows.astype(BF16)
    low = dot((rows - high.astype(F32)).astype(BF16), select).astype(BF16)
    high = dot(high, select).astype(BF16)
    for part in range(3):
        term = dot(high, qkv_ref[part]) + dot(low, qkv_ref[part])
        for head in range(3):
            j = part * 3 + head
            block = term[:, head * HD : (head + 1) * HD]
            term_ref[j * CHANS : (j + 1) * CHANS, :] = block[0:CHANS, :]
            term_ref[9 * CHANS + j : 9 * CHANS + j + 1, :] = block[CHANS : CHANS + 1, :]
    term_ref[9 * CHANS + 9 :, :] = jnp.zeros((term_ref.shape[0] - 9 * CHANS - 9, HD), F32)
    for p in range(payload_ref.shape[0]):
        payload_ref[p] = term_ref[p * PIECE : (p + 1) * PIECE, :].astype(BF16)
    order_ref[0] = 0


def latent_body(
    level_ref, _, hidden_ref, gen_t_ref, noise_t_ref, embed_ref, text_in_ref, noised_ref, gap_ref, send_ref
):
    x_t = dot(gen_t_ref[...], hidden_ref[...], NT)
    noise_scale = noise_scale_of(level_ref[0], x_t.shape)
    noised_t = ((1.0 - noise_scale) * x_t + noise_scale * noise_t_ref[...].astype(F32)).astype(BF16)
    noised = noised_t.astype(F32).T
    noised_ref[...] = noised
    gap_ref[...] = (x_t - noised_t.astype(F32)).T
    width = embed_ref.shape[1]
    step = 512
    embed_mean = jnp.zeros((embed_ref.shape[0], HD), F32)
    for j in range(width // HD):
        embed_mean = embed_mean + embed_ref[:, j * HD : (j + 1) * HD].astype(F32)
    embed_mean = jnp.sum(embed_mean, axis=1, keepdims=True) / width
    row_mean = jnp.sum(noised_t.astype(F32) * embed_mean, axis=0, keepdims=True)
    row_mean = jnp.broadcast_to(row_mean, (HD, noised.shape[0])).T
    row_var = jnp.zeros(row_mean.shape, F32)
    noised_b = noised.astype(BF16)
    for j in range(width // step):
        h = dot(noised_b, embed_ref[:, j * step : (j + 1) * step])
        for k in range(step // HD):
            row_var = row_var + jnp.square(h[:, k * HD : (k + 1) * HD] - row_mean)
    row_var = jnp.sum(row_var, axis=1, keepdims=True) / width
    send_ref[0:CHANS, :] = (noised * lax.rsqrt(row_var + 1e-06)).T.astype(BF16)
    text = text_in_ref[...].astype(F32)
    for j in range(6):
        block = text[:, j // 3, (j % 3) * HD : (j % 3 + 1) * HD]
        send_ref[CHANS + j * 16 : CHANS + (j + 1) * 16, :] = block.astype(BF16)


def total_of(ref, rows):
    total = ref[0, 0:rows, :].astype(F32)
    for i in range(1, ref.shape[0]):
        total = total + ref[i, 0:rows, :].astype(F32)
    return total.astype(BF16)


def far_body(recv_ref, send_ref, out_ref):
    piece = total_of(recv_ref, PIECE)
    channels = send_ref[pl.ds(pl.multiple_of((lax.axis_index("mp") & 3) * PART, PART), PART), :]
    for i in range(out_ref.shape[0]):
        out_ref[i, 0:PIECE, :] = piece
        out_ref[i, PIECE : PIECE + PART, :] = channels
        out_ref[i, PIECE + PART :, :] = send_ref[CHANS:, :]


def spread_body(recv_ref, out_ref, text_ref):
    piece = total_of(recv_ref, PIECE)
    text = PIECE + PART
    for i in range(out_ref.shape[0]):
        out_ref[i, 0:PIECE, :] = piece
        for g in range(recv_ref.shape[0]):
            out_ref[i, PIECE + g * PART : PIECE + (g + 1) * PART, :] = recv_ref[g, PIECE:text, :]
            text_ref[i, g * 96 : (g + 1) * 96, :] = recv_ref[g, text:, :]


def image_body(
    send_ref, recv_ref, other1_ref, other2_ref, other3_ref, gain_ref, out_ref, lat_ref, s_ref, v_ref, m_ref, own_ref, sum_ref
):
    tokens = lat_ref.shape[1]
    chunk = 4096
    n_chunks = tokens // chunk
    ones = jnp.where(lax.broadcasted_iota(jnp.int32, (MROWS - CHANS, HD), 0) == 0, 1.0, 0.0).astype(BF16)
    other_refs = (other1_ref, other2_ref, other3_ref)
    n_far = (recv_ref.shape[1] - PIECE) // PART
    for i in range(tokens // HD):
        near, first = i // n_far, (i % n_far) * PART
        at = slice(i * HD, (i + 1) * HD)
        lat_ref[0:PART, at] = recv_ref[near, PIECE + first : PIECE + first + PART, :]
        for k, ref in enumerate(other_refs):
            lat_ref[(k + 1) * PART : (k + 2) * PART, at] = ref[near, first : first + PART, :]
        lat_ref[CHANS:MROWS, at] = ones
    for i in range(recv_ref.shape[0]):
        m_ref[i * PIECE : (i + 1) * PIECE, :] = recv_ref[i, 0:PIECE, :].astype(F32)
    own_ref[...] = send_ref[0:CHANS, :].astype(F32)

    def reordered(ref, base):
        here = lax.axis_index("mp") & 3
        starts = [pl.multiple_of((here ^ k) * PART + base, PART) for k in range(4)]
        return jnp.concatenate([ref[pl.ds(start, PART), :] for start in starts], axis=0)

    own = jnp.concatenate([reordered(own_ref, 0).astype(BF16), ones], axis=0)
    score_scale = HD ** (-0.5) * 1.4426950408889634
    biases = m_ref[9 * CHANS : 9 * CHANS + 16, :]

    def weight(j):
        block = reordered(m_ref, j * CHANS)
        pad = jnp.zeros((HD - CHANS - 1, HD), F32)
        return jnp.concatenate([block, biases[j : j + 1, :], pad], axis=0).T[:, 0:MROWS].astype(BF16)

    q_image, w_k, w_v = [], [], []
    for head in range(3):
        q_t = dot(weight(head), own)
        q_t = q_t * lax.rsqrt(jnp.mean(q_t * q_t, axis=0, keepdims=True) + 1e-06)
        q = q_t.T * (gain_ref[0:1, :] * score_scale)
        out_ref[3 + head] = q
        q_image.append((q * gain_ref[1:2, :]).astype(BF16))
        w_k.append(weight(3 + head))
        w_v.append(weight(6 + head))
    rows = q_image[0].shape[0]

    def score_step(c, tops):
        at = pl.ds(pl.multiple_of(c * chunk, chunk), chunk)
        lat = lat_ref[:, at]
        out = []
        for head in range(3):
            k_t = dot(w_k[head], lat)
            k_t = k_t * lax.rsqrt(jnp.mean(k_t * k_t, axis=0, keepdims=True) + 1e-06)
            v_ref[head, :, at] = dot(w_v[head], lat).astype(BF16)
            s = dot(q_image[head], k_t.astype(BF16))
            s_ref[head, :, at] = s
            top = tops[head]
            for j in range(chunk // HD):
                top = jnp.maximum(top, s[:, j * HD : (j + 1) * HD])
            out.append(top)
        return tuple(out)

    tops = lax.fori_loop(0, n_chunks, score_step, (jnp.full((rows, HD), -3e38, F32),) * 3)
    tops = [jnp.max(top, axis=1, keepdims=True) for top in tops]
    for head in range(3):
        out_ref[head] = jnp.zeros((rows, HD), F32)
        sum_ref[head] = jnp.zeros((rows, HD), F32)

    def mix_step(c, carry):
        at = pl.ds(pl.multiple_of(c * chunk, chunk), chunk)
        for head in range(3):
            p = jnp.exp2(s_ref[head, :, at] - tops[head])
            total = sum_ref[head]
            for j in range(chunk // HD):
                total = total + p[:, j * HD : (j + 1) * HD]
            sum_ref[head] = total
            out_ref[head] += dot(p.astype(BF16), v_ref[head, :, at], NT)
        return carry

    lax.fori_loop(0, n_chunks, mix_step, 0)
    lane = lax.broadcasted_iota(jnp.int32, (rows, HD), 1)
    numbers = jnp.zeros((rows, HD), F32)
    for head in range(3):
        numbers = jnp.where(lane == head, tops[head], numbers)
        numbers = jnp.where(lane == 3 + head, jnp.sum(sum_ref[head], axis=1, keepdims=True), numbers)
    out_ref[6] = numbers


def text_body(image_ref, text_ref, own_ref, other_ref, att_ref):
    def block(first):
        return text_ref[:, first : first + 16, :].reshape(text_ref.shape[0] * 16, HD)

    for head in range(3):
        s = dot(image_ref[3 + head].astype(BF16), block(head * 16), NT)
        image_top = image_ref[6][:, head : head + 1]
        top = jnp.maximum(image_top, jnp.max(s, axis=1, keepdims=True))
        keep = jnp.exp2(image_top - top)
        p = jnp.exp2(s - top)
        acc = image_ref[head] * keep + dot(p.astype(BF16), block(48 + head * 16))
        total = image_ref[6][:, 3 + head : 4 + head] * keep + jnp.sum(p, axis=1, keepdims=True)
        att_ref[:, :, head * HD : (head + 1) * HD] = (acc / total).reshape(att_ref.shape[0], -1, HD)
    core = lax.axis_index("mp") & 1
    for i in range(own_ref.shape[0]):
        own_ref[i] = att_ref[2 * i + core].astype(BF16)
        other_ref[i] = att_ref[2 * i + 1 - core].astype(BF16)


def project_body(own_ref, other_ref, out_w_ref, y_own_ref, y_other_ref):
    own = own_ref[...].reshape(-1, own_ref.shape[2])
    other = other_ref[...].reshape(-1, own_ref.shape[2])
    step = 512
    for j in range(out_w_ref.shape[1] // step):
        at = slice(j * step, (j + 1) * step)
        out_w = out_w_ref[:, at]
        y_other_ref[:, at] = dot(other, out_w).astype(BF16)
        y_own_ref[:, at] = dot(own, out_w)


def velocity_body(parts_ref, noised_ref, embed_ref, mod_ref, final_t_ref, v_ref):
    total = parts_ref[0].astype(F32)
    for i in range(1, parts_ref.shape[0]):
        total = total + parts_ref[i].astype(F32)
    own_rows = total.shape[0]
    own = noised_ref[pl.ds(pl.multiple_of(lax.axis_index("mp") * own_rows, own_rows), own_rows), :].astype(BF16)
    h = dot(own, embed_ref[...]) + mod_ref[2] * total
    width = h.shape[1]
    h = h - jnp.sum(h, axis=1, keepdims=True) / width
    var = jnp.sum(h * h, axis=1, keepdims=True) / width
    v = dot((h * lax.rsqrt(var + 1e-06)).astype(BF16), final_t_ref[...], NT)
    v = jnp.concatenate([v[0:8, :], v[8:16, :]], axis=1)
    for i in range(v_ref.shape[0]):
        v_ref[i] = v


def grad_body(level_ref, both_ref, gap_ref, hidden_ref, gen_t_ref, piece_ref, share_ref, raw_ref, diff_ref, grad_ref):
    n_mp = both_ref.shape[0] // 2
    chans = gap_ref.shape[1]

    def rows(first):
        blocks = []
        for i in range(first, first + n_mp):
            blocks += [both_ref[i][:, 0:chans], both_ref[i][:, chans : 2 * chans]]
        return jnp.concatenate(blocks, axis=0)

    teacher, student = rows(0), rows(n_mp)
    spread = jnp.abs(gap_ref[...] + noise_scale_of(level_ref[0], gap_ref.shape) * teacher)
    spread = jnp.sum(jnp.sum(spread, axis=1, keepdims=True), axis=0, keepdims=True)
    spread = jnp.broadcast_to(spread, (8, HD))
    diff = teacher - student
    diff_ref[...] = diff.T
    half = chans // 2
    share = diff_ref[pl.ds(pl.multiple_of(lax.axis_index("role") * half, half), half), :]
    share_ref[...] = share
    cols = grad_ref.shape[1]
    hidden = hidden_ref[:, pl.ds(pl.multiple_of(lax.axis_index("mp") * cols, HD), cols)]
    grad_ref[...] = dot(share.astype(BF16), hidden)
    terms = [grad_ref[:, g * HD : (g + 1) * HD] for g in range(3)]
    block = in_parts(jnp.concatenate([*terms, spread], axis=0))
    for i in range(piece_ref.shape[0]):
        piece_ref[i] = block
    feats = raw_ref.shape[1]
    raw_ref[...] = dot(diff.astype(BF16), gen_t_ref[:, pl.ds(pl.multiple_of(lax.axis_index("role") * feats, HD), feats)])


def in_parts(block):
    row = lax.broadcasted_iota(jnp.int32, block.shape, 0) - (block.shape[0] - 8)
    high = block.astype(BF16).astype(F32)
    mid = (block - high).astype(BF16).astype(F32)
    low = block - high - mid
    return jnp.where(row == 1, mid, jnp.where(row == 2, low, high)).astype(BF16)


def whole_total(ref):
    total = ref[0].astype(F32)
    for i in range(1, ref.shape[0]):
        total = total + ref[i].astype(F32)
    last = total.shape[0] - 8
    number = total[last : last + 1, :] + total[last + 1 : last + 2, :] + total[last + 2 : last + 3, :]
    return total[0:last, :], number


def sum_body(recv_ref, out_ref):
    total, number = whole_total(recv_ref)
    out = in_parts(jnp.concatenate([total, jnp.broadcast_to(number, (8, HD))], axis=0))
    for i in range(out_ref.shape[0]):
        out_ref[i] = out


def last_body(level_ref, recv_ref, share_ref, raw_ref, x_ref, hidden_ref, gen_ref, *, entries):
    total, number = whole_total(recv_ref)
    factor = noise_scale_of(level_ref[0], (1, 1)) / (number[:, 0:1] / entries + 1e-06)
    x_ref[...] = share_ref[...] * factor
    hidden_ref[...] = (raw_ref[...] * factor).astype(BF16)
    half = gen_ref.shape[0]
    for g in range(3):
        gen_ref[:, g * HD : (g + 1) * HD] = total[g * half : (g + 1) * half, :] * factor


def exchange(array, axis, groups=None):
    return lax.all_to_all(array, axis, 0, 0, axis_index_groups=groups, tiled=True)


def on_device(
    gen_hidden, w_gen, noise_latent, level_index, w_embed, modulation, w_qkv, qk_gain, text_kv, w_out, w_final
):
    rows_here, width = gen_hidden.shape
    n_seq, n_far, n_mp = lax.axis_size(SEQ), lax.axis_size("z_far"), lax.axis_size("mp")
    chans = w_gen.shape[1]
    tokens = rows_here * n_seq
    sds = jax.ShapeDtypeStruct
    mods = jnp.transpose(modulation, (1, 0, 2))
    embed = w_embed[0]
    gen_t = w_gen.T
    payload, order = call(
        weight_body,
        (sds((8, PIECE, HD), BF16), sds((1,), jnp.int32)),
        (embed, mods, jnp.transpose(w_qkv[0], (1, 0, 2))),
        scratch=(pltpu.VMEM((8 * PIECE, HD), F32),),
        limit=60,
    )
    noised, gap, send = call(
        latent_body,
        (
            sds((rows_here, chans), F32),
            sds((rows_here, chans), F32),
            sds((chans + 96, HD), BF16),
        ),
        (level_index, order, gen_hidden, gen_t, noise_latent.T, embed, text_kv[0]),
        smem=2,
        limit=60,
    )
    pieces = exchange(payload, NEAR)
    pieces = call(far_body, sds((n_far, PIECE + PART + 96, HD), BF16), (pieces, send))
    pieces = exchange(pieces, "z_far")
    pieces, text = call(
        spread_body,
        (sds((8, PIECE + n_far * PART, HD), BF16), sds((8, n_far * 96, HD), BF16)),
        (pieces,),
    )
    pieces = exchange(pieces, NEAR)
    text = exchange(text, NEAR).reshape(n_seq, 96, HD)
    channels = pieces[:, PIECE:, :]
    others = [lax.ppermute(channels, "mp", [(i, i ^ k) for i in range(n_mp)]) for k in (1, 2, 3)]

    image = call(
        image_body,
        sds((7, rows_here, HD), F32),
        (send, pieces, *others, qk_gain[0]),
        scratch=(
            pltpu.VMEM((MROWS, tokens), BF16),
            pltpu.VMEM((3, rows_here, tokens), F32),
            pltpu.VMEM((3, HD, tokens), BF16),
            pltpu.VMEM((8 * PIECE, HD), F32),
            pltpu.VMEM((chans, HD), F32),
            pltpu.VMEM((3, rows_here, HD), F32),
        ),
    )
    own_rows = rows_here // n_mp
    share = sds((n_mp // 2, own_rows, 3 * HD), BF16)
    att_own, att_other = call(
        text_body, (share, share), (image, text), scratch=(pltpu.VMEM((n_mp, own_rows, 3 * HD), F32),)
    )
    y_own, y_other = call(
        project_body,
        (sds((rows_here // 2, width), F32), sds((rows_here // 2, width), BF16)),
        (att_own, att_other, w_out[0]),
    )
    y_other = lax.ppermute(y_other, "mp", [(i, i ^ 1) for i in range(n_mp)])
    y = (y_own + y_other.astype(F32)).astype(BF16)
    same_core = [[2 * x + core for x in range(n_mp // 2)] for core in range(2)]
    parts = exchange(y.reshape(n_mp // 2, own_rows, width), "mp", same_core)
    velocity = call(
        velocity_body,
        sds((2 * n_mp, 8, 2 * chans), F32),
        (parts, noised, embed, mods, w_final[0].T),
    )
    both = exchange(velocity, ("role", "mp"))
    half = chans // 2
    grad_piece, share, raw = call(
        grad_body,
        (sds((n_far, 3 * half + 8, HD), BF16), sds((half, rows_here), F32), sds((rows_here, width // 2), F32)),
        (level_index, both, gap, gen_hidden, gen_t),
        scratch=(pltpu.VMEM((chans, rows_here), F32), pltpu.VMEM((half, 3 * HD), F32)),
        smem=1,
    )
    far = exchange(grad_piece, "z_far")
    far = call(sum_body, sds((n_seq // n_far, 3 * half + 8, HD), BF16), (far,))
    everything = exchange(far, NEAR)

    def last(*refs):
        last_body(*refs, entries=tokens * chans)

    grad_x_t, grad_hidden, grad_gen_t = call(
        last,
        (sds((half, rows_here), F32), sds((rows_here, width // 2), BF16), sds((half, 3 * HD), F32)),
        (level_index, everything, share, raw),
        smem=1,
    )
    return grad_x_t.T, grad_hidden, grad_gen_t.T


def solution(mesh):
    n_role, n_seq, n_mp = (mesh.shape[name] for name in ("role", "seq", "mp"))
    names = ("role", *SEQ, "mp")
    mesh = jax.sharding.Mesh(mesh.devices.reshape(n_role, n_seq // 8, 4, 2, n_mp), names)
    placed = (
        P(SEQ, None),
        P(),
        P(SEQ, None),
        P(),
        P("role", None, None),
        P("role", None, None),
        P("role", SEQ, None, "mp"),
        P("role", None, None),
        P("role", SEQ, None, "mp"),
        P("role", "mp", None),
        P("role", None, None),
    )
    return jax.shard_map(
        on_device,
        mesh=mesh,
        in_specs=placed,
        out_specs=(P(SEQ, "role"), P(SEQ, "role"), P("mp", "role")),
        check_vma=False,
    )
```
